32 devices in a mesh: dp: 16 (over z, y, x), tensor: 2 (over core).
Axes of the slice: x: 2, y: 2, z: 4, core: 2. Of those that a mesh axis runs over, the one named last changes fastest.
Arguments:
- input_rows: bfloat16 [32768, 768], P(('dp', 'tensor')), may hold values from -6 to 6
- first_values: bfloat16 [32768, 384], P('dp', 'tensor'), may hold values from -6 to 6
- doc_split: int32 [16], P('dp'), may hold values from 1024 to 2048, as said below
- gain_norm1: bfloat16 [768], replicated, may hold values from 0.5 to 1.5
- bias_norm1: bfloat16 [768], replicated, may hold values from -2 to 2
- w_query: bfloat16 [768, 768], P(None, 'tensor'), may hold values from -0.21875 to 0.21875
- bias_query: bfloat16 [768], P('tensor'), may hold values from -3 to 3
- w_key: bfloat16 [768, 768], P(None, 'tensor'), may hold values from -0.21875 to 0.21875
- w_value: bfloat16 [768, 384], P(None, 'tensor'), may hold values from -0.21875 to 0.21875
- bias_value: bfloat16 [384], P('tensor'), may hold values from -3 to 3
- w_out: bfloat16 [768, 768], P('tensor'), may hold values from -0.875 to 0.875
- bias_attn_out: bfloat16 [768], replicated, may hold values from -2 to 2
- gain_norm2: bfloat16 [768], replicated, may hold values from 0.5 to 1.5
- bias_norm2: bfloat16 [768], replicated, may hold values from -2 to 2
- w_up: bfloat16 [768, 3072], P(None, 'tensor'), may hold values from -0.21875 to 0.21875
- bias_up: bfloat16 [3072], P('tensor'), may hold values from -3 to 3
- w_down: bfloat16 [3072, 768], P('tensor'), may hold values from -0.109375 to 0.109375
- bias_down: bfloat16 [768], replicated, may hold values from -2 to 2
- cotangent: bfloat16 [32768, 768], P(('dp', 'tensor')), may hold values from -6 to 6
Outputs:
- output: bfloat16 [32768, 768], P(('dp', 'tensor'))
- grad_input: float32 [32768, 768], P(('dp', 'tensor'))
- grad_first_values: float32 [32768, 384], P('dp', 'tensor')
- grad_gain_norm1: float32 [768], replicated
- grad_bias_norm1: float32 [768], replicated
- grad_w_query: float32 [768, 768], P(None, 'tensor')
- grad_bias_query: float32 [768], P('tensor')
- grad_w_key: float32 [768, 768], P(None, 'tensor')
- grad_w_value: float32 [768, 384], P(None, 'tensor')
- grad_bias_value: float32 [384], P('tensor')
- grad_w_out: float32 [768, 768], P('tensor')
- grad_bias_attn_out: float32 [768], replicated
- grad_gain_norm2: float32 [768], replicated
- grad_bias_norm2: float32 [768], replicated
- grad_w_up: float32 [768, 3072], P(None, 'tensor')
- grad_bias_up: float32 [3072], P('tensor')
- grad_w_down: float32 [3072, 768], P('tensor')
- grad_bias_down: float32 [768], replicated
The draws below stay inside these ranges and needn't reach their ends.
Inputs may be any that keep to these rules, and one draw needn't show every extreme that they name: `doc_split`: each entry is 1024 (the group holds two documents of 1024 tokens) or 2 * 1024 (one document of 2048 tokens); both occur in every draw.
All inputs are finite; a program needn't handle non-finite values.
Results may differ from the reference program's by a relative error of at most 0.012.
Values may be sent and summed in bfloat16 or wider, within the bound.
A program may use at most 256 MiB of HBM per device.

```python
import jax
import jax.numpy as jnp
from jax import lax

D = 768
HEADS = 12
HEAD_DIM = 64
FF = 3072
SEQ_SHORT = 1024
VDIM = 384
GROUP_TOK = 2048
TOKENS = 32768
N_DP = 16


def draw_doc_split(key, part):
    key = jax.random.fold_in(key, 11)
    pick_key, ordering_key = jax.random.split(key)
    counts = jax.random.randint(pick_key, (N_DP,), 1, 3)
    ordering = jax.random.permutation(ordering_key, N_DP)
    counts = counts.at[ordering[0]].set(2).at[ordering[1]].set(1)
    return (counts * SEQ_SHORT).astype(jnp.int32)


def shard_levels(stream_key, dims, cuts, smallest, top_value):
    factor_of = 1.0
    for dim, blocks in cuts:
        steps = jax.random.uniform(jax.random.fold_in(jax.random.fold_in(stream_key, 6), dim), (blocks,), jnp.float32, smallest / len(cuts), top_value / len(cuts))
        factor_of = factor_of * jnp.repeat(jnp.exp(steps), dims[dim] // blocks).reshape((-1,) + (1,) * (len(dims) - 1 - dim))
    return factor_of


def centred(rng, extent, width, reach, pieces=(), kind=jnp.bfloat16):
    entries = width * jax.random.normal(rng, extent, jnp.float32)
    if pieces:
        entries = entries * shard_levels(rng, extent, pieces, -0.22, 0.18)
    return jnp.clip(entries, -reach, reach).astype(kind)


def setup_inputs(seed: int = 0) -> dict:
    arg_keys = jax.random.split(jax.random.key(seed), 20)
    input_rows = centred(arg_keys[0], (TOKENS, D), 1.0, 6.0, ((0, 32),))
    first_values = centred(arg_keys[1], (TOKENS, VDIM), 1.0, 6.0, ((0, 16), (1, 2)))
    doc_split = draw_doc_split(jax.random.fold_in(arg_keys[19], 71), 0)
    gain_norm1 = jnp.clip(1.0 + 0.1 * jax.random.normal(arg_keys[3], (D,), jnp.float32), 0.5, 1.5).astype(jnp.bfloat16)
    bias_norm1 = centred(arg_keys[4], (D,), 0.3, 2.0)
    w_query = centred(arg_keys[5], (D, D), D ** -0.5, 0.21875, ((1, 2),))
    bias_query = centred(arg_keys[6], (D,), 0.5, 3.0, ((0, 2),))
    w_key = centred(arg_keys[7], (D, D), D ** -0.5, 0.21875, ((1, 2),))
    w_value = centred(arg_keys[8], (D, VDIM), D ** -0.5, 0.21875, ((1, 2),))
    bias_value = centred(arg_keys[9], (VDIM,), 0.5, 3.0, ((0, 2),))
    w_out = centred(arg_keys[10], (D, D), (D // 16) ** -0.5, 0.875, ((0, 2),))
    bias_attn_out = centred(arg_keys[11], (D,), 0.3, 2.0)
    gain_norm2 = jnp.clip(1.0 + 0.1 * jax.random.normal(arg_keys[12], (D,), jnp.float32), 0.5, 1.5).astype(jnp.bfloat16)
    bias_norm2 = centred(arg_keys[13], (D,), 0.3, 2.0)
    w_up = centred(arg_keys[14], (D, FF), D ** -0.5, 0.21875, ((1, 2),))
    bias_up = centred(arg_keys[15], (FF,), 0.5, 3.0, ((0, 2),))
    w_down = centred(arg_keys[16], (FF, D), FF ** -0.5, 0.109375, ((0, 2),))
    bias_down = centred(arg_keys[17], (D,), 0.3, 2.0)
    cotangent = centred(arg_keys[18], (TOKENS, D), 1.0, 6.0, ((0, 32),))
    return {"input_rows": input_rows, "first_values": first_values, "doc_split": doc_split, "gain_norm1": gain_norm1, "bias_norm1": bias_norm1, "w_query": w_query, "bias_query": bias_query, "w_key": w_key, "w_value": w_value, "bias_value": bias_value, "w_out": w_out, "bias_attn_out": bias_attn_out, "gain_norm2": gain_norm2, "bias_norm2": bias_norm2, "w_up": w_up, "bias_up": bias_up, "w_down": w_down, "bias_down": bias_down, "cotangent": cotangent}


@jax.custom_vjp
def low(v):
    return lax.optimization_barrier(v.astype(jnp.bfloat16)).astype(jnp.float32)

@jax.custom_vjp
def low_back(v):
    return v

def low_keep(v):
    return (low(v), None)

def low_pass(kept, grad):
    return (grad,)

def back_keep(v):
    return (v, None)

def back_low(kept, grad):
    return (low(grad),)
low.defvjp(low_keep, low_pass)
low_back.defvjp(back_keep, back_low)

def layer_norm(rows_in, norm_gain, norm_shift):
    center = lax.optimization_barrier(jnp.mean(rows_in, axis=1, keepdims=True))
    centered = rows_in - center
    inverse = lax.rsqrt(lax.optimization_barrier(jnp.mean(centered * centered, axis=1, keepdims=True)) + 1e-05)
    return centered * inverse * norm_gain + norm_shift

def matmul(left_array, right_array):
    return jnp.dot(left_array, right_array, precision=lax.Precision.HIGHEST)

def group_forward(rows_in, first_rows, boundary, params):
    gain_one, shift_one, w_query, bias_query, w_key, w_value, bias_value, w_out, bias_attn, gain_two, shift_two, w_up, bias_up, w_down, bias_down = params
    group_rows = rows_in.shape[0]
    ln_one = low(layer_norm(rows_in, gain_one, shift_one))
    queries = low_back(low(matmul(ln_one, w_query) + bias_query)).reshape(group_rows, HEADS, HEAD_DIM)
    key_rows = low_back(low(matmul(ln_one, w_key))).reshape(group_rows, HEADS, HEAD_DIM)
    fresh_values = low_back(low(matmul(ln_one, w_value) + bias_value)).reshape(group_rows, 2, HEADS // 4, HEAD_DIM)
    reused = first_rows.reshape(group_rows, 2, HEADS // 4, HEAD_DIM)
    values = jnp.concatenate([fresh_values, reused], axis=2).reshape(group_rows, HEADS, HEAD_DIM)
    scores = jnp.einsum('qhd,khd->hqk', queries, key_rows, precision=lax.Precision.HIGHEST)
    scores = low_back(scores * HEAD_DIM ** (-0.5))
    position = jnp.arange(group_rows, dtype=jnp.int32)
    document = (position >= boundary).astype(jnp.int32)
    allowed = (position[None, :] <= position[:, None]) & (document[None, :] == document[:, None])
    scores = jnp.where(allowed[None], scores, -1000000000.0)
    top_score = lax.optimization_barrier(jnp.max(scores, axis=2, keepdims=True))
    weights_exp = jnp.exp(scores - top_score)
    probabilities = low(weights_exp / lax.optimization_barrier(jnp.sum(weights_exp, axis=2, keepdims=True)))
    attended = jnp.einsum('hqk,khd->qhd', probabilities, values, precision=lax.Precision.HIGHEST)
    attended = low_back(low(attended)).reshape(group_rows, HEADS * HEAD_DIM)
    middle = rows_in + low_back(matmul(attended, w_out) + bias_attn)
    ln_two = low(layer_norm(middle, gain_two, shift_two))
    hidden = low_back(matmul(ln_two, w_up) + bias_up)
    activated = low(jax.nn.gelu(hidden, approximate=True))
    return middle + low_back(matmul(activated, w_down) + bias_down)

def reference(input_rows, first_values, doc_split, gain_norm1, bias_norm1, w_query, bias_query, w_key, w_value, bias_value, w_out, bias_attn_out, gain_norm2, bias_norm2, w_up, bias_up, w_down, bias_down, cotangent):
    params = tuple((weight.astype(jnp.float32) for weight in (gain_norm1, bias_norm1, w_query, bias_query, w_key, w_value, bias_value, w_out, bias_attn_out, gain_norm2, bias_norm2, w_up, bias_up, w_down, bias_down)))
    inputs_all = input_rows.astype(jnp.float32).reshape(N_DP, GROUP_TOK, D)
    firsts_all = first_values.astype(jnp.float32).reshape(N_DP, GROUP_TOK, VDIM)
    cotangents = cotangent.astype(jnp.float32).reshape(N_DP, GROUP_TOK, D)

    def group_step(totals, group_item):
        rows_in, first_rows, cot_rows, boundary = group_item
        result, pullback = jax.vjp(lambda arg_rows, arg_first, arg_params: group_forward(arg_rows, arg_first, boundary, arg_params), rows_in, first_rows, params)
        grad_rows, grad_first, grad_params = pullback(cot_rows)
        totals = tuple((total_now + grad_now for total_now, grad_now in zip(totals, grad_params)))
        return (totals, (result.astype(jnp.bfloat16), grad_rows, grad_first))
    zeros_init = tuple((jnp.zeros_like(weight) for weight in params))
    totals, (results, grads_in, grads_first) = lax.scan(group_step, zeros_init, (inputs_all, firsts_all, cotangents, doc_split.astype(jnp.int32)))
    return (results.reshape(TOKENS, D), grads_in.reshape(TOKENS, D), grads_first.reshape(TOKENS, VDIM), totals[0], totals[1], totals[2], totals[3], totals[4], totals[5], totals[6], totals[7], totals[8], totals[9], totals[10], totals[11], totals[12], totals[13], totals[14])
```

```python
import functools

import jax
import jax.numpy as jnp
from jax import lax
from jax.experimental import pallas as pl
from jax.experimental.pallas import tpu as pltpu
from jax.sharding import PartitionSpec as P

HEAD_DIM = 64
NORM_EPS = 1e-05
GELU_ROOT = 0.7978845608028654
GELU_CUBE = 0.044715
NN = (((1,), (0,)), ((), ()))
NT = (((1,), (1,)), ((), ()))
TN = (((0,), (0,)), ((), ()))
F32 = jnp.float32
BF16 = jnp.bfloat16
VMEM_LIMIT = 60 << 20


def dot(left, right, dims=NN):
    return lax.dot_general(left, right, dims, preferred_element_type=F32)


def whole(array):
    return pl.BlockSpec(array.shape, lambda *_, nd=array.ndim: (0,) * nd)


def whole_shape(shape):
    return pl.BlockSpec(shape, lambda *_, nd=len(shape): (0,) * nd)


def row_normalize(rows):
    centered = rows - jnp.mean(rows, axis=1, keepdims=True)
    inverse = lax.rsqrt(jnp.mean(centered * centered, axis=1, keepdims=True) + NORM_EPS)
    return centered * inverse, inverse


def row_normalize_back(scaled, normed, inverse):
    return inverse * (
        scaled
        - jnp.mean(scaled, axis=1, keepdims=True)
        - normed * jnp.mean(scaled * normed, axis=1, keepdims=True)
    )


def project_kernel(place, x_own, x_other, first, gain, bias, wq, bq, wk, wv, bv, ln, qt, k, kt, v, vt):
    step = pl.program_id(0)
    rows = jnp.where(step == 0, x_own[...], x_other[...]).astype(F32)
    normed, _ = row_normalize(rows)
    low = (normed * gain[...].astype(F32) + bias[...].astype(F32)).astype(BF16)
    ln[...] = low
    scale = HEAD_DIM ** (-0.5)
    queries = (dot(low, wq[...]) + bq[...].astype(F32)).astype(BF16).astype(F32) * scale
    qt[...] = queries.astype(BF16).T
    keys = dot(low, wk[...]).astype(BF16)
    k[...] = keys
    kt[...] = keys.T
    fresh = (dot(low, wv[...]) + bv[...].astype(F32)).astype(BF16)
    values = jnp.concatenate([fresh, first[...]], axis=1)
    v[...] = values
    vt[...] = values.T


def project(place, x_own, x_other, first, gain, bias, wq, bq, wk, wv, bv):
    rows, width = x_own.shape
    heads = wq.shape[1]

    def spot(j, place):
        return jnp.where(j == 0, place[0], 1 - place[0])

    shapes = (
        ((2 * rows, width), (rows, width), lambda j, p: (spot(j, p), 0)),
        ((heads, 2 * rows), (heads, rows), lambda j, p: (0, spot(j, p))),
        ((2 * rows, heads), (rows, heads), lambda j, p: (spot(j, p), 0)),
        ((heads, 2 * rows), (heads, rows), lambda j, p: (0, spot(j, p))),
        ((2 * rows, heads), (rows, heads), lambda j, p: (spot(j, p), 0)),
        ((heads, 2 * rows), (heads, rows), lambda j, p: (0, spot(j, p))),
    )
    operands = (x_own, x_other, first, gain, bias, wq, bq, wk, wv, bv)
    specs = [whole(a) for a in operands]
    specs[2] = pl.BlockSpec((rows, first.shape[1]), lambda j, p: (spot(j, p), 0))
    return pl.pallas_call(
        project_kernel,
        out_shape=[jax.ShapeDtypeStruct(s, BF16) for s, _, _ in shapes],
        grid_spec=pltpu.PrefetchScalarGridSpec(
            num_scalar_prefetch=1,
            grid=(2,),
            in_specs=specs,
            out_specs=[pl.BlockSpec(b, m) for _, b, m in shapes],
        ),
        compiler_params=pltpu.CompilerParams(vmem_limit_bytes=VMEM_LIMIT),
        name="project",
    )(place, *operands)


def causal(size):
    keys = lax.broadcasted_iota(jnp.int32, (size, size), 0)
    return keys <= lax.broadcasted_iota(jnp.int32, (size, size), 1)


def query_blocks(tokens, block, two_docs, body):
    half = tokens // 2
    for start in range(0, tokens, block):
        if start < half:
            body(start, 0)
        else:

            @pl.when(two_docs)
            def _():
                body(start, half)

            @pl.when(jnp.logical_not(two_docs))
            def _():
                body(start, 0)


def attend_kernel(block, split, qt, k, vt, attended, lse, sums):
    width, tokens = qt.shape
    two_docs = split[0] < tokens
    ones = (lax.broadcasted_iota(jnp.int32, (16, tokens), 0) == 0).astype(BF16)
    sums[0, HEAD_DIM:, :] = ones
    sums[1, HEAD_DIM:, :] = ones

    def pair_step(pair, _):
        col = pl.multiple_of(pair * 2 * HEAD_DIM, 2 * HEAD_DIM)
        sums[0, :HEAD_DIM, :] = vt[pl.ds(col, HEAD_DIM), :]
        sums[1, :HEAD_DIM, :] = vt[pl.ds(col + HEAD_DIM, HEAD_DIM), :]
        owner = lax.broadcasted_iota(jnp.int32, (2 * HEAD_DIM, block), 0) // HEAD_DIM

        def body(start, low):
            stop = start + block
            inner = start - low
            queries = qt[pl.ds(col, 2 * HEAD_DIM), start:stop]
            keys = k[low:stop, pl.ds(col, 2 * HEAD_DIM)]
            scores = [
                dot(keys, jnp.where(owner == j, queries, jnp.zeros_like(queries))) for j in range(2)
            ]
            for j in range(2):
                edge = jnp.where(causal(block), scores[j][inner:], -1e30)
                top = jnp.max(edge, axis=0, keepdims=True)
                if inner:
                    near = scores[j][:inner]
                    top = jnp.maximum(top, jnp.max(near, axis=0, keepdims=True))
                    weights = jnp.concatenate(
                        [jnp.exp(near - top).astype(BF16), jnp.exp(edge - top).astype(BF16)], axis=0
                    )
                else:
                    weights = jnp.exp(edge - top).astype(BF16)
                total = dot(sums[j, :, low:stop], weights)
                denominator = total[HEAD_DIM : HEAD_DIM + 1]
                attended[pl.ds(col + HEAD_DIM * j, HEAD_DIM), start:stop] = (
                    total[:HEAD_DIM] * (1.0 / denominator)
                ).astype(BF16)
                lse[pl.ds(pair * 2 + j, 1), :, start:stop] = (top + jnp.log(denominator))[None]

        query_blocks(tokens, block, two_docs, body)
        return 0

    lax.fori_loop(0, width // (2 * HEAD_DIM), pair_step, 0)


def attend(split, qt, k, vt, block=512):
    width, tokens = qt.shape
    vmem = pl.BlockSpec(memory_space=pltpu.VMEM)
    return pl.pallas_call(
        functools.partial(attend_kernel, block),
        out_shape=(
            jax.ShapeDtypeStruct((width, tokens), BF16),
            jax.ShapeDtypeStruct((width // HEAD_DIM, 1, tokens), F32),
        ),
        in_specs=[pl.BlockSpec(memory_space=pltpu.SMEM), vmem, vmem, vmem],
        out_specs=(vmem, vmem),
        scratch_shapes=[pltpu.VMEM((2, HEAD_DIM + 16, tokens), BF16)],
        compiler_params=pltpu.CompilerParams(vmem_limit_bytes=VMEM_LIMIT),
        name="attend",
    )(split, qt, k, vt)


def extra_rows(row):
    high = row.astype(BF16).astype(F32)
    middle = (row - high).astype(BF16).astype(F32)
    low = row - high - middle
    index = lax.broadcasted_iota(jnp.int32, (HEAD_DIM, row.shape[1]), 0)
    rest = jnp.where(index == 2, low, 0.0)
    return jnp.where(index == 0, high, jnp.where(index == 1, middle, rest)).astype(BF16)


def attend_back_kernel(
    block, split, place, qt, k, kt, v, do_own, do_other, attended, lse,
    dqt, dkt, dvt, grads, q_aug, d_aug, k_aug, v_aug, dk_sum, dv_sum,
):
    width, tokens = qt.shape
    half = tokens // 2
    two_docs = split[0] < tokens
    own = pl.multiple_of(place[0] * half, half)
    other = pl.multiple_of((1 - place[0]) * half, half)
    grads[:, pl.ds(own, half)] = do_own[...]
    grads[:, pl.ds(other, half)] = do_other[...]

    def pair_step(pair, _):
        col = pl.multiple_of(pair * 2 * HEAD_DIM, 2 * HEAD_DIM)
        lane = lax.broadcasted_iota(jnp.int32, (tokens, 2 * HEAD_DIM), 1)
        ones = jnp.where(lax.rem(lane, HEAD_DIM) < 3, 1.0, 0.0).astype(BF16)
        keys = k[:, pl.ds(col, 2 * HEAD_DIM)]
        values = v[:, pl.ds(col, 2 * HEAD_DIM)]
        dk_sum[...] = jnp.zeros_like(dk_sum)
        dv_sum[...] = jnp.zeros_like(dv_sum)
        head_rows = [pl.ds(pl.multiple_of(col + HEAD_DIM * j, HEAD_DIM), HEAD_DIM) for j in range(2)]
        for j in range(2):
            mine = lane // HEAD_DIM == j
            k_aug[j] = jnp.where(mine, keys, ones)
            v_aug[j] = jnp.where(mine, values, ones)
            grad = grads[head_rows[j], :]
            inner = jnp.sum(
                grad.astype(F32) * attended[head_rows[j], :].astype(F32), axis=0, keepdims=True
            )
            base, extra = HEAD_DIM * j, HEAD_DIM * (1 - j)
            q_aug[j, base : base + HEAD_DIM, :] = qt[head_rows[j], :]
            q_aug[j, extra : extra + HEAD_DIM, :] = extra_rows(-lse[pl.ds(pair * 2 + j, 1)][0])
            d_aug[j, base : base + HEAD_DIM, :] = grad
            d_aug[j, extra : extra + HEAD_DIM, :] = extra_rows(-inner)

        def body(start, low):
            stop = start + block
            inner = start - low
            for j in range(2):
                scores = dot(k_aug[j, low:stop, :], q_aug[j, :, start:stop])
                grad_probs = dot(v_aug[j, low:stop, :], d_aug[j, :, start:stop])
                probs = jnp.where(causal(block), jnp.exp(scores[inner:]), 0.0)
                if inner:
                    probs = jnp.concatenate([jnp.exp(scores[:inner]), probs], axis=0)
                grad_scores = (probs * grad_probs).astype(BF16)
                probs = probs.astype(BF16)
                rows = head_rows[j]
                dqt[rows, start:stop] = (
                    dot(kt[rows, low:stop], grad_scores) * HEAD_DIM ** (-0.5)
                ).astype(BF16)
                dv_sum[j, :, low:stop] += dot(grads[rows, start:stop], probs, NT)
                dk_sum[j, :, low:stop] += dot(qt[rows, start:stop], grad_scores, NT)

        query_blocks(tokens, block, two_docs, body)
        for j in range(2):
            dkt[head_rows[j], :] = dk_sum[j].astype(BF16)
            dvt[head_rows[j], :] = dv_sum[j]
        return 0

    lax.fori_loop(0, width // (2 * HEAD_DIM), pair_step, 0)


def attend_back(split, place, qt, k, kt, v, do_own, do_other, attended, lse, block=512):
    width, tokens = qt.shape
    vmem = pl.BlockSpec(memory_space=pltpu.VMEM)
    smem = pl.BlockSpec(memory_space=pltpu.SMEM)
    pair = 2 * HEAD_DIM
    return pl.pallas_call(
        functools.partial(attend_back_kernel, block),
        out_shape=(
            jax.ShapeDtypeStruct((width, tokens), BF16),
            jax.ShapeDtypeStruct((width, tokens), BF16),
            jax.ShapeDtypeStruct((width, tokens), F32),
        ),
        in_specs=[smem, smem] + [vmem] * 8,
        out_specs=(vmem, vmem, vmem),
        scratch_shapes=[
            pltpu.VMEM((width, tokens), BF16),
            pltpu.VMEM((2, pair, tokens), BF16),
            pltpu.VMEM((2, pair, tokens), BF16),
            pltpu.VMEM((2, tokens, pair), BF16),
            pltpu.VMEM((2, tokens, pair), BF16),
            pltpu.VMEM((2, HEAD_DIM, tokens), F32),
            pltpu.VMEM((2, HEAD_DIM, tokens), F32),
        ],
        compiler_params=pltpu.CompilerParams(vmem_limit_bytes=VMEM_LIMIT),
        name="attend_back",
    )(split, place, qt, k, kt, v, do_own, do_other, attended, lse)


def gelu_both(v):
    square = v * v
    tanh = jnp.tanh(v * (GELU_ROOT + (GELU_ROOT * GELU_CUBE) * square))
    half = 0.5 * v
    slope = 0.5 + 0.5 * tanh + half * (1.0 - tanh * tanh) * (
        GELU_ROOT + (3.0 * GELU_ROOT * GELU_CUBE) * square
    )
    return half + half * tanh, slope


def feed_kernel(
    steps, x, cot, att_own, att_other, wo_own, wo_other, bias_o, gain, bias,
    up_other, up_own, bu_other, bu_own, down_other, down_own, bias_d,
    out, grad_mid, grad_att, grad_up, grad_down, grad_wo, grad_bu, small,
    ln, ln_t, normed, inverse, middle, total, grad_ln,
):
    step = pl.program_id(0)
    heads = att_own.shape[0]

    @pl.when(step == 0)
    def _():
        branch = dot(att_own[...], wo_own[...], TN) + dot(att_other[...], wo_other[...], TN)
        mid = x[...].astype(F32) + (branch + bias_o[...].astype(F32))
        middle[...] = mid
        norm, inv = row_normalize(mid)
        normed[...] = norm
        inverse[...] = jnp.broadcast_to(inv, inverse.shape)
        low = (norm * gain[...].astype(F32) + bias[...].astype(F32)).astype(BF16)
        ln[...] = low
        ln_t[...] = low.T
        total[...] = jnp.zeros_like(total)
        grad_ln[...] = jnp.zeros_like(grad_ln)

    def chunk(up, bias_up, down):
        hidden = dot(ln[...], up[...]) + bias_up[...].astype(F32)
        act, slope = gelu_both(hidden)
        act = act.astype(BF16)
        grad_hidden = (dot(cot[...], down[...], NT) * slope).astype(BF16)
        total[...] += dot(act, down[...])
        grad_ln[...] += dot(grad_hidden, up[...], NT)
        grad_down[0] = dot(act, cot[...], TN).astype(BF16)
        grad_up[0] = dot(ln_t[...], grad_hidden).astype(BF16)
        grad_bu[0] = jnp.sum(grad_hidden.astype(F32), axis=0, keepdims=True)

    @pl.when(step < steps // 2)
    def _():
        chunk(up_other, bu_other, down_other)

    @pl.when(step >= steps // 2)
    def _():
        chunk(up_own, bu_own, down_own)

    @pl.when(step == steps - 1)
    def _():
        out[...] = (middle[...] + (total[...] + bias_d[...].astype(F32))).astype(BF16)
        grad = grad_ln[...]
        norm = normed[...]
        cot32 = cot[...].astype(F32)
        back = row_normalize_back(grad * gain[...].astype(F32), norm, inverse[:, :1])
        mid = cot32 + back
        grad_mid[...] = mid
        low = mid.astype(BF16)
        small[0:1, :] = jnp.sum(grad * norm, axis=0, keepdims=True)
        small[1:2, :] = jnp.sum(grad, axis=0, keepdims=True)
        small[2:3, :] = jnp.sum(low.astype(F32), axis=0, keepdims=True)
        small[3:4, :] = jnp.sum(cot32, axis=0, keepdims=True)
        grad_wo[:heads] = dot(att_own[...], low).astype(BF16)
        grad_wo[heads:] = dot(att_other[...], low).astype(BF16)
        grad_att[:heads] = dot(wo_own[...], low, NT).astype(BF16)
        grad_att[heads:] = dot(wo_other[...], low, NT).astype(BF16)


def feed(
    x, cot, att_own, att_other, wo_own, wo_other, bias_o, gain, bias,
    up_other, up_own, bu_other, bu_own, down_other, down_own, bias_d, chunk=512,
):
    rows, width = x.shape
    hidden = up_own.shape[1]
    steps = 2 * hidden // chunk
    half = steps // 2
    heads = att_own.shape[0]

    def first(j):
        return jnp.minimum(j, half - 1)

    def second(j):
        return jnp.maximum(j - half, 0)

    operands = (
        x, cot, att_own, att_other, wo_own, wo_other, bias_o, gain, bias,
        up_other, up_own, bu_other, bu_own, down_other, down_own, bias_d,
    )
    specs = [whole(a) for a in operands]
    specs[9] = pl.BlockSpec((width, chunk), lambda j: (0, first(j)))
    specs[10] = pl.BlockSpec((width, chunk), lambda j: (0, second(j)))
    specs[11] = pl.BlockSpec((1, chunk), lambda j: (0, first(j)))
    specs[12] = pl.BlockSpec((1, chunk), lambda j: (0, second(j)))
    specs[13] = pl.BlockSpec((chunk, width), lambda j: (first(j), 0))
    specs[14] = pl.BlockSpec((chunk, width), lambda j: (second(j), 0))
    results = [
        ((rows, width), BF16),
        ((rows, width), F32),
        ((2 * heads, rows), BF16),
        ((2, width, hidden), BF16),
        ((2, hidden, width), BF16),
        ((2 * heads, width), BF16),
        ((2, 1, hidden), F32),
        ((8, width), F32),
    ]
    out_specs = [whole_shape(s) for s, _ in results]
    out_specs[3] = pl.BlockSpec((1, width, chunk), lambda j: (j // half, 0, lax.rem(j, half)))
    out_specs[4] = pl.BlockSpec((1, chunk, width), lambda j: (j // half, lax.rem(j, half), 0))
    out_specs[6] = pl.BlockSpec((1, 1, chunk), lambda j: (j // half, 0, lax.rem(j, half)))
    return pl.pallas_call(
        functools.partial(feed_kernel, steps),
        grid=(steps,),
        in_specs=specs,
        out_specs=out_specs,
        out_shape=[jax.ShapeDtypeStruct(s, t) for s, t in results],
        scratch_shapes=[
            pltpu.VMEM((rows, width), BF16),
            pltpu.VMEM((width, rows), BF16),
            pltpu.VMEM((rows, width), F32),
            pltpu.VMEM((rows, 128), F32),
            pltpu.VMEM((rows, width), F32),
            pltpu.VMEM((rows, width), F32),
            pltpu.VMEM((rows, width), F32),
        ],
        compiler_params=pltpu.CompilerParams(vmem_limit_bytes=VMEM_LIMIT),
        name="feed",
    )(*operands)


def swap(array):
    return lax.ppermute(array, "tensor", [(0, 1), (1, 0)])


def on_device(
    input_rows, first_values, doc_split, gain_norm1, bias_norm1, w_query, bias_query, w_key,
    w_value, bias_value, w_out, bias_attn_out, gain_norm2, bias_norm2, w_up, bias_up, w_down,
    bias_down, cotangent,
):
    rows = input_rows.shape[0]
    heads = w_query.shape[1]
    fresh = w_value.shape[1]
    here = lax.axis_index("tensor")
    place = here.reshape(1).astype(jnp.int32)
    row = lambda a: a.reshape(1, -1)
    x_other = swap(input_rows)
    ln, qt, k, kt, v, vt = project(
        place, input_rows, x_other, first_values, row(gain_norm1), row(bias_norm1), w_query,
        row(bias_query), w_key, w_value, row(bias_value),
    )
    up_other, down_other, wo_other = swap(w_up), swap(w_down), swap(w_out)
    bu_other = swap(row(bias_up))
    attended, lse = attend(doc_split, qt, k, vt)
    mine = lambda a: lax.dynamic_slice_in_dim(a, here * rows, rows, 1)
    theirs = lambda a: lax.dynamic_slice_in_dim(a, (1 - here) * rows, rows, 1)
    att_other = swap(theirs(attended))
    output, grad_middle, grad_att, grad_up, grad_down, grad_wo, grad_bu, small = feed(
        input_rows, cotangent, mine(attended), att_other, w_out, wo_other, row(bias_attn_out),
        row(gain_norm2), row(bias_norm2), up_other, w_up, row(bu_other), row(bias_up), down_other,
        w_down, row(bias_down),
    )
    do_other = swap(grad_att[heads:])
    joined = lambda a: (a[1].astype(F32) + swap(a[0]).astype(F32)).astype(BF16)
    grad_up = joined(grad_up)
    grad_down = joined(grad_down)
    grad_wo = (grad_wo[:heads].astype(F32) + swap(grad_wo[heads:]).astype(F32)).astype(BF16)
    grad_bu = grad_bu[1, 0] + swap(grad_bu[0, 0])
    dqt, dkt, dvt = attend_back(
        doc_split, place, qt, k, kt, v, grad_att[:heads], do_other, attended, lse
    )
    grad_first = dvt[fresh:].T
    dft = dvt[:fresh].astype(BF16)
    stack = jnp.concatenate([dqt, dkt, dft], axis=0)
    weights = jnp.concatenate([w_query, w_key, w_value], axis=1)
    grad_qkv = dot(ln, stack, (((0,), (1,)), ((), ()))).astype(BF16)
    bias_sums = jnp.sum(stack.astype(F32), axis=1)
    terms_other = dot(theirs(stack), weights, (((0,), (1,)), ((), ()))).astype(BF16)
    terms = dot(mine(stack), weights, (((0,), (1,)), ((), ())))
    grad_ln = terms + swap(terms_other).astype(F32)
    normed, inverse = row_normalize(input_rows.astype(F32))
    grad_input = grad_middle + row_normalize_back(
        grad_ln * gain_norm1.astype(F32), normed, inverse
    )
    grad_up, grad_down, grad_wo, grad_qkv = lax.psum(
        (grad_up, grad_down, grad_wo, grad_qkv), "dp"
    )
    grad_bu, bias_sums = lax.psum((grad_bu, bias_sums), "dp")
    gain_one, shift_one, small = lax.psum(
        (jnp.sum(grad_ln * normed, axis=0), jnp.sum(grad_ln, axis=0), small[:4]), ("dp", "tensor")
    )
    grad_qkv = grad_qkv.astype(F32)
    return (
        output,
        grad_input,
        grad_first,
        gain_one,
        shift_one,
        grad_qkv[:, :heads],
        bias_sums[:heads],
        grad_qkv[:, heads : 2 * heads],
        grad_qkv[:, 2 * heads :],
        bias_sums[2 * heads :],
        grad_wo.astype(F32),
        small[2],
        small[0],
        small[1],
        grad_up.astype(F32),
        grad_bu,
        grad_down.astype(F32),
        small[3],
    )


def solution(mesh):
    rows = P(("dp", "tensor"), None)
    cols = P(None, "tensor")
    split = P("tensor")
    firsts = P("dp", "tensor")
    wide = P("tensor", None)
    return jax.shard_map(
        on_device,
        mesh=mesh,
        in_specs=(
            rows, firsts, P("dp"), P(), P(), cols, split, cols, cols, split, wide, P(), P(), P(),
            cols, split, wide, P(), rows,
        ),
        out_specs=(
            rows, rows, firsts, P(), P(), cols, split, cols, cols, split, wide, P(), P(), P(),
            cols, split, wide, P(),
        ),
        check_vma=False,
    )
```

```python
import functools

import jax
import jax.numpy as jnp
from jax import lax
from jax.experimental import pallas as pl
from jax.experimental.pallas import tpu as pltpu
from jax.sharding import PartitionSpec as P

HEAD_DIM = 64
NORM_EPS = 1e-05
GELU_ROOT = 0.7978845608028654
GELU_CUBE = 0.044715
NN = (((1,), (0,)), ((), ()))
NT = (((1,), (1,)), ((), ()))
TN = (((0,), (0,)), ((), ()))
F32 = jnp.float32
BF16 = jnp.bfloat16
VMEM_LIMIT = 60 << 20
MESH = pl.DeviceIdType.MESH


def dot(left, right, dims=NN):
    return lax.dot_general(left, right, dims, preferred_element_type=F32)


def whole(array):
    return pl.BlockSpec(array.shape, lambda *_, nd=array.ndim: (0,) * nd)


def whole_shape(shape):
    return pl.BlockSpec(shape, lambda *_, nd=len(shape): (0,) * nd)


def row_normalize(rows):
    centered = rows - jnp.mean(rows, axis=1, keepdims=True)
    inverse = lax.rsqrt(jnp.mean(centered * centered, axis=1, keepdims=True) + NORM_EPS)
    return centered * inverse, inverse


def row_normalize_back(scaled, normed, inverse):
    return inverse * (
        scaled
        - jnp.mean(scaled, axis=1, keepdims=True)
        - normed * jnp.mean(scaled * normed, axis=1, keepdims=True)
    )


AXES = ("x", "y", "z")
SIZE = {"x": 2, "y": 2, "z": 4}


class Place:
    def __init__(self, row_chips):
        index = lax.axis_index("dp")
        self.core = lax.axis_index("tensor")
        self.wide = row_chips
        self.index = index
        self.x = lax.rem(index, row_chips)
        self.y = lax.rem(index // row_chips, row_chips)
        self.z = index // (row_chips * row_chips)
        self.at = {"x": lax.rem(self.x, 2), "y": lax.rem(self.y, 2), "z": self.z}

    def peer(self, axis, step):
        size = SIZE[axis]
        spot = lax.rem(self.at[axis] + step, size)
        stride = {"x": 1, "y": self.wide, "z": self.wide * self.wide}[axis]
        return spot, (self.index + (spot - self.at[axis]) * stride, self.core)

    def twin(self):
        return (self.index, 1 - self.core)

    def others(self):
        return [self.twin()] + [self.peer(a, k)[1] for a in AXES for k in range(1, SIZE[a])]


def greet(place):
    barrier = pltpu.get_barrier_semaphore()
    devices = place.others()
    for device in devices:
        pl.semaphore_signal(barrier, inc=1, device_id=device, device_id_type=MESH)
    return lambda: pl.semaphore_wait(barrier, len(devices))


class Sum:
    def __init__(self, place, order, held, slots, result, sems):
        self.place, self.order, self.held = place, order, held
        self.slots, self.result, self.sems = slots, result, sems
        self.rows = (held if held is not None else result).shape[0]

    def region(self, depth):
        start, size = 0, self.rows
        for axis in self.order[:depth]:
            size //= SIZE[axis]
            start = start + self.place.at[axis] * size
        return start, size

    def span(self, depth):
        start, size = self.region(depth)
        return pl.ds(pl.multiple_of(start, 16) if depth else start, size)

    def first_sem(self, gather, stage):
        count = 0
        for axis in self.order[:stage]:
            count += SIZE[axis] - 1
        return count + (5 if gather else 0)

    def scatter_copies(self, stage):
        axis = self.order[stage]
        start, size = self.region(stage)
        piece = size // SIZE[axis]
        base = self.first_sem(False, stage)
        copies = []
        for step in range(1, SIZE[axis]):
            spot, device = self.place.peer(axis, step)
            copies.append(
                pltpu.make_async_remote_copy(
                    src_ref=self.held.at[pl.ds(pl.multiple_of(start + spot * piece, 16), piece), :],
                    dst_ref=self.slots[stage].at[step - 1],
                    send_sem=self.sems.at[0, base + step - 1],
                    recv_sem=self.sems.at[1, base + step - 1],
                    device_id=device,
                    device_id_type=MESH,
                )
            )
        return copies

    def scatter_end(self, stage):
        for copy in self.scatter_copies(stage):
            copy.wait()
        span = self.span(stage + 1)
        total = self.held[span, :].astype(F32)
        for step in range(SIZE[self.order[stage]] - 1):
            total = total + self.slots[stage][step].astype(F32)
        self.held[span, :] = total.astype(BF16)

    def gather_copies(self, stage, source):
        axis = self.order[stage]
        span = self.span(stage + 1)
        base = self.first_sem(True, stage)
        copies = []
        origin = self.result if source is None else source
        for step in range(1, SIZE[axis]):
            _, device = self.place.peer(axis, step)
            copies.append(
                pltpu.make_async_remote_copy(
                    src_ref=origin.at[span, :],
                    dst_ref=self.result.at[span, :],
                    send_sem=self.sems.at[0, base + step - 1],
                    recv_sem=self.sems.at[1, base + step - 1],
                    device_id=device,
                    device_id_type=MESH,
                )
            )
        if source is not None:
            copies.append(
                pltpu.make_async_copy(
                    source.at[span, :], self.result.at[span, :], self.sems.at[0, 10]
                )
            )
        return copies

    def run(self, action, source=None):
        verb, letter = action
        gather = letter in "cba"
        stage = "abc".index(letter) if gather else "ABC".index(letter)
        if gather:
            for copy in self.gather_copies(stage, source):
                copy.start() if verb == "s" else copy.wait()
        elif verb == "s":
            for copy in self.scatter_copies(stage):
                copy.start()
        else:
            self.scatter_end(stage)


def slot_shapes(order, rows, cols, stages="ABC"):
    shapes = []
    for letter, axis in zip("ABC", order):
        rows //= SIZE[axis]
        if letter in stages:
            shapes.append((SIZE[axis] - 1, rows, cols))
    return shapes


def as_slots(refs, stages="ABC"):
    refs = list(refs)
    return [refs.pop(0) if letter in stages else None for letter in "ABC"]


def project_kernel(
    x, first_t, gain, bias, wq, bq, wk, wv_t, bv, ln, qt, k, kt, v, vt,
    x_other, weights, s_ln, s_qt, s_k, s_kt, s_v, s_vt, pair_sems, out_sems,
):
    rows = x.shape[0]
    heads, fresh = wq.shape[1], wv_t.shape[0]
    core = lax.axis_index("tensor")
    twin = (lax.axis_index("dp"), 1 - core)
    barrier = pltpu.get_barrier_semaphore()
    pl.semaphore_signal(barrier, inc=1, device_id=twin, device_id_type=MESH)
    weights[:, :heads] = wq[...]
    weights[:, heads : 2 * heads] = wk[...]
    weights[:, 2 * heads :] = wv_t[...].T
    pl.semaphore_wait(barrier, 1)
    send = pltpu.make_async_remote_copy(
        src_ref=x, dst_ref=x_other, send_sem=pair_sems.at[0], recv_sem=pair_sems.at[1],
        device_id=twin, device_id_type=MESH,
    )
    send.start()
    gain_row = gain[...].astype(F32).reshape(1, -1)
    bias_row = bias[...].astype(F32).reshape(1, -1)
    bq_row = bq[...].astype(F32).reshape(1, -1)
    bv_row = bv[...].astype(F32).reshape(1, -1)
    copies = []
    for part, source in enumerate((x, x_other)):
        if part:
            send.wait_recv()
        spot = pl.multiple_of((core if part == 0 else 1 - core) * rows, rows)
        normed, _ = row_normalize(source[...].astype(F32))
        low = (normed * gain_row + bias_row).astype(BF16)
        s_ln[part] = low
        product = dot(low, weights[...])
        queries = (product[:, :heads] + bq_row).astype(BF16).astype(F32) * HEAD_DIM ** (-0.5)
        s_qt[part] = queries.astype(BF16).T
        keys = product[:, heads : 2 * heads].astype(BF16)
        s_k[part] = keys
        s_kt[part] = keys.T
        values = (product[:, 2 * heads :] + bv_row).astype(BF16)
        reused = first_t[:, pl.ds(spot, rows)]
        s_vt[part, :fresh] = values.T
        s_vt[part, fresh:] = reused
        s_v[part] = jnp.concatenate([values, reused.T], axis=1)
        targets = (
            (s_ln, ln.at[pl.ds(spot, rows), :]),
            (s_qt, qt.at[:, pl.ds(spot, rows)]),
            (s_k, k.at[pl.ds(spot, rows), :]),
            (s_kt, kt.at[:, pl.ds(spot, rows)]),
            (s_v, v.at[pl.ds(spot, rows), :]),
            (s_vt, vt.at[:, pl.ds(spot, rows)]),
        )
        for i, (held, target) in enumerate(targets):
            copy = pltpu.make_async_copy(held.at[part], target, out_sems.at[part, i])
            copy.start()
            copies.append(copy)
    send.wait_send()
    for copy in copies:
        copy.wait()


def project(x, first_t, gain, bias, wq, bq, wk, wv_t, bv):
    rows, width = x.shape
    heads = wq.shape[1]
    tall, flat = (rows, heads), (heads, rows)
    vmem = pl.BlockSpec(memory_space=pltpu.VMEM)
    shapes = ((2 * rows, width), (heads, 2 * rows), (2 * rows, heads)) + (
        (heads, 2 * rows), (2 * rows, heads), (heads, 2 * rows),
    )
    scratch = [(rows, width), (width, 2 * heads + wv_t.shape[0])]
    scratch += [(2,) + s for s in ((rows, width), flat, tall, flat, tall, flat)]
    return pl.pallas_call(
        project_kernel,
        out_shape=[jax.ShapeDtypeStruct(s, BF16) for s in shapes],
        in_specs=[vmem] * 9,
        out_specs=[pl.BlockSpec(memory_space=pl.ANY)] * 6,
        scratch_shapes=[pltpu.VMEM(s, BF16) for s in scratch]
        + [pltpu.SemaphoreType.DMA((2,)), pltpu.SemaphoreType.DMA((2, 6))],
        compiler_params=pltpu.CompilerParams(
            vmem_limit_bytes=VMEM_LIMIT, collective_id=1, has_side_effects=True
        ),
        name="project",
    )(x, first_t, gain, bias, wq, bq, wk, wv_t, bv)


def causal(size):
    keys = lax.broadcasted_iota(jnp.int32, (size, size), 0)
    return keys <= lax.broadcasted_iota(jnp.int32, (size, size), 1)


def query_blocks(tokens, block, two_docs, body):
    half = tokens // 2
    for start in range(0, tokens, block):
        if start < half:
            body(start, 0)
        else:

            @pl.when(two_docs)
            def _():
                body(start, half)

            @pl.when(jnp.logical_not(two_docs))
            def _():
                body(start, 0)


def attend_kernel(block, split, qt, k, vt, attended, lse, sums):
    width, tokens = qt.shape
    two_docs = split[0] < tokens
    ones = (lax.broadcasted_iota(jnp.int32, (16, tokens), 0) == 0).astype(BF16)
    sums[0, HEAD_DIM:, :] = ones
    sums[1, HEAD_DIM:, :] = ones

    def pair_step(pair, _):
        col = pl.multiple_of(pair * 2 * HEAD_DIM, 2 * HEAD_DIM)
        sums[0, :HEAD_DIM, :] = vt[pl.ds(col, HEAD_DIM), :]
        sums[1, :HEAD_DIM, :] = vt[pl.ds(col + HEAD_DIM, HEAD_DIM), :]
        owner = lax.broadcasted_iota(jnp.int32, (2 * HEAD_DIM, block), 0) // HEAD_DIM

        def body(start, low):
            stop = start + block
            inner = start - low
            queries = qt[pl.ds(col, 2 * HEAD_DIM), start:stop]
            keys = k[low:stop, pl.ds(col, 2 * HEAD_DIM)]
            scores = [
                dot(keys, jnp.where(owner == j, queries, jnp.zeros_like(queries))) for j in range(2)
            ]
            for j in range(2):
                edge = jnp.where(causal(block), scores[j][inner:], -1e30)
                top = jnp.max(edge, axis=0, keepdims=True)
                if inner:
                    near = scores[j][:inner]
                    top = jnp.maximum(top, jnp.max(near, axis=0, keepdims=True))
                    weights = jnp.concatenate(
                        [jnp.exp(near - top).astype(BF16), jnp.exp(edge - top).astype(BF16)], axis=0
                    )
                else:
                    weights = jnp.exp(edge - top).astype(BF16)
                total = dot(sums[j, :, low:stop], weights)
                denominator = total[HEAD_DIM : HEAD_DIM + 1]
                attended[pl.ds(col + HEAD_DIM * j, HEAD_DIM), start:stop] = (
                    total[:HEAD_DIM] * (1.0 / denominator)
                ).astype(BF16)
                lse[pl.ds(pair * 2 + j, 1), :, start:stop] = (top + jnp.log(denominator))[None]

        query_blocks(tokens, block, two_docs, body)
        return 0

    lax.fori_loop(0, width // (2 * HEAD_DIM), pair_step, 0)


def attend(split, qt, k, vt, block=512):
    width, tokens = qt.shape
    vmem = pl.BlockSpec(memory_space=pltpu.VMEM)
    return pl.pallas_call(
        functools.partial(attend_kernel, block),
        out_shape=(
            jax.ShapeDtypeStruct((width, tokens), BF16),
            jax.ShapeDtypeStruct((width // HEAD_DIM, 1, tokens), F32),
        ),
        in_specs=[pl.BlockSpec(memory_space=pltpu.SMEM), vmem, vmem, vmem],
        out_specs=(vmem, vmem),
        scratch_shapes=[pltpu.VMEM((2, HEAD_DIM + 16, tokens), BF16)],
        compiler_params=pltpu.CompilerParams(vmem_limit_bytes=VMEM_LIMIT),
        name="attend",
    )(split, qt, k, vt)


def gelu_both(v):
    square = v * v
    tanh = jnp.tanh(v * (GELU_ROOT + (GELU_ROOT * GELU_CUBE) * square))
    half = 0.5 * v
    slope = 0.5 + 0.5 * tanh + half * (1.0 - tanh * tanh) * (
        GELU_ROOT + (3.0 * GELU_ROOT * GELU_CUBE) * square
    )
    return half + half * tanh, slope


SUM_ROWS = 16
ROW_BU, ROW_BU_OTHER, ROW_BQ, ROW_BV = 6, 9, 12, 13


def feed_kernel(
    row_chips, x, cot, attended, wo_own, wo_other, bias_o, gain, bias,
    up_other, up_own, bu_other, bu_own, down_other, down_own, bias_d,
    out, grad_mid, grad_att, state, grad_wo, small,
    att_own, att_other, ln, normed, inverse, total, grad_ln, att_stage, stage, held,
    slots_a, slots_b, slots_c, move_sems, pair_sems, sum_sems,
):
    step = pl.program_id(0)
    place = Place(row_chips)
    core = place.core
    rows = x.shape[0]
    heads = att_own.shape[0]
    chunk = up_own.shape[1]
    index = step // 2
    own = pl.ds(pl.multiple_of(core * rows, rows), rows)
    theirs = pl.ds(pl.multiple_of((1 - core) * rows, rows), rows)

    def to_twin(source, target, i):
        return pltpu.make_async_remote_copy(
            src_ref=source, dst_ref=target, send_sem=pair_sems.at[0, i],
            recv_sem=pair_sems.at[1, i], device_id=place.twin(), device_id_type=MESH,
        )

    def stage_copy(i):
        return to_twin(stage.at[i], held.at[i], i)

    def part(i, j):
        return Sum(
            place, ("xyz", "yxz")[j], held.at[i, j],
            [slots_a.at[i, j], slots_b.at[i, j] if i < 2 else None, slots_c.at[j] if i < 1 else None],
            state.at[i, j], sum_sems.at[i, j],
        )

    def act(i, *actions):
        for action in actions:
            for j in range(2):
                part(i, j).run(action, held.at[i, j] if action[1] == "c" else None)

    @pl.when(step == 0)
    def _():
        ready = greet(place)
        local = pltpu.make_async_copy(attended.at[:, own], att_own, move_sems.at[0])
        local.start()
        ready()
        exchange = to_twin(attended.at[:, theirs], att_other, 3)
        exchange.start()
        total[...] = x[...].astype(F32) + bias_o[...].astype(F32).reshape(1, -1)
        grad_ln[...] = jnp.zeros_like(grad_ln)
        small[...] = jnp.zeros_like(small)
        local.wait()
        total[...] += dot(att_own[...], wo_own[...], TN)
        exchange.wait()
        mid = total[...] + dot(att_other[...], wo_other[...], TN)
        total[...] = mid + bias_d[...].astype(F32).reshape(1, -1)
        norm, inv = row_normalize(mid)
        normed[...] = norm
        inverse[...] = jnp.broadcast_to(inv, inverse.shape)
        ln[...] = (
            norm * gain[...].astype(F32).reshape(1, -1) + bias[...].astype(F32).reshape(1, -1)
        ).astype(BF16)

    def weight_grads(up, bias_up, down):
        hidden = dot(ln[...], up[...]) + bias_up[
            pl.ds(pl.multiple_of(index * chunk, chunk), chunk)
        ].astype(F32).reshape(1, -1)
        activated, slope = gelu_both(hidden)
        activated = activated.astype(BF16)
        grad_hidden = (dot(cot[...], down[...], NT) * slope).astype(BF16)
        grad_down = dot(activated, cot[...], TN)
        grad_up = dot(grad_hidden, ln[...], TN)
        sums = jnp.sum(grad_hidden.astype(F32), axis=0, keepdims=True)
        return activated, grad_hidden, grad_down, grad_up, sums

    def row_terms(activated, grad_hidden, up, down):
        total[...] += dot(activated, down[...])
        grad_ln[...] += dot(grad_hidden, up[...], NT)

    @pl.when(lax.rem(step, 2) == 0)
    def _():
        activated, grad_hidden, grad_down, grad_up, sums = weight_grads(
            up_other, bu_other, down_other
        )
        stage[index, 0] = grad_down.astype(BF16)
        stage[index, 1] = grad_up.astype(BF16)
        stage_copy(index).start()
        small[pl.ds(ROW_BU_OTHER + index, 1), :chunk] = sums
        row_terms(activated, grad_hidden, up_other, down_other)

        @pl.when(step == 2)
        def _():
            act(0, "fA", "sB")

        @pl.when(step == 4)
        def _():
            act(0, "fC", "sc")
            act(1, "fA", "sB")

    @pl.when(lax.rem(step, 2) == 1)
    def _():
        activated, grad_hidden, grad_down, grad_up, sums = weight_grads(up_own, bu_own, down_own)
        stage_copy(index).wait()
        held[index, 0] = (grad_down + held[index, 0].astype(F32)).astype(BF16)
        held[index, 1] = (grad_up + held[index, 1].astype(F32)).astype(BF16)
        small[pl.ds(ROW_BU + index, 1), :chunk] = sums

        @pl.when(step == 1)
        def _():
            act(0, "sA")

        @pl.when(step == 3)
        def _():
            act(0, "fB", "sC")
            act(1, "sA")

        @pl.when(step == 5)
        def _():
            act(1, "fB")
            act(2, "sA")

        row_terms(activated, grad_hidden, up_own, down_own)

    @pl.when(step == 5)
    def _():
        grad = grad_ln[...]
        norm = normed[...]
        cot32 = cot[...].astype(F32)
        scaled = grad * gain[...].astype(F32).reshape(1, -1)
        mid = cot32 + row_normalize_back(scaled, norm, inverse[:, :1])
        grad_mid[...] = mid
        low = mid.astype(BF16)
        att_stage[1] = dot(wo_other[...], low, NT).astype(BF16)
        exchange = to_twin(att_stage.at[1], grad_att.at[:, own], 4)
        exchange.start()
        att_stage[0] = dot(wo_own[...], low, NT).astype(BF16)
        local = pltpu.make_async_copy(att_stage.at[0], grad_att.at[:, own], move_sems.at[0])
        local.start()
        out[...] = total[...].astype(BF16)
        small[0:1, :] = jnp.sum(grad * norm, axis=0, keepdims=True)
        small[1:2, :] = jnp.sum(grad, axis=0, keepdims=True)
        small[2:3, :] = jnp.sum(low.astype(F32), axis=0, keepdims=True)
        small[3:4, :] = jnp.sum(cot32, axis=0, keepdims=True)
        grad_wo[:heads] = dot(att_own[...], low).astype(BF16)
        grad_wo[heads:] = dot(att_other[...], low).astype(BF16)
        act(0, "fc")
        act(2, "fA")
        moves = [local]
        for i, depth in ((1, 2), (2, 1)):
            for j in range(2):
                span = part(i, j).span(depth)
                move = pltpu.make_async_copy(
                    held.at[i, j, span, :], state.at[i, j, span, :], move_sems.at[1 + 2 * i + j]
                )
                move.start()
                moves.append(move)
        exchange.wait()
        for move in moves:
            move.wait()


def feed(
    row_chips, x, cot, attended, wo_own, wo_other, bias_o, gain, bias,
    up_other, up_own, bu_other, bu_own, down_other, down_own, bias_d,
):
    rows, width = x.shape
    hidden = up_own.shape[1]
    heads = wo_own.shape[0]
    chunk = hidden // 3
    once = pl.Buffered(1)
    fixed = lambda s: pl.BlockSpec(s, lambda j, nd=len(s): (0,) * nd, pipeline_mode=once)
    anywhere = pl.BlockSpec(memory_space=pl.ANY)
    up_spec = pl.BlockSpec((width, chunk), lambda j: (0, j // 2))
    down_spec = pl.BlockSpec((chunk, width), lambda j: (j // 2, 0))
    operands = (
        x, cot, attended, wo_own, wo_other, bias_o, gain, bias,
        up_other, up_own, bu_other, bu_own, down_other, down_own, bias_d,
    )
    specs = [fixed(a.shape) for a in operands]
    specs[2] = anywhere
    specs[8] = specs[9] = up_spec
    specs[12] = specs[13] = down_spec
    results = [
        ((rows, width), BF16),
        ((rows, width), F32),
        ((heads, 2 * rows), BF16),
        ((3, 2, chunk, width), BF16),
        ((2 * heads, width), BF16),
        ((SUM_ROWS, width), F32),
    ]
    out_specs = [fixed(s) for s, _ in results]
    out_specs[2] = out_specs[3] = anywhere
    part = slot_shapes("xyz", chunk, width)
    return pl.pallas_call(
        functools.partial(feed_kernel, row_chips),
        grid=(6,),
        in_specs=specs,
        out_specs=out_specs,
        out_shape=[jax.ShapeDtypeStruct(s, t) for s, t in results],
        scratch_shapes=[
            pltpu.VMEM((heads, rows), BF16),
            pltpu.VMEM((heads, rows), BF16),
            pltpu.VMEM((rows, width), BF16),
            pltpu.VMEM((rows, width), F32),
            pltpu.VMEM((rows, 128), F32),
            pltpu.VMEM((rows, width), F32),
            pltpu.VMEM((rows, width), F32),
            pltpu.VMEM((2, heads, rows), BF16),
            pltpu.VMEM((3, 2, chunk, width), BF16),
            pltpu.VMEM((3, 2, chunk, width), BF16),
            pltpu.VMEM((3, 2) + part[0], BF16),
            pltpu.VMEM((2, 2) + part[1], BF16),
            pltpu.VMEM((2,) + part[2], BF16),
            pltpu.SemaphoreType.DMA((7,)),
            pltpu.SemaphoreType.DMA((2, 5)),
            pltpu.SemaphoreType.DMA((3, 2, 2, 11)),
        ],
        compiler_params=pltpu.CompilerParams(
            vmem_limit_bytes=VMEM_LIMIT, collective_id=2, has_side_effects=True,
            dimension_semantics=("arbitrary",),
        ),
        name="feed",
    )(*operands)


def extra_rows(row, fourth):
    high = row.astype(BF16).astype(F32)
    middle = (row - high).astype(BF16).astype(F32)
    low = row - high - middle
    index = lax.broadcasted_iota(jnp.int32, (HEAD_DIM, row.shape[1]), 0)
    rest = jnp.where(index == 2, low, jnp.where(index == 3, fourth, 0.0))
    return jnp.where(index == 0, high, jnp.where(index == 1, middle, rest)).astype(BF16)


BACK_PLAN = {
    "start": ((0, "sb"), (2, "sB"), (1, "sC")),
    (0, 2): ((0, "fb"), (0, "sa"), (2, "fB")),
    (0, 3): ((1, "fC"), (1, "sc"), (2, "sC")),
    (1, 1): ((0, "fa"), (3, "sA")),
    (1, 2): ((1, "fc"), (1, "sb")),
    (1, 3): ((3, "fA"), (3, "sB"), (1, "fb"), (1, "sa")),
    (2, 1): ((2, "fC"), (2, "sc"), (3, "fB"), (3, "sC")),
    (2, 2): ((1, "fa"), (4, "sA")),
    (2, 3): ((2, "fc"), (2, "sb"), (4, "fA"), (4, "sB")),
    "e0": ((5, "sA"),),
    "e1": ((3, "fC"), (3, "sc"), (2, "fb"), (2, "sa"), (4, "fB"), (4, "sC")),
    "e2": ((5, "fA"), (5, "sB"), (3, "fc"), (3, "sb")),
    "e3": ((4, "fC"), (4, "sc"), (5, "fB"), (5, "sC"), (3, "fb"), (3, "sa")),
    "e4": ((2, "fa"), (4, "fc"), (4, "sb")),
    "e5": ((5, "fC"), (5, "sc"), (4, "fb"), (4, "sa")),
    "e6": ((3, "fa"), (5, "fc"), (5, "sb")),
    "e7": ((5, "fb"), (5, "sa")),
    "e8": ((4, "fa"), (5, "fa")),
}


def attend_back_kernel(
    row_chips, block, split, qt, k, kt, v, do, attended, lse, ln, x, gain, wq, wk, wv_t, grad_wo,
    small, state,
    back, dv_first, sums, red_down, red_up, red_wo, red_low, red_v, red_last,
    stack, q_aug, d_aug, k_aug, v_aug, dk_sum, dv_sum, weights, terms_send, terms_got,
    wo_got, held, held_wo, held_low, held_v, held_last, sums_got,
    one_c, two_b, two_c, wo_a, wo_b, wo_c, low_a, low_b, low_c, v_a, v_b, v_c,
    last_a, last_b, last_c, move_sems, pair_sems, tiny_sems, sum_sems,
):
    width, tokens = qt.shape
    half = tokens // 2
    fresh = wv_t.shape[0]
    place = Place(row_chips)
    core = place.core
    pair_width = 2 * HEAD_DIM
    own = pl.ds(pl.multiple_of(core * half, half), half)
    theirs = pl.ds(pl.multiple_of((1 - core) * half, half), half)
    orders = ("xyz", "yxz")

    def to_twin(source, target, i):
        return pltpu.make_async_remote_copy(
            src_ref=source, dst_ref=target, send_sem=pair_sems.at[0, i],
            recv_sem=pair_sems.at[1, i], device_id=place.twin(), device_id_type=MESH,
        )

    def part(i, j):
        sems = sum_sems.at[i, j]
        if i < 3:
            result = (red_down, red_up)[j].at[i]
            slots = [
                None,
                two_b.at[j] if i == 2 else None,
                (None, one_c, two_c)[i].at[j] if i else None,
            ]
            return Sum(place, orders[j], held.at[i - 1, j] if i else None, slots, result, sems)
        if i == 4:
            given = (held_low, [low_a, low_b, low_c], red_low)
            if j:
                given = (held_v, [v_a, v_b, v_c], red_v)
            return Sum(place, orders[j], given[0], given[1], given[2], sems)
        holder, slots, result = {
            3: (held_wo, [wo_a, wo_b, wo_c], red_wo),
            5: (held_last, [last_a, last_b, last_c], red_last),
        }[i]
        return Sum(place, orders[j], holder.at[j], [s.at[j] for s in slots], result.at[j], sems)

    def act(point):
        for i, action in BACK_PLAN.get(point, ()):
            for j in range(2):
                one = part(i, j)
                source = None
                if i == 0 and action[1] == "b":
                    source = state.at[0, j]
                elif action[1] == "c":
                    source = one.held
                one.run(action, source)

    loads = [
        pltpu.make_async_copy(
            state.at[i, j, part(i, j).span(depth), :],
            held.at[i - 1, j, part(i, j).span(depth), :],
            move_sems.at[2 * (i - 1) + j],
        )
        for i, depth in ((1, 2), (2, 1))
        for j in range(2)
    ]
    ready = greet(place)
    for load in loads:
        load.start()
    weights[:width] = wq[...].T
    weights[width : 2 * width] = wk[...].T
    weights[2 * width :] = wv_t[...]
    ready()
    wo_exchange = to_twin(grad_wo.at[width:, :], wo_got, 0)
    wo_exchange.start()
    for load in loads:
        load.wait()
    act("start")
    far = jnp.where(split[0] < tokens, -1e9, 0.0)
    token = lax.broadcasted_iota(jnp.int32, (1, tokens), 1)
    far_row = jnp.where(token >= half, far, 0.0)

    def weight_rows(rows):
        return dot(stack[rows, :], ln[...]).astype(BF16)

    def by_columns(target, start, values):
        cols = target.shape[2]
        for j in range(2):
            target[j, start : start + values.shape[0], :] = values[:, j * cols : (j + 1) * cols]

    def pair_step(pair, _):
        col = pl.multiple_of(pair * pair_width, pair_width)
        lane = lax.broadcasted_iota(jnp.int32, (tokens, pair_width), 1)
        key = lax.broadcasted_iota(jnp.int32, (tokens, pair_width), 0)
        within = lax.rem(lane, HEAD_DIM)
        ones = jnp.where((within < 3) | ((within == 3) & (key < half)), 1.0, 0.0).astype(BF16)
        keys = k[:, pl.ds(col, pair_width)]
        values = v[:, pl.ds(col, pair_width)]
        dk_sum[...] = jnp.zeros_like(dk_sum)
        dv_sum[...] = jnp.zeros_like(dv_sum)
        head_rows = [pl.ds(pl.multiple_of(col + HEAD_DIM * j, HEAD_DIM), HEAD_DIM) for j in range(2)]
        for j in range(2):
            mine = lane // HEAD_DIM == j
            k_aug[j] = jnp.where(mine, keys, ones)
            v_aug[j] = jnp.where(mine, values, ones)
            grad = do[head_rows[j], :]
            inner = jnp.sum(
                grad.astype(F32) * attended[head_rows[j], :].astype(F32), axis=0, keepdims=True
            )
            base, extra = HEAD_DIM * j, HEAD_DIM * (1 - j)
            q_aug[j, base : base + HEAD_DIM, :] = qt[head_rows[j], :]
            q_aug[j, extra : extra + HEAD_DIM, :] = extra_rows(
                -lse[pl.ds(pair * 2 + j, 1)][0], far_row
            )
            d_aug[j, base : base + HEAD_DIM, :] = grad
            d_aug[j, extra : extra + HEAD_DIM, :] = extra_rows(-inner, 0.0)

        for number in range(tokens // block):
            start = number * block
            stop = start + block
            for j in range(2):
                scores = dot(k_aug[j, :stop, :], q_aug[j, :, start:stop])
                grad_probs = dot(v_aug[j, :stop, :], d_aug[j, :, start:stop])
                probs = jnp.where(causal(block), jnp.exp(scores[start:]), 0.0)
                if start:
                    probs = jnp.concatenate([jnp.exp(scores[:start]), probs], axis=0)
                grad_scores = (probs * grad_probs).astype(BF16)
                probs = probs.astype(BF16)
                rows = head_rows[j]
                stack[rows, start:stop] = (
                    dot(kt[rows, :stop], grad_scores) * HEAD_DIM ** (-0.5)
                ).astype(BF16)
                dv_sum[j, :, :stop] += dot(do[rows, start:stop], probs, NT)
                dk_sum[j, :, :stop] += dot(qt[rows, start:stop], grad_scores, NT)
            for p in range(width // pair_width):
                if number < tokens // block - 1 and (p, number) in BACK_PLAN:
                    pl.when(pair == p)(functools.partial(act, (p, number)))

        for j in range(2):
            stack[pl.ds(pl.multiple_of(width + col + HEAD_DIM * j, HEAD_DIM), HEAD_DIM), :] = dk_sum[
                j
            ].astype(BF16)

        @pl.when(pair == 0)
        def _():
            stack[2 * width : 2 * width + HEAD_DIM, :] = dv_sum[0].astype(BF16)
            stack[2 * width + HEAD_DIM : 2 * width + 2 * HEAD_DIM, :] = dv_sum[1].astype(BF16)
            wo_exchange.wait()
            summed = (grad_wo[:width].astype(F32) + wo_got[...].astype(F32)).astype(BF16)
            by_columns(held_wo, 0, summed)
            for i in range(3):
                by_columns(
                    held_wo,
                    width + i * pair_width,
                    weight_rows(slice(i * width, i * width + pair_width)),
                )
            act((0, 3))

        @pl.when(pair == 1)
        def _():
            stack[2 * width + 2 * HEAD_DIM :, :] = dv_sum[0].astype(BF16)
            dv_first[:HEAD_DIM, :] = dv_sum[1]
            for i in range(2):
                held_low[i * pair_width : (i + 1) * pair_width] = weight_rows(
                    slice(i * width + pair_width, i * width + 2 * pair_width)
                )
            rest = weight_rows(slice(2 * width + 2 * HEAD_DIM, 2 * width + 3 * HEAD_DIM))
            cols = held_v.shape[1]
            held_v[...] = jnp.zeros_like(held_v)
            for j in range(2):
                held_v[HEAD_DIM * j : HEAD_DIM * (j + 1), :] = rest[:, j * cols : (j + 1) * cols]
            act((1, 3))

        @pl.when(pair == 2)
        def _():
            dv_first[HEAD_DIM : 2 * HEAD_DIM, :] = dv_sum[0]
            dv_first[2 * HEAD_DIM :, :] = dv_sum[1]
            for i in range(2):
                by_columns(
                    held_last,
                    i * pair_width,
                    weight_rows(slice(i * width + 2 * pair_width, i * width + 3 * pair_width)),
                )
            act((2, 3))

        return 0

    lax.fori_loop(0, width // pair_width, pair_step, 0)

    act("e0")
    terms_send[...] = dot(stack[:, theirs], weights[...], TN).astype(BF16)
    terms_exchange = to_twin(terms_send, terms_got, 1)
    terms_exchange.start()
    back[...] = dot(stack[:, own], weights[...], TN)
    act("e1")
    normed, inverse = row_normalize(x[...].astype(F32))
    terms_exchange.wait()
    grad = back[...] + terms_got[...].astype(F32)
    sums[...] = small[...]
    sums[4:5, :] = jnp.sum(grad * normed, axis=0, keepdims=True)
    sums[5:6, :] = jnp.sum(grad, axis=0, keepdims=True)
    biases = dot(jnp.ones((8, tokens), BF16), stack[...], NT)
    sums[ROW_BQ : ROW_BQ + 1, :width] = biases[:1, :width]
    sums[ROW_BV : ROW_BV + 1, :fresh] = biases[:1, 2 * width :]
    tiny = to_twin(sums, sums_got.at[0], 2)
    tiny.start()
    back[...] = row_normalize_back(grad * gain[...].astype(F32).reshape(1, -1), normed, inverse)
    tiny.wait()
    sums[:ROW_BU, :] = sums[:ROW_BU, :] + sums_got[0, :ROW_BU, :]
    sums[ROW_BU:ROW_BU_OTHER, :] = (
        sums[ROW_BU:ROW_BU_OTHER, :] + sums_got[0, ROW_BU_OTHER:ROW_BQ, :]
    )
    slot = 1
    points = iter(("e2", "e3", "e4"))
    for axis in AXES:
        copies = []
        for step in range(1, SIZE[axis]):
            _, device = place.peer(axis, step)
            copies.append(
                pltpu.make_async_remote_copy(
                    src_ref=sums, dst_ref=sums_got.at[slot], send_sem=tiny_sems.at[0, slot],
                    recv_sem=tiny_sems.at[1, slot], device_id=device, device_id_type=MESH,
                )
            )
            copies[-1].start()
            slot += 1
        act(next(points))
        for copy in copies:
            copy.wait()
        total = sums[...]
        for i in range(slot - len(copies), slot):
            total = total + sums_got[i]
        sums[...] = total
    for point in ("e5", "e6", "e7", "e8"):
        act(point)


def attend_back(
    row_chips, split, qt, k, kt, v, do, attended, lse, ln, x, gain, wq, wk, wv_t, grad_wo, small,
    state, block=512,
):
    width, tokens = qt.shape
    rows, model = x.shape
    fresh = wv_t.shape[0]
    pair = 2 * HEAD_DIM
    chunk = state.shape[2]
    low_rows = 2 * pair
    cols = model // 2
    vmem = pl.BlockSpec(memory_space=pltpu.VMEM)
    anywhere = pl.BlockSpec(memory_space=pl.ANY)
    results = [
        ((rows, model), F32, vmem),
        ((width - fresh, tokens), F32, vmem),
        ((SUM_ROWS, model), F32, vmem),
        ((3, chunk, model), BF16, anywhere),
        ((3, chunk, model), BF16, anywhere),
        ((2, 2 * width, cols), BF16, anywhere),
        ((low_rows, model), BF16, anywhere),
        ((low_rows, cols), BF16, anywhere),
        ((2, low_rows, cols), BF16, anywhere),
    ]
    part = slot_shapes("xyz", chunk, model)
    wo = slot_shapes("xyz", 2 * width, cols)
    low = slot_shapes("xyz", low_rows, model)
    thin = slot_shapes("xyz", low_rows, cols)
    two = lambda s: (2,) + s
    scratch = [
        ((2 * width + fresh, tokens), BF16),
        ((2, pair, tokens), BF16),
        ((2, pair, tokens), BF16),
        ((2, tokens, pair), BF16),
        ((2, tokens, pair), BF16),
        ((2, HEAD_DIM, tokens), F32),
        ((2, HEAD_DIM, tokens), F32),
        ((2 * width + fresh, model), BF16),
        ((rows, model), BF16),
        ((rows, model), BF16),
        ((width, model), BF16),
        ((2, 2, chunk, model), BF16),
        ((2, 2 * width, cols), BF16),
        ((low_rows, model), BF16),
        ((low_rows, cols), BF16),
        ((2, low_rows, cols), BF16),
        ((6, SUM_ROWS, model), F32),
        (two(part[2]), BF16),
        (two(part[1]), BF16),
        (two(part[2]), BF16),
    ]
    scratch += [(two(s), BF16) for s in wo]
    scratch += [(s, BF16) for s in low]
    scratch += [(s, BF16) for s in thin]
    scratch += [(two(s), BF16) for s in thin]
    return pl.pallas_call(
        functools.partial(attend_back_kernel, row_chips, block),
        out_shape=[jax.ShapeDtypeStruct(s, t) for s, t, _ in results],
        in_specs=[pl.BlockSpec(memory_space=pltpu.SMEM)] + [vmem] * 15 + [anywhere],
        out_specs=[spec for _, _, spec in results],
        scratch_shapes=[pltpu.VMEM(s, t) for s, t in scratch]
        + [
            pltpu.SemaphoreType.DMA((4,)),
            pltpu.SemaphoreType.DMA((2, 3)),
            pltpu.SemaphoreType.DMA((2, 6)),
            pltpu.SemaphoreType.DMA((6, 2, 2, 11)),
        ],
        compiler_params=pltpu.CompilerParams(
            vmem_limit_bytes=VMEM_LIMIT, collective_id=3, has_side_effects=True
        ),
        name="attend_back",
    )(split, qt, k, kt, v, do, attended, lse, ln, x, gain, wq, wk, wv_t, grad_wo, small, state)


def swap(array):
    return lax.ppermute(array, "tensor", [(0, 1), (1, 0)])


def across_blocks(array, row_chips):
    chips = 4 * row_chips * row_chips
    shift = 2
    while shift < row_chips:
        for stride in (shift, shift * row_chips):
            pairs = [(i, i ^ stride) for i in range(chips)]
            array = array + lax.ppermute(array, "dp", pairs)
        shift *= 2
    return array


def on_device(
    row_chips,
    input_rows, first_values, doc_split, gain_norm1, bias_norm1, w_query, bias_query, w_key,
    w_value, bias_value, w_out, bias_attn_out, gain_norm2, bias_norm2, w_up, bias_up, w_down,
    bias_down, cotangent,
):
    heads = w_query.shape[1]
    fresh = w_value.shape[1]
    hidden = w_up.shape[1]
    pair = 2 * HEAD_DIM
    wv_t = w_value.T
    ln, qt, k, kt, v, vt = project(
        input_rows, first_values.T, gain_norm1, bias_norm1, w_query, bias_query, w_key, wv_t,
        bias_value,
    )
    up, down, wo, bu, vt = lax.optimization_barrier((w_up, w_down, w_out, bias_up, vt))
    up_other, down_other, wo_other, bu_other = swap(up), swap(down), swap(wo), swap(bu)
    attended, lse = attend(doc_split, qt, k, vt)
    output, grad_middle, grad_att, state, grad_wo, small = feed(
        row_chips, input_rows, cotangent, attended, w_out, wo_other, bias_attn_out, gain_norm2,
        bias_norm2, up_other, w_up, bu_other, bias_up, down_other, w_down, bias_down,
    )
    back, dv_first, sums, red_down, red_up, red_wo, red_low, red_v, red_last = attend_back(
        row_chips, doc_split, qt, k, kt, v, grad_att, attended, lse, ln, input_rows, gain_norm1,
        w_query, w_key, wv_t, grad_wo, small, state,
    )
    red_down, red_up, red_wo, red_low, red_v, red_last, sums = [
        across_blocks(a, row_chips)
        for a in (red_down, red_up, red_wo, red_low, red_v, red_last, sums)
    ]
    red_wo = jnp.concatenate([red_wo[0], red_wo[1]], axis=1)
    red_last = jnp.concatenate([red_last[0], red_last[1]], axis=1)
    rest = jnp.concatenate([red_v[:HEAD_DIM], red_v[HEAD_DIM:pair]], axis=1)
    first = heads
    grad_q = jnp.concatenate([red_wo[first : first + pair], red_low[:pair], red_last[:pair]])
    grad_k = jnp.concatenate(
        [red_wo[first + pair : first + 2 * pair], red_low[pair:], red_last[pair:]]
    )
    grad_v = jnp.concatenate([red_wo[first + 2 * pair :], rest])
    grad_bu = sums[ROW_BU:ROW_BU_OTHER, : hidden // 3].reshape(-1)
    return (
        output,
        grad_middle + back,
        dv_first.T,
        sums[4],
        sums[5],
        grad_q.astype(F32).T,
        sums[ROW_BQ, :heads],
        grad_k.astype(F32).T,
        grad_v.astype(F32).T,
        sums[ROW_BV, :fresh],
        red_wo[:heads].astype(F32),
        sums[2],
        sums[0],
        sums[1],
        red_up.reshape(hidden, -1).astype(F32).T,
        grad_bu,
        red_down.reshape(hidden, -1).astype(F32),
        sums[3],
    )


def solution(mesh):
    row_chips = 1
    while 4 * row_chips * row_chips < mesh.shape["dp"]:
        row_chips += 1
    rows = P(("dp", "tensor"), None)
    cols = P(None, "tensor")
    split = P("tensor")
    firsts = P("dp", "tensor")
    wide = P("tensor", None)
    return jax.shard_map(
        functools.partial(on_device, row_chips),
        mesh=mesh,
        in_specs=(
            rows, firsts, P("dp"), P(), P(), cols, split, cols, cols, split, wide, P(), P(), P(),
            cols, split, wide, P(), rows,
        ),
        out_specs=(
            rows, rows, firsts, P(), P(), cols, split, cols, cols, split, wide, P(), P(), P(),
            cols, split, wide, P(),
        ),
        check_vma=False,
    )
```

```python
import functools

import jax
import jax.numpy as jnp
from jax import lax
from jax.experimental import pallas as pl
from jax.experimental.pallas import tpu as pltpu
from jax.sharding import PartitionSpec as P

HEAD_DIM = 64
NORM_EPS = 1e-05
GELU_ROOT = 0.7978845608028654
GELU_CUBE = 0.044715
NN = (((1,), (0,)), ((), ()))
NT = (((1,), (1,)), ((), ()))
TN = (((0,), (0,)), ((), ()))
F32 = jnp.float32
BF16 = jnp.bfloat16
VMEM_LIMIT = 60 << 20
MESH = pl.DeviceIdType.MESH


def dot(left, right, dims=NN):
    return lax.dot_general(left, right, dims, preferred_element_type=F32)


def whole(array):
    return pl.BlockSpec(array.shape, lambda *_, nd=array.ndim: (0,) * nd)


def whole_shape(shape):
    return pl.BlockSpec(shape, lambda *_, nd=len(shape): (0,) * nd)


def row_normalize(rows):
    centered = rows - jnp.mean(rows, axis=1, keepdims=True)
    inverse = lax.rsqrt(jnp.mean(centered * centered, axis=1, keepdims=True) + NORM_EPS)
    return centered * inverse, inverse


def row_normalize_back(scaled, normed, inverse):
    return inverse * (
        scaled
        - jnp.mean(scaled, axis=1, keepdims=True)
        - normed * jnp.mean(scaled * normed, axis=1, keepdims=True)
    )


AXES = ("x", "y", "z")
SIZE = {"x": 2, "y": 2, "z": 4}


class Place:
    def __init__(self, row_chips):
        index = lax.axis_index("dp")
        self.core = lax.axis_index("tensor")
        self.wide = row_chips
        self.index = index
        self.x = lax.rem(index, row_chips)
        self.y = lax.rem(index // row_chips, row_chips)
        self.z = index // (row_chips * row_chips)
        self.at = {"x": lax.rem(self.x, 2), "y": lax.rem(self.y, 2), "z": self.z}

    def peer(self, axis, step):
        size = SIZE[axis]
        spot = lax.rem(self.at[axis] + step, size)
        stride = {"x": 1, "y": self.wide, "z": self.wide * self.wide}[axis]
        return spot, (self.index + (spot - self.at[axis]) * stride, self.core)

    def twin(self):
        return (self.index, 1 - self.core)

    def others(self):
        return [self.twin()] + [self.peer(a, k)[1] for a in AXES for k in range(1, SIZE[a])]


def greet(place):
    barrier = pltpu.get_barrier_semaphore()
    devices = place.others()
    for device in devices:
        pl.semaphore_signal(barrier, inc=1, device_id=device, device_id_type=MESH)
    return lambda: pl.semaphore_wait(barrier, len(devices))


class Sum:
    def __init__(self, place, order, held, slots, result, sems):
        self.place, self.order, self.held = place, order, held
        self.slots, self.result, self.sems = slots, result, sems
        self.rows = (held if held is not None else result).shape[0]

    def region(self, depth):
        start, size = 0, self.rows
        for axis in self.order[:depth]:
            size //= SIZE[axis]
            start = start + self.place.at[axis] * size
        return start, size

    def span(self, depth):
        start, size = self.region(depth)
        return pl.ds(pl.multiple_of(start, 16) if depth else start, size)

    def first_sem(self, gather, stage):
        count = 0
        for axis in self.order[:stage]:
            count += SIZE[axis] - 1
        return count + (5 if gather else 0)

    def scatter_copies(self, stage):
        axis = self.order[stage]
        start, size = self.region(stage)
        piece = size // SIZE[axis]
        base = self.first_sem(False, stage)
        copies = []
        for step in range(1, SIZE[axis]):
            spot, device = self.place.peer(axis, step)
            copies.append(
                pltpu.make_async_remote_copy(
                    src_ref=self.held.at[pl.ds(pl.multiple_of(start + spot * piece, 16), piece), :],
                    dst_ref=self.slots[stage].at[step - 1],
                    send_sem=self.sems.at[0, base + step - 1],
                    recv_sem=self.sems.at[1, base + step - 1],
                    device_id=device,
                    device_id_type=MESH,
                )
            )
        return copies

    def scatter_end(self, stage):
        for copy in self.scatter_copies(stage):
            copy.wait()
        span = self.span(stage + 1)
        total = self.held[span, :].astype(F32)
        for step in range(SIZE[self.order[stage]] - 1):
            total = total + self.slots[stage][step].astype(F32)
        self.held[span, :] = total.astype(BF16)

    def gather_copies(self, stage, source):
        axis = self.order[stage]
        span = self.span(stage + 1)
        base = self.first_sem(True, stage)
        copies = []
        origin = self.result if source is None else source
        for step in range(1, SIZE[axis]):
            _, device = self.place.peer(axis, step)
            copies.append(
                pltpu.make_async_remote_copy(
                    src_ref=origin.at[span, :],
                    dst_ref=self.result.at[span, :],
                    send_sem=self.sems.at[0, base + step - 1],
                    recv_sem=self.sems.at[1, base + step - 1],
                    device_id=device,
                    device_id_type=MESH,
                )
            )
        if source is not None:
            copies.append(
                pltpu.make_async_copy(
                    source.at[span, :], self.result.at[span, :], self.sems.at[0, 10]
                )
            )
        return copies

    def run(self, action, source=None):
        verb, letter = action
        gather = letter in "cba"
        stage = "abc".index(letter) if gather else "ABC".index(letter)
        if gather:
            for copy in self.gather_copies(stage, source):
                copy.start() if verb == "s" else copy.wait()
        elif verb == "s":
            for copy in self.scatter_copies(stage):
                copy.start()
        else:
            self.scatter_end(stage)


def slot_shapes(order, rows, cols):
    shapes = []
    for axis in order:
        rows //= SIZE[axis]
        shapes.append((SIZE[axis] - 1, rows, cols))
    return shapes


ORDERS = ("xyz", "yxz")
FEED_PLAN = {
    "s1m": ((0, "sA"),),
    "s3m": ((0, "fA"), (0, "sB"), (1, "sA"),),
    "s4m": ((0, "fB"), (0, "sC"),),
    "s5e": ((1, "fA"), (1, "sB"),),
    "f_end": ((0, "fC"), (1, "fB"),),
}
BACK_PLAN = {
    (0, 0): ((0, "sc"), (1, "sC"), (2, "sA"),),
    (0, 3): ((0, "fc"), (2, "fA"), (0, "sb"), (2, "sB"), (3, "sA"),),
    (1, 2): ((0, "fb"), (1, "fC"), (0, "sa"), (1, "sc"),),
    (1, 3): ((2, "fB"), (2, "sC"), (4, "sA"),),
    (2, 0): ((3, "fA"), (3, "sB"),),
    (2, 1): ((1, "fc"), (1, "sb"),),
    (2, 3): ((0, "fa"), (2, "fC"), (4, "fA"), (2, "sc"), (4, "sB"), (5, "sA"),),
    "e2": ((3, "fB"), (3, "sC"),),
    "e3": ((1, "fb"), (1, "sa"),),
    "e4": ((4, "fB"), (4, "sC"),),
    "e5": ((2, "fc"), (5, "fA"), (2, "sb"), (5, "sB"),),
    "e7": ((3, "fC"), (3, "sc"),),
    "w0": ((1, "fa"),),
    "w1": ((4, "fC"), (4, "sc"),),
    "w2": ((2, "fb"), (2, "sa"),),
    "w3": ((5, "fB"), (5, "sC"),),
    "w4": ((3, "fc"), (3, "sb"),),
    "w5": ((4, "fc"), (4, "sb"),),
    "w6": ((5, "fC"), (5, "sc"),),
    "w7": ((2, "fa"),),
    "w8": ((5, "fc"), (5, "sb"),),
    "w9": ((3, "fb"), (3, "sa"),),
    "w10": ((4, "fb"), (4, "sa"),),
    "w11": ((5, "fb"), (5, "sa"),),
    "w12": ((3, "fa"),),
    "w13": ((4, "fa"),),
    "w14": ((5, "fa"),),
}


def started(plan):
    return [(i, action[1]) for actions in plan.values() for i, action in actions if action[0] == "s"]


def progress(batch):
    return sum(1 for i, _ in started(FEED_PLAN) if i == batch)


def scatter_slots(plan, shapes):
    slots = {}
    for i, letter in started(plan):
        if letter in "ABC":
            for j, order in enumerate(ORDERS):
                shape = slot_shapes(order, *shapes[i][j])["ABC".index(letter)]
                slots[i, j, letter] = shape
    return slots


def project_kernel(
    x, first_t, gain, bias, wq, bq, wk, wv_t, bv, ln, qt, k, kt, v, vt,
    x_other, weights, s_ln, s_qt, s_k, s_kt, s_v, s_vt, pair_sems, out_sems,
):
    rows = x.shape[0]
    heads, fresh = wq.shape[1], wv_t.shape[0]
    core = lax.axis_index("tensor")
    twin = (lax.axis_index("dp"), 1 - core)
    barrier = pltpu.get_barrier_semaphore()
    pl.semaphore_signal(barrier, inc=1, device_id=twin, device_id_type=MESH)
    weights[:, :heads] = wq[...]
    weights[:, heads : 2 * heads] = wk[...]
    weights[:, 2 * heads :] = wv_t[...].T
    pl.semaphore_wait(barrier, 1)
    send = pltpu.make_async_remote_copy(
        src_ref=x, dst_ref=x_other, send_sem=pair_sems.at[0], recv_sem=pair_sems.at[1],
        device_id=twin, device_id_type=MESH,
    )
    send.start()
    gain_row = gain[...].astype(F32).reshape(1, -1)
    bias_row = bias[...].astype(F32).reshape(1, -1)
    bq_row = bq[...].astype(F32).reshape(1, -1)
    bv_row = bv[...].astype(F32).reshape(1, -1)
    copies = []
    for part, source in enumerate((x, x_other)):
        if part:
            send.wait_recv()
        spot = pl.multiple_of((core if part == 0 else 1 - core) * rows, rows)
        normed, _ = row_normalize(source[...].astype(F32))
        low = (normed * gain_row + bias_row).astype(BF16)
        s_ln[part] = low
        product = dot(low, weights[...])
        queries = (product[:, :heads] + bq_row).astype(BF16).astype(F32) * HEAD_DIM ** (-0.5)
        s_qt[part] = queries.astype(BF16).T
        keys = product[:, heads : 2 * heads].astype(BF16)
        s_k[part] = keys
        s_kt[part] = keys.T
        values = (product[:, 2 * heads :] + bv_row).astype(BF16)
        reused = first_t[:, pl.ds(spot, rows)]
        s_vt[part, :fresh] = values.T
        s_vt[part, fresh:] = reused
        s_v[part] = jnp.concatenate([values, reused.T], axis=1)
        targets = (
            (s_ln, ln.at[pl.ds(spot, rows), :]),
            (s_qt, qt.at[:, pl.ds(spot, rows)]),
            (s_k, k.at[pl.ds(spot, rows), :]),
            (s_kt, kt.at[:, pl.ds(spot, rows)]),
            (s_v, v.at[pl.ds(spot, rows), :]),
            (s_vt, vt.at[:, pl.ds(spot, rows)]),
        )
        for i, (held, target) in enumerate(targets):
            copy = pltpu.make_async_copy(held.at[part], target, out_sems.at[part, i])
            copy.start()
            copies.append(copy)
    send.wait_send()
    for copy in copies:
        copy.wait()


def project(x, first_t, gain, bias, wq, bq, wk, wv_t, bv):
    rows, width = x.shape
    heads = wq.shape[1]
    tall, flat = (rows, heads), (heads, rows)
    vmem = pl.BlockSpec(memory_space=pltpu.VMEM)
    shapes = ((2 * rows, width), (heads, 2 * rows), (2 * rows, heads)) + (
        (heads, 2 * rows), (2 * rows, heads), (heads, 2 * rows),
    )
    scratch = [(rows, width), (width, 2 * heads + wv_t.shape[0])]
    scratch += [(2,) + s for s in ((rows, width), flat, tall, flat, tall, flat)]
    return pl.pallas_call(
        project_kernel,
        out_shape=[jax.ShapeDtypeStruct(s, BF16) for s in shapes],
        in_specs=[vmem] * 9,
        out_specs=[pl.BlockSpec(memory_space=pl.ANY)] * 6,
        scratch_shapes=[pltpu.VMEM(s, BF16) for s in scratch]
        + [pltpu.SemaphoreType.DMA((2,)), pltpu.SemaphoreType.DMA((2, 6))],
        compiler_params=pltpu.CompilerParams(
            vmem_limit_bytes=VMEM_LIMIT, collective_id=1, has_side_effects=True
        ),
        name="project",
    )(x, first_t, gain, bias, wq, bq, wk, wv_t, bv)


def causal(size):
    keys = lax.broadcasted_iota(jnp.int32, (size, size), 0)
    return keys <= lax.broadcasted_iota(jnp.int32, (size, size), 1)


def query_blocks(tokens, block, two_docs, body):
    half = tokens // 2
    for start in range(0, tokens, block):
        if start < half:
            body(start, 0)
        else:

            @pl.when(two_docs)
            def _():
                body(start, half)

            @pl.when(jnp.logical_not(two_docs))
            def _():
                body(start, 0)


def attend_kernel(block, split, qt, k, vt, attended, lse, sums):
    width, tokens = qt.shape
    two_docs = split[0] < tokens
    ones = (lax.broadcasted_iota(jnp.int32, (16, tokens), 0) == 0).astype(BF16)
    sums[0, HEAD_DIM:, :] = ones
    sums[1, HEAD_DIM:, :] = ones

    def pair_step(pair, _):
        col = pl.multiple_of(pair * 2 * HEAD_DIM, 2 * HEAD_DIM)
        sums[0, :HEAD_DIM, :] = vt[pl.ds(col, HEAD_DIM), :]
        sums[1, :HEAD_DIM, :] = vt[pl.ds(col + HEAD_DIM, HEAD_DIM), :]
        owner = lax.broadcasted_iota(jnp.int32, (2 * HEAD_DIM, block), 0) // HEAD_DIM

        def body(start, low):
            stop = start + block
            inner = start - low
            queries = qt[pl.ds(col, 2 * HEAD_DIM), start:stop]
            keys = k[low:stop, pl.ds(col, 2 * HEAD_DIM)]
            scores = [
                dot(keys, jnp.where(owner == j, queries, jnp.zeros_like(queries))) for j in range(2)
            ]
            for j in range(2):
                edge = jnp.where(causal(block), scores[j][inner:], -1e30)
                top = jnp.max(edge, axis=0, keepdims=True)
                if inner:
                    near = scores[j][:inner]
                    top = jnp.maximum(top, jnp.max(near, axis=0, keepdims=True))
                    weights = jnp.concatenate(
                        [jnp.exp(near - top).astype(BF16), jnp.exp(edge - top).astype(BF16)], axis=0
                    )
                else:
                    weights = jnp.exp(edge - top).astype(BF16)
                total = dot(sums[j, :, low:stop], weights)
                denominator = total[HEAD_DIM : HEAD_DIM + 1]
                attended[pl.ds(col + HEAD_DIM * j, HEAD_DIM), start:stop] = (
                    total[:HEAD_DIM] * (1.0 / denominator)
                ).astype(BF16)
                lse[pl.ds(pair * 2 + j, 1), :, start:stop] = (top + jnp.log(denominator))[None]

        query_blocks(tokens, block, two_docs, body)
        return 0

    lax.fori_loop(0, width // (2 * HEAD_DIM), pair_step, 0)


def attend(split, qt, k, vt, block=512):
    width, tokens = qt.shape
    vmem = pl.BlockSpec(memory_space=pltpu.VMEM)
    return pl.pallas_call(
        functools.partial(attend_kernel, block),
        out_shape=(
            jax.ShapeDtypeStruct((width, tokens), BF16),
            jax.ShapeDtypeStruct((width // HEAD_DIM, 1, tokens), F32),
        ),
        in_specs=[pl.BlockSpec(memory_space=pltpu.SMEM), vmem, vmem, vmem],
        out_specs=(vmem, vmem),
        scratch_shapes=[pltpu.VMEM((2, HEAD_DIM + 16, tokens), BF16)],
        compiler_params=pltpu.CompilerParams(vmem_limit_bytes=VMEM_LIMIT),
        name="attend",
    )(split, qt, k, vt)


def gelu_both(v):
    square = v * v
    tanh = jnp.tanh(v * (GELU_ROOT + (GELU_ROOT * GELU_CUBE) * square))
    half = 0.5 * v
    slope = 0.5 + 0.5 * tanh + half * (1.0 - tanh * tanh) * (
        GELU_ROOT + (3.0 * GELU_ROOT * GELU_CUBE) * square
    )
    return half + half * tanh, slope


SUM_ROWS = 16
ROW_BU, ROW_BU_OTHER, ROW_BQ, ROW_BV = 6, 9, 12, 13


def feed_kernel(
    row_chips, slot_keys, x, cot, attended, wo_own, wo_other, bias_o, gain, bias,
    up_other, up_own, bu_other, bu_own, down_other, down_own, bias_d,
    out, grad_mid, grad_att, state_down, state_up, grad_wo, small,
    att_own, att_other, ln, ln_t, normed, inverse, total, grad_ln, att_stage, stage_down, stage_up,
    held_down, held_up, move_sems, pair_sems, sum_sems, *slot_refs,
):
    state, stage, held = (state_down, state_up), (stage_down, stage_up), (held_down, held_up)
    slots = dict(zip(slot_keys, slot_refs))
    step = pl.program_id(0)
    place = Place(row_chips)
    core = place.core
    rows = x.shape[0]
    heads = att_own.shape[0]
    chunk = up_own.shape[1]
    index = step // 2
    own = pl.ds(pl.multiple_of(core * rows, rows), rows)
    theirs = pl.ds(pl.multiple_of((1 - core) * rows, rows), rows)

    def to_twin(source, target, i):
        return pltpu.make_async_remote_copy(
            src_ref=source, dst_ref=target, send_sem=pair_sems.at[0, i],
            recv_sem=pair_sems.at[1, i], device_id=place.twin(), device_id_type=MESH,
        )

    def stage_copies(i):
        return [to_twin(stage[j].at[i], held[j].at[i], 2 + 2 * i + j) for j in range(2)]

    def part(i, j):
        return Sum(
            place, ORDERS[j], held[j].at[i], [slots.get((i, j, letter)) for letter in "ABC"],
            state[j].at[i], sum_sems.at[i, j],
        )

    def act(point):
        for i, action in FEED_PLAN.get(point, ()):
            for j in range(2):
                part(i, j).run(action, held[j].at[i] if action[1] == "c" else None)

    def act_at(name, odd):
        for k in range(odd, 6, 2):
            point = "s%d%s" % (k, name)
            if point in FEED_PLAN:
                pl.when(step == k)(functools.partial(act, point))

    @pl.when(step == 0)
    def _():
        ready = greet(place)
        local = pltpu.make_async_copy(attended.at[:, own], att_own, move_sems.at[0])
        local.start()
        ready()
        exchange = to_twin(attended.at[:, theirs], att_other, 0)
        exchange.start()
        total[...] = x[...].astype(F32) + bias_o[...].astype(F32).reshape(1, -1)
        grad_ln[...] = jnp.zeros_like(grad_ln)
        small[...] = jnp.zeros_like(small)
        local.wait()
        total[...] += dot(att_own[...], wo_own[...], TN)
        exchange.wait()
        mid = total[...] + dot(att_other[...], wo_other[...], TN)
        total[...] = mid + bias_d[...].astype(F32).reshape(1, -1)
        norm, inv = row_normalize(mid)
        normed[...] = norm
        inverse[...] = jnp.broadcast_to(inv, inverse.shape)
        low = (
            norm * gain[...].astype(F32).reshape(1, -1) + bias[...].astype(F32).reshape(1, -1)
        ).astype(BF16)
        ln[...] = low
        ln_t[...] = low.T

    def weight_grads(up, bias_up, down):
        hidden = dot(ln[...], up[...]) + bias_up[
            pl.ds(pl.multiple_of(index * chunk, chunk), chunk)
        ].astype(F32).reshape(1, -1)
        activated, slope = gelu_both(hidden)
        activated = activated.astype(BF16)
        grad_hidden = (dot(cot[...], down[...], NT) * slope).astype(BF16)
        grad_down = dot(activated, cot[...], TN)
        grad_up = dot(ln_t[...], grad_hidden)
        sums = jnp.sum(grad_hidden.astype(F32), axis=0, keepdims=True)
        return activated, grad_hidden, grad_down, grad_up, sums

    def row_terms(activated, grad_hidden, up, down):
        total[...] += dot(activated, down[...])
        grad_ln[...] += dot(grad_hidden, up[...], NT)

    @pl.when(lax.rem(step, 2) == 0)
    def _():
        activated, grad_hidden, grad_down, grad_up, sums = weight_grads(
            up_other, bu_other, down_other
        )
        stage_down[index] = grad_down.astype(BF16)
        stage_up[index] = grad_up.astype(BF16)
        for copy in stage_copies(index):
            copy.start()
        small[pl.ds(ROW_BU_OTHER + index, 1), :chunk] = sums
        act_at("m", 0)
        row_terms(activated, grad_hidden, up_other, down_other)
        act_at("e", 0)

    @pl.when(lax.rem(step, 2) == 1)
    def _():
        activated, grad_hidden, grad_down, grad_up, sums = weight_grads(up_own, bu_own, down_own)
        for copy in stage_copies(index):
            copy.wait()
        held_down[index] = (grad_down + held_down[index].astype(F32)).astype(BF16)
        held_up[index] = (grad_up + held_up[index].astype(F32)).astype(BF16)
        small[pl.ds(ROW_BU + index, 1), :chunk] = sums

        act_at("m", 1)
        row_terms(activated, grad_hidden, up_own, down_own)
        act_at("e", 1)

    @pl.when(step == 5)
    def _():
        grad = grad_ln[...]
        norm = normed[...]
        cot32 = cot[...].astype(F32)
        scaled = grad * gain[...].astype(F32).reshape(1, -1)
        mid = cot32 + row_normalize_back(scaled, norm, inverse[:, :1])
        grad_mid[...] = mid
        low = mid.astype(BF16)
        att_stage[1] = dot(wo_other[...], low, NT).astype(BF16)
        exchange = to_twin(att_stage.at[1], grad_att.at[:, own], 1)
        exchange.start()
        att_stage[0] = dot(wo_own[...], low, NT).astype(BF16)
        local = pltpu.make_async_copy(att_stage.at[0], grad_att.at[:, own], move_sems.at[0])
        local.start()
        out[...] = total[...].astype(BF16)
        small[0:1, :] = jnp.sum(grad * norm, axis=0, keepdims=True)
        small[1:2, :] = jnp.sum(grad, axis=0, keepdims=True)
        small[2:3, :] = jnp.sum(low.astype(F32), axis=0, keepdims=True)
        small[3:4, :] = jnp.sum(cot32, axis=0, keepdims=True)
        grad_wo[:heads] = dot(att_own[...], low).astype(BF16)
        grad_wo[heads:] = dot(att_other[...], low).astype(BF16)
        act("f_end")
        moves = [local]
        for i in range(3):
            if progress(i) > 3:
                continue
            for j in range(2):
                span = part(i, j).span(progress(i))
                move = pltpu.make_async_copy(
                    held[j].at[i, span, :], state[j].at[i, span, :], move_sems.at[1 + 2 * i + j]
                )
                move.start()
                moves.append(move)
        exchange.wait()
        for move in moves:
            move.wait()


def feed(
    row_chips, x, cot, attended, wo_own, wo_other, bias_o, gain, bias,
    up_other, up_own, bu_other, bu_own, down_other, down_own, bias_d,
):
    rows, width = x.shape
    hidden = up_own.shape[1]
    heads = wo_own.shape[0]
    chunk = hidden // 3
    once = pl.Buffered(1)
    fixed = lambda s: pl.BlockSpec(s, lambda j, nd=len(s): (0,) * nd, pipeline_mode=once)
    anywhere = pl.BlockSpec(memory_space=pl.ANY)
    up_spec = pl.BlockSpec((width, chunk), lambda j: (0, j // 2))
    down_spec = pl.BlockSpec((chunk, width), lambda j: (j // 2, 0))
    operands = (
        x, cot, attended, wo_own, wo_other, bias_o, gain, bias,
        up_other, up_own, bu_other, bu_own, down_other, down_own, bias_d,
    )
    specs = [fixed(a.shape) for a in operands]
    specs[2] = anywhere
    specs[8] = specs[9] = up_spec
    specs[12] = specs[13] = down_spec
    results = [
        ((rows, width), BF16),
        ((rows, width), F32),
        ((heads, 2 * rows), BF16),
        ((3, chunk, width), BF16),
        ((3, width, chunk), BF16),
        ((2 * heads, width), BF16),
        ((SUM_ROWS, width), F32),
    ]
    out_specs = [fixed(s) for s, _ in results]
    out_specs[2] = out_specs[3] = out_specs[4] = anywhere
    slots = scatter_slots(FEED_PLAN, {i: ((chunk, width), (width, chunk)) for i in range(3)})
    return pl.pallas_call(
        functools.partial(feed_kernel, row_chips, list(slots)),
        grid=(6,),
        in_specs=specs,
        out_specs=out_specs,
        out_shape=[jax.ShapeDtypeStruct(s, t) for s, t in results],
        scratch_shapes=[
            pltpu.VMEM((heads, rows), BF16),
            pltpu.VMEM((heads, rows), BF16),
            pltpu.VMEM((rows, width), BF16),
            pltpu.VMEM((width, rows), BF16),
            pltpu.VMEM((rows, width), F32),
            pltpu.VMEM((rows, 128), F32),
            pltpu.VMEM((rows, width), F32),
            pltpu.VMEM((rows, width), F32),
            pltpu.VMEM((2, heads, rows), BF16),
            pltpu.VMEM((3, chunk, width), BF16),
            pltpu.VMEM((3, width, chunk), BF16),
            pltpu.VMEM((3, chunk, width), BF16),
            pltpu.VMEM((3, width, chunk), BF16),
            pltpu.SemaphoreType.DMA((7,)),
            pltpu.SemaphoreType.DMA((2, 8)),
            pltpu.SemaphoreType.DMA((3, 2, 2, 11)),
        ]
        + [pltpu.VMEM(shape, BF16) for shape in slots.values()],
        compiler_params=pltpu.CompilerParams(
            vmem_limit_bytes=VMEM_LIMIT, collective_id=2, has_side_effects=True,
            dimension_semantics=("arbitrary",),
        ),
        name="feed",
    )(*operands)


def extra_rows(row, fourth):
    high = row.astype(BF16).astype(F32)
    middle = (row - high).astype(BF16).astype(F32)
    low = row - high - middle
    index = lax.broadcasted_iota(jnp.int32, (HEAD_DIM, row.shape[1]), 0)
    rest = jnp.where(index == 2, low, jnp.where(index == 3, fourth, 0.0))
    return jnp.where(index == 0, high, jnp.where(index == 1, middle, rest)).astype(BF16)


def attend_back_kernel(
    row_chips, block, slot_keys, split, gain, small, qt_far, k_far, kt_far, v_far, do_far, attended_far, lse_far,
    ln_far, x_far, wq_far, wk_far, wv_far, grad_wo_far, state_down, state_up,
    back, dv_first, sums, red_down, red_up, red_wo, red_low, red_v, red_last,
    stack, q_aug, d_aug, k_aug, v_aug, dk_sum, dv_sum, weights, terms_send, terms_got,
    wo_got, held_down, held_up, held_wo, held_low, held_v, held_last, sums_got,
    qt, k, kt, v, do, attended, lse, ln, x, grad_wo,
    move_sems, load_sems, pair_sems, tiny_sems, sum_sems, *slot_refs,
):
    state, held = (state_down, state_up), (held_down, held_up)
    slots = dict(zip(slot_keys, slot_refs))
    width, tokens = qt.shape
    half = tokens // 2
    fresh, model = wv_far.shape
    place = Place(row_chips)
    core = place.core
    pair_width = 2 * HEAD_DIM
    own = pl.ds(pl.multiple_of(core * half, half), half)
    theirs = pl.ds(pl.multiple_of((1 - core) * half, half), half)

    def to_twin(source, target, i):
        return pltpu.make_async_remote_copy(
            src_ref=source, dst_ref=target, send_sem=pair_sems.at[0, i],
            recv_sem=pair_sems.at[1, i], device_id=place.twin(), device_id_type=MESH,
        )

    def part(i, j):
        chunk = state_down.shape[1]
        if i < 3:
            holder = held[j].at[i]
            result = red_up.at[:, i * chunk : (i + 1) * chunk] if j else red_down.at[i]
        else:
            holder, result = {
                3: (held_wo.at[j], red_wo.at[j]),
                4: ((held_low, red_low), (held_v, red_v))[j],
                5: (held_last.at[j], red_last.at[j]),
            }[i]
        return Sum(
            place, ORDERS[j], holder, [slots.get((i, j, letter)) for letter in "ABC"], result,
            sum_sems.at[i, j],
        )

    def act(point):
        for i, action in BACK_PLAN.get(point, ()):
            for j in range(2):
                one = part(i, j)
                source = None
                if action[1] == "c":
                    source = one.held
                elif action[1] == "b" and i < 3 and progress(i) == 4:
                    source = state[j].at[i]
                one.run(action, source)

    loads = []
    for i in range(3):
        if progress(i) < 4:
            for j in range(2):
                span = part(i, j).span(progress(i))
                loads.append(
                    pltpu.make_async_copy(
                        state[j].at[i, span, :], held[j].at[i, span, :], move_sems.at[2 * i + j]
                    )
                )
    ready = greet(place)
    for load in loads:
        load.start()
    arriving = [
        pltpu.make_async_copy(far, near, load_sems.at[i])
        for i, (far, near) in enumerate(
            (
                (k_far, k), (qt_far, qt), (v_far, v), (do_far, do), (attended_far, attended),
                (lse_far, lse), (kt_far, kt), (wq_far, terms_send.at[:model, :width]),
                (wk_far, terms_send.at[:model, width:]), (wv_far, weights.at[2 * width :, :]), (ln_far, ln),
                (grad_wo_far.at[:width, :], grad_wo), (x_far, x),
            )
        )
    ]
    for copy in arriving:
        copy.start()
    ready()
    wo_exchange = to_twin(grad_wo_far.at[width:, :], wo_got, 0)
    wo_exchange.start()
    for load in loads:
        load.wait()
    act("start")
    for copy in arriving:
        copy.wait()
    weights[:width] = terms_send[:model, :width].T
    weights[width : 2 * width] = terms_send[:model, width:].T
    far = jnp.where(split[0] < tokens, -1e9, 0.0)
    token = lax.broadcasted_iota(jnp.int32, (1, tokens), 1)
    far_row = jnp.where(token >= half, far, 0.0)

    def weight_rows(rows):
        return dot(stack[rows, :], ln[...]).astype(BF16)

    def by_columns(target, start, values):
        cols = target.shape[2]
        for j in range(2):
            target[j, start : start + values.shape[0], :] = values[:, j * cols : (j + 1) * cols]

    def pair_step(pair, _):
        col = pl.multiple_of(pair * pair_width, pair_width)
        lane = lax.broadcasted_iota(jnp.int32, (tokens, pair_width), 1)
        key = lax.broadcasted_iota(jnp.int32, (tokens, pair_width), 0)
        within = lax.rem(lane, HEAD_DIM)
        ones = jnp.where((within < 3) | ((within == 3) & (key < half)), 1.0, 0.0).astype(BF16)
        keys = k[:, pl.ds(col, pair_width)]
        values = v[:, pl.ds(col, pair_width)]
        dk_sum[...] = jnp.zeros_like(dk_sum)
        dv_sum[...] = jnp.zeros_like(dv_sum)
        head_rows = [pl.ds(pl.multiple_of(col + HEAD_DIM * j, HEAD_DIM), HEAD_DIM) for j in range(2)]
        for j in range(2):
            mine = lane // HEAD_DIM == j
            k_aug[j] = jnp.where(mine, keys, ones)
            v_aug[j] = jnp.where(mine, values, ones)
            grad = do[head_rows[j], :]
            inner = jnp.sum(
                grad.astype(F32) * attended[head_rows[j], :].astype(F32), axis=0, keepdims=True
            )
            base, extra = HEAD_DIM * j, HEAD_DIM * (1 - j)
            q_aug[j, base : base + HEAD_DIM, :] = qt[head_rows[j], :]
            q_aug[j, extra : extra + HEAD_DIM, :] = extra_rows(
                -lse[pl.ds(pair * 2 + j, 1)][0], far_row
            )
            d_aug[j, base : base + HEAD_DIM, :] = grad
            d_aug[j, extra : extra + HEAD_DIM, :] = extra_rows(-inner, 0.0)

        for number in range(tokens // block):
            start = number * block
            stop = start + block
            for j in range(2):
                scores = dot(k_aug[j, :stop, :], q_aug[j, :, start:stop])
                grad_probs = dot(v_aug[j, :stop, :], d_aug[j, :, start:stop])
                probs = jnp.where(causal(block), jnp.exp(scores[start:]), 0.0)
                if start:
                    probs = jnp.concatenate([jnp.exp(scores[:start]), probs], axis=0)
                grad_scores = (probs * grad_probs).astype(BF16)
                probs = probs.astype(BF16)
                rows = head_rows[j]
                stack[rows, start:stop] = (
                    dot(kt[rows, :stop], grad_scores) * HEAD_DIM ** (-0.5)
                ).astype(BF16)
                dv_sum[j, :, :stop] += dot(do[rows, start:stop], probs, NT)
                dk_sum[j, :, :stop] += dot(qt[rows, start:stop], grad_scores, NT)
            for p in range(width // pair_width):
                if number < tokens // block - 1 and (p, number) in BACK_PLAN:
                    pl.when(pair == p)(functools.partial(act, (p, number)))

        for j in range(2):
            stack[pl.ds(pl.multiple_of(width + col + HEAD_DIM * j, HEAD_DIM), HEAD_DIM), :] = dk_sum[
                j
            ].astype(BF16)

        @pl.when(pair == 0)
        def _():
            stack[2 * width : 2 * width + HEAD_DIM, :] = dv_sum[0].astype(BF16)
            stack[2 * width + HEAD_DIM : 2 * width + 2 * HEAD_DIM, :] = dv_sum[1].astype(BF16)
            wo_exchange.wait()
            summed = (grad_wo[...].astype(F32) + wo_got[...].astype(F32)).astype(BF16)
            by_columns(held_wo, 0, summed)
            for i in range(3):
                by_columns(
                    held_wo,
                    width + i * pair_width,
                    weight_rows(slice(i * width, i * width + pair_width)),
                )
            act((0, 3))

        @pl.when(pair == 1)
        def _():
            stack[2 * width + 2 * HEAD_DIM :, :] = dv_sum[0].astype(BF16)
            dv_first[:HEAD_DIM, :] = dv_sum[1]
            for i in range(2):
                held_low[i * pair_width : (i + 1) * pair_width] = weight_rows(
                    slice(i * width + pair_width, i * width + 2 * pair_width)
                )
            rest = weight_rows(slice(2 * width + 2 * HEAD_DIM, 2 * width + 3 * HEAD_DIM))
            cols = held_v.shape[1]
            held_v[...] = jnp.zeros_like(held_v)
            for j in range(2):
                held_v[HEAD_DIM * j : HEAD_DIM * (j + 1), :] = rest[:, j * cols : (j + 1) * cols]
            act((1, 3))

        @pl.when(pair == 2)
        def _():
            dv_first[HEAD_DIM : 2 * HEAD_DIM, :] = dv_sum[0]
            dv_first[2 * HEAD_DIM :, :] = dv_sum[1]
            for i in range(2):
                by_columns(
                    held_last,
                    i * pair_width,
                    weight_rows(slice(i * width + 2 * pair_width, i * width + 3 * pair_width)),
                )
            act((2, 3))

        return 0

    lax.fori_loop(0, width // pair_width, pair_step, 0)

    act("e0")
    terms_send[...] = dot(stack[:, theirs], weights[...], TN).astype(BF16)
    terms_exchange = to_twin(terms_send, terms_got, 1)
    terms_exchange.start()
    act("e1")
    back[...] = dot(stack[:, own], weights[...], TN)
    act("e2")
    normed, inverse = row_normalize(x[...].astype(F32))
    terms_exchange.wait()
    grad = back[...] + terms_got[...].astype(F32)
    sums[...] = small[...]
    sums[4:5, :] = jnp.sum(grad * normed, axis=0, keepdims=True)
    sums[5:6, :] = jnp.sum(grad, axis=0, keepdims=True)
    biases = dot(jnp.ones((8, tokens), BF16), stack[...], NT)
    sums[ROW_BQ : ROW_BQ + 1, :width] = biases[:1, :width]
    sums[ROW_BV : ROW_BV + 1, :fresh] = biases[:1, 2 * width :]
    tiny = to_twin(sums, sums_got.at[0], 2)
    tiny.start()
    act("e3")
    back[...] = row_normalize_back(grad * gain[...].astype(F32).reshape(1, -1), normed, inverse)
    tiny.wait()
    sums[:ROW_BU, :] = sums[:ROW_BU, :] + sums_got[0, :ROW_BU, :]
    sums[ROW_BU:ROW_BU_OTHER, :] = (
        sums[ROW_BU:ROW_BU_OTHER, :] + sums_got[0, ROW_BU_OTHER:ROW_BQ, :]
    )
    slot = 1
    points = iter(("e4", "e5", "e6"))
    for axis in AXES:
        copies = []
        for step in range(1, SIZE[axis]):
            _, device = place.peer(axis, step)
            copies.append(
                pltpu.make_async_remote_copy(
                    src_ref=sums, dst_ref=sums_got.at[slot], send_sem=tiny_sems.at[0, slot],
                    recv_sem=tiny_sems.at[1, slot], device_id=device, device_id_type=MESH,
                )
            )
            copies[-1].start()
            slot += 1
        act(next(points))
        for copy in copies:
            copy.wait()
        total = sums[...]
        for i in range(slot - len(copies), slot):
            total = total + sums_got[i]
        sums[...] = total
    for point in BACK_PLAN:
        if point == "e7" or point[0] == "w":
            act(point)


def attend_back(
    row_chips, split, gain, small, qt, k, kt, v, do, attended, lse, ln, x, wq, wk, wv_t, grad_wo,
    state_down, state_up, block=512,
):
    width, tokens = qt.shape
    rows, model = x.shape
    fresh = wv_t.shape[0]
    pair = 2 * HEAD_DIM
    chunk = state_down.shape[1]
    low_rows = 2 * pair
    cols = model // 2
    vmem = pl.BlockSpec(memory_space=pltpu.VMEM)
    anywhere = pl.BlockSpec(memory_space=pl.ANY)
    results = [
        ((rows, model), F32, vmem),
        ((width - fresh, tokens), F32, vmem),
        ((SUM_ROWS, model), F32, vmem),
        ((3, chunk, model), BF16, anywhere),
        ((model, 3 * chunk), BF16, anywhere),
        ((2, 2 * width, cols), BF16, anywhere),
        ((low_rows, model), BF16, anywhere),
        ((low_rows, cols), BF16, anywhere),
        ((2, low_rows, cols), BF16, anywhere),
    ]
    shapes = {i: ((chunk, model), (model, chunk)) for i in range(3)}
    shapes[3] = ((2 * width, cols),) * 2
    shapes[4] = ((low_rows, model), (low_rows, cols))
    shapes[5] = ((low_rows, cols),) * 2
    slots = scatter_slots(BACK_PLAN, shapes)
    scratch = [
        ((2 * width + fresh, tokens), BF16),
        ((2, pair, tokens), BF16),
        ((2, pair, tokens), BF16),
        ((2, tokens, pair), BF16),
        ((2, tokens, pair), BF16),
        ((2, HEAD_DIM, tokens), F32),
        ((2, HEAD_DIM, tokens), F32),
        ((2 * width + fresh, model), BF16),
        ((rows, model), BF16),
        ((rows, model), BF16),
        ((width, model), BF16),
        ((3, chunk, model), BF16),
        ((3, model, chunk), BF16),
        ((2, 2 * width, cols), BF16),
        ((low_rows, model), BF16),
        ((low_rows, cols), BF16),
        ((2, low_rows, cols), BF16),
        ((6, SUM_ROWS, model), F32),
    ]
    near = (qt, k, kt, v, do, attended, lse, ln, x)
    scratch += [(a.shape, a.dtype) for a in near] + [((width, model), BF16)]
    return pl.pallas_call(
        functools.partial(attend_back_kernel, row_chips, block, list(slots)),
        out_shape=[jax.ShapeDtypeStruct(s, t) for s, t, _ in results],
        in_specs=[pl.BlockSpec(memory_space=pltpu.SMEM), vmem, vmem] + [anywhere] * 15,
        out_specs=[spec for _, _, spec in results],
        scratch_shapes=[pltpu.VMEM(s, t) for s, t in scratch]
        + [
            pltpu.SemaphoreType.DMA((6,)),
            pltpu.SemaphoreType.DMA((13,)),
            pltpu.SemaphoreType.DMA((2, 3)),
            pltpu.SemaphoreType.DMA((2, 6)),
            pltpu.SemaphoreType.DMA((6, 2, 2, 11)),
        ]
        + [pltpu.VMEM(shape, BF16) for shape in slots.values()],
        compiler_params=pltpu.CompilerParams(
            vmem_limit_bytes=VMEM_LIMIT, collective_id=3, has_side_effects=True
        ),
        name="attend_back",
    )(
        split, gain, small, qt, k, kt, v, do, attended, lse, ln, x, wq, wk, wv_t, grad_wo,
        state_down, state_up,
    )


def finish_kernel(
    mid, back, dv, sums, down, up, wo, low, thin, last,
    grad_input, grad_first, grad_down, grad_up, grad_wo, grad_q, grad_k, grad_v, bu,
    bias_q, bias_v, gain_two, shift_two, bias_o, bias_d, gain_one, shift_one,
):
    step = pl.program_id(0)
    cols = wo.shape[2]
    pair = 2 * HEAD_DIM
    grad_input[...] = mid[...] + back[...].astype(F32)
    grad_first[...] = dv[...]
    grad_down[...] = down[0].astype(F32)
    grad_up[...] = up[...].astype(F32)

    @pl.when(step == 0)
    def _():
        heads = grad_wo.shape[0]
        for j in range(2):
            span = slice(j * cols, (j + 1) * cols)
            grad_wo[:, span] = wo[j, :heads].astype(F32)
            grad_v[:pair, span] = wo[j, heads + 2 * pair :].astype(F32)
            grad_v[pair:, span] = thin[HEAD_DIM * j : HEAD_DIM * (j + 1)].astype(F32)
            for i, target in enumerate((grad_q, grad_k)):
                first = heads + i * pair
                target[span, :pair] = wo[j, first : first + pair].astype(F32).T
                target[span, 2 * pair :] = last[j, i * pair : (i + 1) * pair].astype(F32).T
        for i, target in enumerate((grad_q, grad_k)):
            target[:, pair : 2 * pair] = low[i * pair : (i + 1) * pair].astype(F32).T
        chunk = bu.shape[0] // 3
        for i in range(3):
            bu[i * chunk : (i + 1) * chunk] = sums[ROW_BU + i, :chunk]
        bias_q[...] = sums[ROW_BQ, : bias_q.shape[0]]
        bias_v[...] = sums[ROW_BV, : bias_v.shape[0]]
        for i, target in enumerate((gain_two, shift_two, bias_o, bias_d, gain_one, shift_one)):
            target[...] = sums[i, :]


def finish(mid, back, dv, sums, down, up, wo, low, thin, last):
    rows, width = mid.shape
    heads = wo.shape[1] // 2
    fresh = heads // 2
    hidden = up.shape[1]
    steps = 6
    chunk = down.shape[1]
    half = chunk // 2
    out_rows = 192
    operands = (mid, back, dv, sums, down, up, wo, low, thin, last)
    once = pl.Buffered(1)
    fixed = lambda s: pl.BlockSpec(s, lambda i, nd=len(s): (0,) * nd, pipeline_mode=once)
    by_rows = lambda n, c: pl.BlockSpec((n, c), lambda i: (i, 0))
    specs = [fixed(a.shape) for a in operands]
    specs[0] = specs[1] = by_rows(out_rows, width)
    specs[2] = by_rows(dv.shape[0] // steps, dv.shape[1])
    specs[4] = pl.BlockSpec((1, half, width), lambda i: (i // 2, lax.rem(i, 2), 0))
    specs[5] = by_rows(width // steps, hidden)
    shapes = [(rows, width), dv.shape, (hidden, width), (width, hidden), (heads, width)]
    shapes += [(width, heads), (width, heads), (fresh, width)]
    shapes += [(hidden,), (heads,), (fresh,)] + [(width,)] * 6
    out_specs = [fixed(s) for s in shapes]
    out_specs[0], out_specs[1] = specs[0], specs[2]
    out_specs[2], out_specs[3] = by_rows(half, width), specs[5]
    return pl.pallas_call(
        finish_kernel,
        grid=(steps,),
        in_specs=specs,
        out_specs=out_specs,
        out_shape=[jax.ShapeDtypeStruct(s, F32) for s in shapes],
        compiler_params=pltpu.CompilerParams(vmem_limit_bytes=VMEM_LIMIT),
        name="finish",
    )(*operands)


def swap(array):
    return lax.ppermute(array, "tensor", [(0, 1), (1, 0)])


def across_blocks(array, row_chips):
    chips = 4 * row_chips * row_chips
    shift = 2
    while shift < row_chips:
        for stride in (shift, shift * row_chips):
            pairs = [(i, i ^ stride) for i in range(chips)]
            array = array + lax.ppermute(array, "dp", pairs)
        shift *= 2
    return array


def on_device(
    row_chips,
    input_rows, first_values, doc_split, gain_norm1, bias_norm1, w_query, bias_query, w_key,
    w_value, bias_value, w_out, bias_attn_out, gain_norm2, bias_norm2, w_up, bias_up, w_down,
    bias_down, cotangent,
):
    heads = w_query.shape[1]
    fresh = w_value.shape[1]
    hidden = w_up.shape[1]
    pair = 2 * HEAD_DIM
    wv_t = w_value.T
    ln, qt, k, kt, v, vt = project(
        input_rows, first_values.T, gain_norm1, bias_norm1, w_query, bias_query, w_key, wv_t,
        bias_value,
    )
    up, down, wo, bu, vt = lax.optimization_barrier((w_up, w_down, w_out, bias_up, vt))
    up_other, down_other, wo_other, bu_other = swap(up), swap(down), swap(wo), swap(bu)
    attended, lse = attend(doc_split, qt, k, vt)
    output, grad_middle, grad_att, state_down, state_up, grad_wo, small = feed(
        row_chips, input_rows, cotangent, attended, w_out, wo_other, bias_attn_out, gain_norm2,
        bias_norm2, up_other, w_up, bu_other, bias_up, down_other, w_down, bias_down,
    )
    back, dv_first, *reduced = attend_back(
        row_chips, doc_split, gain_norm1, small, qt, k, kt, v, grad_att, attended, lse, ln,
        input_rows, w_query, w_key, wv_t, grad_wo, state_down, state_up,
    )
    reduced = [across_blocks(a, row_chips) for a in reduced]
    (
        grad_input, grad_first, grad_down, grad_up, grad_wo, grad_q, grad_k, grad_v, bias_grad_up,
        bias_grad_q, bias_grad_v, gain_two, shift_two, bias_grad_o, bias_grad_d, gain_one, shift_one,
    ) = finish(grad_middle, back, dv_first, *reduced)
    return (
        output, grad_input, grad_first.T, gain_one, shift_one, grad_q, bias_grad_q, grad_k, grad_v.T,
        bias_grad_v, grad_wo, bias_grad_o, gain_two, shift_two, grad_up, bias_grad_up, grad_down,
        bias_grad_d,
    )


def solution(mesh):
    row_chips = 1
    while 4 * row_chips * row_chips < mesh.shape["dp"]:
        row_chips += 1
    rows = P(("dp", "tensor"), None)
    cols = P(None, "tensor")
    split = P("tensor")
    firsts = P("dp", "tensor")
    wide = P("tensor", None)
    return jax.shard_map(
        functools.partial(on_device, row_chips),
        mesh=mesh,
        in_specs=(
            rows, firsts, P("dp"), P(), P(), cols, split, cols, cols, split, wide, P(), P(), P(),
            cols, split, wide, P(), rows,
        ),
        out_specs=(
            rows, rows, firsts, P(), P(), cols, split, cols, cols, split, wide, P(), P(), P(),
            cols, split, wide, P(),
        ),
        check_vma=False,
    )
```

```python
import functools

import jax
import jax.numpy as jnp
from jax import lax
from jax.experimental import pallas as pl
from jax.experimental.pallas import tpu as pltpu
from jax.sharding import PartitionSpec as P

HEAD_DIM = 64
NORM_EPS = 1e-05
GELU_ROOT = 0.7978845608028654
GELU_CUBE = 0.044715
NN = (((1,), (0,)), ((), ()))
NT = (((1,), (1,)), ((), ()))
TN = (((0,), (0,)), ((), ()))
F32 = jnp.float32
BF16 = jnp.bfloat16
VMEM_LIMIT = 60 << 20
MESH = pl.DeviceIdType.MESH


def dot(left, right, dims=NN):
    return lax.dot_general(left, right, dims, preferred_element_type=F32)


def whole(array):
    return pl.BlockSpec(array.shape, lambda *_, nd=array.ndim: (0,) * nd)


def whole_shape(shape):
    return pl.BlockSpec(shape, lambda *_, nd=len(shape): (0,) * nd)


def row_normalize(rows):
    centered = rows - jnp.mean(rows, axis=1, keepdims=True)
    inverse = lax.rsqrt(jnp.mean(centered * centered, axis=1, keepdims=True) + NORM_EPS)
    return centered * inverse, inverse


def row_normalize_back(scaled, normed, inverse):
    return inverse * (
        scaled
        - jnp.mean(scaled, axis=1, keepdims=True)
        - normed * jnp.mean(scaled * normed, axis=1, keepdims=True)
    )


AXES = ("x", "y", "z")
SIZE = {"x": 2, "y": 2, "z": 4}


class Place:
    def __init__(self, row_chips):
        index = lax.axis_index("dp")
        self.core = lax.axis_index("tensor")
        self.wide = row_chips
        self.index = index
        self.x = lax.rem(index, row_chips)
        self.y = lax.rem(index // row_chips, row_chips)
        self.z = index // (row_chips * row_chips)
        self.at = {"x": lax.rem(self.x, 2), "y": lax.rem(self.y, 2), "z": self.z}

    def peer(self, axis, step):
        size = SIZE[axis]
        spot = lax.rem(self.at[axis] + step, size)
        stride = {"x": 1, "y": self.wide, "z": self.wide * self.wide}[axis]
        return spot, (self.index + (spot - self.at[axis]) * stride, self.core)

    def twin(self):
        return (self.index, 1 - self.core)

    def others(self):
        return [self.twin()] + [self.peer(a, k)[1] for a in AXES for k in range(1, SIZE[a])]


def greet(place):
    barrier = pltpu.get_barrier_semaphore()
    devices = place.others()
    for device in devices:
        pl.semaphore_signal(barrier, inc=1, device_id=device, device_id_type=MESH)
    return lambda: pl.semaphore_wait(barrier, len(devices))


class Sum:
    def __init__(self, place, order, held, slots, result, sems):
        self.place, self.order, self.held = place, order, held
        self.slots, self.result, self.sems = slots, result, sems
        self.rows = (held if held is not None else result).shape[0]

    def region(self, depth):
        start, size = 0, self.rows
        for axis in self.order[:depth]:
            size //= SIZE[axis]
            start = start + self.place.at[axis] * size
        return start, size

    def span(self, depth):
        start, size = self.region(depth)
        return pl.ds(pl.multiple_of(start, 16) if depth else start, size)

    def first_sem(self, gather, stage):
        count = 0
        for axis in self.order[:stage]:
            count += SIZE[axis] - 1
        return count + (5 if gather else 0)

    def scatter_copies(self, stage):
        axis = self.order[stage]
        start, size = self.region(stage)
        piece = size // SIZE[axis]
        base = self.first_sem(False, stage)
        copies = []
        for step in range(1, SIZE[axis]):
            spot, device = self.place.peer(axis, step)
            copies.append(
                pltpu.make_async_remote_copy(
                    src_ref=self.held.at[pl.ds(pl.multiple_of(start + spot * piece, 16), piece), :],
                    dst_ref=self.slots[stage].at[step - 1],
                    send_sem=self.sems.at[0, base + step - 1],
                    recv_sem=self.sems.at[1, base + step - 1],
                    device_id=device,
                    device_id_type=MESH,
                )
            )
        return copies

    def scatter_end(self, stage):
        for copy in self.scatter_copies(stage):
            copy.wait()
        span = self.span(stage + 1)
        total = self.held[span, :].astype(F32)
        for step in range(SIZE[self.order[stage]] - 1):
            total = total + self.slots[stage][step].astype(F32)
        self.held[span, :] = total.astype(BF16)

    def gather_copies(self, stage, source):
        axis = self.order[stage]
        span = self.span(stage + 1)
        base = self.first_sem(True, stage)
        copies = []
        origin = self.result if source is None else source
        for step in range(1, SIZE[axis]):
            _, device = self.place.peer(axis, step)
            copies.append(
                pltpu.make_async_remote_copy(
                    src_ref=origin.at[span, :],
                    dst_ref=self.result.at[span, :],
                    send_sem=self.sems.at[0, base + step - 1],
                    recv_sem=self.sems.at[1, base + step - 1],
                    device_id=device,
                    device_id_type=MESH,
                )
            )
        if source is not None:
            copies.append(
                pltpu.make_async_copy(
                    source.at[span, :], self.result.at[span, :], self.sems.at[0, 10]
                )
            )
        return copies

    def run(self, action, source=None):
        verb, letter = action
        gather = letter in "cba"
        stage = "abc".index(letter) if gather else "ABC".index(letter)
        if gather:
            for copy in self.gather_copies(stage, source):
                copy.start() if verb == "s" else copy.wait()
        elif verb == "s":
            for copy in self.scatter_copies(stage):
                copy.start()
        else:
            self.scatter_end(stage)


def slot_shapes(order, rows, cols):
    shapes = []
    for axis in order:
        rows //= SIZE[axis]
        shapes.append((SIZE[axis] - 1, rows, cols))
    return shapes


ORDERS = ("xyz", "yxz")
FEED_PLAN = {
    "s1m": ((0, "sA"),),
    "s3m": ((0, "fA"), (0, "sB"), (1, "sA"),),
    "s4m": ((0, "fB"), (0, "sC"),),
    "s5e": ((1, "fA"), (1, "sB"),),
    "f_end": ((0, "fC"), (1, "fB"),),
}
BACK_PLAN = {
    (0, 0): ((1, "sC"), (2, "sA"), (0, "sc"),),
    (0, 7): ((1, "fC"), (2, "fA"), (2, "sB"), (3, "sA"), (1, "sc"),),
    (1, 5): ((2, "fB"), (0, "fc"), (2, "sC"), (0, "sb"),),
    (1, 7): ((3, "fA"), (3, "sB"), (4, "sA"),),
    (2, 0): ((1, "fc"), (1, "sb"),),
    (2, 2): ((0, "fb"), (0, "sa"),),
    (2, 4): ((3, "fB"), (3, "sC"),),
    (2, 6): ((2, "fC"), (4, "fA"), (4, "sB"), (2, "sc"),),
    (2, 7): ((5, "sA"),),
    "e1": ((1, "fb"), (3, "fC"), (1, "sa"), (3, "sc"),),
    "e5": ((0, "fa"), (4, "fB"), (2, "fc"), (4, "sC"), (2, "sb"),),
    "e6": ((5, "fA"), (5, "sB"),),
    "w0": ((3, "fc"), (3, "sb"),),
    "w1": ((4, "fC"), (4, "sc"),),
    "w2": ((1, "fa"),),
    "w3": ((2, "fb"), (4, "fc"), (2, "sa"), (4, "sb"),),
    "w4": ((5, "fB"), (5, "sC"),),
    "w5": ((3, "fb"), (3, "sa"),),
    "w6": ((5, "fC"), (5, "sc"),),
    "w7": ((5, "fc"), (5, "sb"),),
    "w8": ((2, "fa"),),
    "w9": ((4, "fb"), (4, "sa"),),
    "w10": ((3, "fa"),),
    "w11": ((5, "fb"), (5, "sa"),),
    "w12": ((4, "fa"),),
    "w13": ((5, "fa"),),
}


def started(plan):
    return [(i, action[1]) for actions in plan.values() for i, action in actions if action[0] == "s"]


def progress(batch):
    return sum(1 for i, _ in started(FEED_PLAN) if i == batch)


def scatter_slots(plan, shapes):
    slots = {}
    for i, letter in started(plan):
        if letter in "ABC":
            for j, order in enumerate(ORDERS):
                shape = slot_shapes(order, *shapes[i][j])["ABC".index(letter)]
                slots[i, j, letter] = shape
    return slots


def project_kernel(
    block, x, first_t, gain, bias, wq, bq, wk, wv_t, bv, ln, qt, k, kt, v, vt,
    x_other, weights, s_ln, s_qt, s_k, s_kt, s_v, s_vt, pair_sems, out_sems,
):
    rows = x.shape[0]
    heads, fresh = wq.shape[1], wv_t.shape[0]
    core = lax.axis_index("tensor")
    twin = (lax.axis_index("dp"), 1 - core)
    barrier = pltpu.get_barrier_semaphore()
    pl.semaphore_signal(barrier, inc=1, device_id=twin, device_id_type=MESH)
    weights[:, :heads] = wq[...]
    weights[:, heads : 2 * heads] = wk[...]
    weights[:, 2 * heads :] = wv_t[...].T
    pl.semaphore_wait(barrier, 1)
    send = pltpu.make_async_remote_copy(
        src_ref=x, dst_ref=x_other, send_sem=pair_sems.at[0], recv_sem=pair_sems.at[1],
        device_id=twin, device_id_type=MESH,
    )
    send.start()
    gain_row = gain[...].astype(F32).reshape(1, -1)
    bias_row = bias[...].astype(F32).reshape(1, -1)
    bq_row = bq[...].astype(F32).reshape(1, -1)
    bv_row = bv[...].astype(F32).reshape(1, -1)
    copies = []
    for part, source in enumerate((x, x_other)):
        if part:
            send.wait_recv()
        spot = pl.multiple_of((core if part == 0 else 1 - core) * rows, rows)
        for first in range(0, rows, block):
            span = pl.ds(first, block)
            normed, _ = row_normalize(source[span, :].astype(F32))
            low = (normed * gain_row + bias_row).astype(BF16)
            s_ln[part, span] = low
            product = dot(low, weights[...])
            queries = (product[:, :heads] + bq_row).astype(BF16).astype(F32) * HEAD_DIM ** (-0.5)
            s_qt[part, :, span] = queries.astype(BF16).T
            keys = product[:, heads : 2 * heads].astype(BF16)
            s_k[part, span] = keys
            s_kt[part, :, span] = keys.T
            values = (product[:, 2 * heads :] + bv_row).astype(BF16)
            reused = first_t[:, pl.ds(pl.multiple_of(spot + first, block), block)]
            s_vt[part, :fresh, span] = values.T
            s_vt[part, fresh:, span] = reused
            s_v[part, span] = jnp.concatenate([values, reused.T], axis=1)
        targets = (
            (s_ln, ln.at[pl.ds(spot, rows), :]),
            (s_qt, qt.at[:, pl.ds(spot, rows)]),
            (s_k, k.at[pl.ds(spot, rows), :]),
            (s_kt, kt.at[:, pl.ds(spot, rows)]),
            (s_v, v.at[pl.ds(spot, rows), :]),
            (s_vt, vt.at[:, pl.ds(spot, rows)]),
        )
        for i, (held, target) in enumerate(targets):
            copy = pltpu.make_async_copy(held.at[part], target, out_sems.at[part, i])
            copy.start()
            copies.append(copy)
    send.wait_send()
    for copy in copies:
        copy.wait()


def project(x, first_t, gain, bias, wq, bq, wk, wv_t, bv, block=256):
    rows, width = x.shape
    heads = wq.shape[1]
    tall, flat = (rows, heads), (heads, rows)
    vmem = pl.BlockSpec(memory_space=pltpu.VMEM)
    shapes = ((2 * rows, width), (heads, 2 * rows), (2 * rows, heads)) + (
        (heads, 2 * rows), (2 * rows, heads), (heads, 2 * rows),
    )
    scratch = [(rows, width), (width, 2 * heads + wv_t.shape[0])]
    scratch += [(2,) + s for s in ((rows, width), flat, tall, flat, tall, flat)]
    return pl.pallas_call(
        functools.partial(project_kernel, block),
        out_shape=[jax.ShapeDtypeStruct(s, BF16) for s in shapes],
        in_specs=[vmem] * 9,
        out_specs=[pl.BlockSpec(memory_space=pl.ANY)] * 6,
        scratch_shapes=[pltpu.VMEM(s, BF16) for s in scratch]
        + [pltpu.SemaphoreType.DMA((2,)), pltpu.SemaphoreType.DMA((2, 6))],
        compiler_params=pltpu.CompilerParams(
            vmem_limit_bytes=VMEM_LIMIT, collective_id=1, has_side_effects=True
        ),
        name="project",
    )(x, first_t, gain, bias, wq, bq, wk, wv_t, bv)


def causal(size):
    keys = lax.broadcasted_iota(jnp.int32, (size, size), 0)
    return keys <= lax.broadcasted_iota(jnp.int32, (size, size), 1)


def attend_kernel(block, ahead, split, qt, k, vt, attended, lse, sums, k_aug, q_aug):
    width, tokens = qt.shape
    half = tokens // 2
    pair_width = 2 * HEAD_DIM
    far = jnp.where(split[0] < tokens, -1e9, 0.0)
    row = lax.broadcasted_iota(jnp.int32, (HEAD_DIM, tokens), 0)
    token = lax.broadcasted_iota(jnp.int32, (HEAD_DIM, tokens), 1)
    far_rows = jnp.where((row == 0) & (token >= half), far, 0.0).astype(BF16)
    lane = lax.broadcasted_iota(jnp.int32, (tokens, pair_width), 1)
    key = lax.broadcasted_iota(jnp.int32, (tokens, pair_width), 0)
    first_half = jnp.where((lax.rem(lane, HEAD_DIM) == 0) & (key < half), 1.0, 0.0).astype(BF16)
    ones = (lax.broadcasted_iota(jnp.int32, (16, tokens), 0) == 0).astype(BF16)
    for j in range(2):
        sums[j, HEAD_DIM:, :] = ones
        extra = HEAD_DIM * (1 - j)
        q_aug[j, extra : extra + HEAD_DIM, :] = far_rows

    def pair_step(pair, _):
        col = pl.multiple_of(pair * pair_width, pair_width)
        head_rows = [pl.ds(pl.multiple_of(col + HEAD_DIM * j, HEAD_DIM), HEAD_DIM) for j in range(2)]
        keys = k[:, pl.ds(col, pair_width)]
        for j in range(2):
            base = HEAD_DIM * j
            sums[j, :HEAD_DIM, :] = vt[head_rows[j], :]
            k_aug[j] = jnp.where(lane // HEAD_DIM == j, keys, first_half)
            q_aug[j, base : base + HEAD_DIM, :] = qt[head_rows[j], :]

        def products(number, j):
            start, stop = number * block, (number + 1) * block
            return dot(k_aug[j, :stop, :], q_aug[j, :, start:stop])

        def average(number, j, scores):
            start, stop = number * block, (number + 1) * block
            edge = jnp.where(causal(block), scores[start:], -1e30)
            top = jnp.max(edge, axis=0, keepdims=True)
            if start:
                near = scores[:start]
                top = jnp.maximum(top, jnp.max(near, axis=0, keepdims=True))
                weights = jnp.concatenate(
                    [jnp.exp(near - top).astype(BF16), jnp.exp(edge - top).astype(BF16)], axis=0
                )
            else:
                weights = jnp.exp(edge - top).astype(BF16)
            total = dot(sums[j, :, :stop], weights)
            denominator = total[HEAD_DIM : HEAD_DIM + 1]
            attended[head_rows[j], start:stop] = (total[:HEAD_DIM] * (1.0 / denominator)).astype(BF16)
            lse[pl.ds(pair * 2 + j, 1), :, start:stop] = (top + jnp.log(denominator))[None]

        units = [(number, j) for number in range(tokens // block) for j in range(2)]
        queue = [products(*unit) for unit in units[:ahead]]
        for i, unit in enumerate(units):
            if i + ahead < len(units):
                queue.append(products(*units[i + ahead]))
            average(*unit, queue.pop(0))
        return 0

    lax.fori_loop(0, width // pair_width, pair_step, 0)


def attend(split, qt, k, vt, block=256, ahead=4):
    width, tokens = qt.shape
    pair_width = 2 * HEAD_DIM
    vmem = pl.BlockSpec(memory_space=pltpu.VMEM)
    return pl.pallas_call(
        functools.partial(attend_kernel, block, ahead),
        out_shape=(
            jax.ShapeDtypeStruct((width, tokens), BF16),
            jax.ShapeDtypeStruct((width // HEAD_DIM, 1, tokens), F32),
        ),
        in_specs=[pl.BlockSpec(memory_space=pltpu.SMEM), vmem, vmem, vmem],
        out_specs=(vmem, vmem),
        scratch_shapes=[
            pltpu.VMEM((2, HEAD_DIM + 16, tokens), BF16),
            pltpu.VMEM((2, tokens, pair_width), BF16),
            pltpu.VMEM((2, pair_width, tokens), BF16),
        ],
        compiler_params=pltpu.CompilerParams(vmem_limit_bytes=VMEM_LIMIT),
        name="attend",
    )(split, qt, k, vt)


def gelu_both(v):
    square = v * v
    tanh = jnp.tanh(v * (GELU_ROOT + (GELU_ROOT * GELU_CUBE) * square))
    half = 0.5 * v
    slope = 0.5 + 0.5 * tanh + half * (1.0 - tanh * tanh) * (
        GELU_ROOT + (3.0 * GELU_ROOT * GELU_CUBE) * square
    )
    return half + half * tanh, slope


SUM_ROWS = 16
ROW_BU, ROW_BU_OTHER, ROW_BQ, ROW_BV = 6, 9, 12, 13


def feed_kernel(
    row_chips, slot_keys, x_far, cot_far, attended, wo_own_far, wo_other_far, bias_o, gain, bias,
    up_other, up_own, bu_other, bu_own, down_other, down_own, bias_d,
    out, grad_mid, grad_att, state_down, state_up, grad_wo, small,
    att_own, att_other, ln, ln_t, normed, inverse, total, grad_ln, att_stage, stage_down, stage_up,
    held_down, held_up, x, cot, wo_own, wo_other, kept_act, kept_grad,
    move_sems, load_sems, pair_sems, sum_sems, *slot_refs,
):
    state, stage, held = (state_down, state_up), (stage_down, stage_up), (held_down, held_up)
    slots = dict(zip(slot_keys, slot_refs))
    step = pl.program_id(0)
    place = Place(row_chips)
    core = place.core
    rows = x.shape[0]
    heads = att_own.shape[0]
    chunk = up_own.shape[1]
    index = step // 2
    own = pl.ds(pl.multiple_of(core * rows, rows), rows)
    theirs = pl.ds(pl.multiple_of((1 - core) * rows, rows), rows)

    def to_twin(source, target, i):
        return pltpu.make_async_remote_copy(
            src_ref=source, dst_ref=target, send_sem=pair_sems.at[0, i],
            recv_sem=pair_sems.at[1, i], device_id=place.twin(), device_id_type=MESH,
        )

    def stage_copies(i):
        return [to_twin(stage[j].at[i], held[j].at[i], 2 + 2 * i + j) for j in range(2)]

    def part(i, j):
        return Sum(
            place, ORDERS[j], held[j].at[i], [slots.get((i, j, letter)) for letter in "ABC"],
            state[j].at[i], sum_sems.at[i, j],
        )

    def act(point):
        for i, action in FEED_PLAN.get(point, ()):
            for j in range(2):
                part(i, j).run(action, held[j].at[i] if action[1] == "c" else None)

    def act_at(name, odd):
        for k in range(odd, 6, 2):
            point = "s%d%s" % (k, name)
            if point in FEED_PLAN:
                pl.when(step == k)(functools.partial(act, point))

    @pl.when(step == 0)
    def _():
        ready = greet(place)
        loads = [
            pltpu.make_async_copy(source, target, load_sems.at[i])
            for i, (source, target) in enumerate(
                (
                    (attended.at[:, own], att_own), (wo_own_far, wo_own), (x_far, x),
                    (wo_other_far, wo_other), (cot_far, cot),
                )
            )
        ]
        for load in loads:
            load.start()
        ready()
        exchange = to_twin(attended.at[:, theirs], att_other, 0)
        exchange.start()
        grad_ln[...] = jnp.zeros_like(grad_ln)
        small[...] = jnp.zeros_like(small)
        for load in loads:
            load.wait()
        total[...] = x[...].astype(F32) + (
            dot(att_own[...], wo_own[...], TN) + bias_o[...].astype(F32).reshape(1, -1)
        )
        exchange.wait()
        mid = total[...] + dot(att_other[...], wo_other[...], TN)
        total[...] = mid + bias_d[...].astype(F32).reshape(1, -1)
        norm, inv = row_normalize(mid)
        normed[...] = norm
        inverse[...] = jnp.broadcast_to(inv, inverse.shape)
        low = (
            norm * gain[...].astype(F32).reshape(1, -1) + bias[...].astype(F32).reshape(1, -1)
        ).astype(BF16)
        ln[...] = low
        ln_t[...] = low.T

    def weight_grads(up, bias_up, down):
        hidden = dot(ln[...], up[...]) + bias_up[
            pl.ds(pl.multiple_of(index * chunk, chunk), chunk)
        ].astype(F32).reshape(1, -1)
        activated, slope = gelu_both(hidden)
        activated = activated.astype(BF16)
        grad_hidden = (dot(cot[...], down[...], NT) * slope).astype(BF16)
        grad_down = dot(activated, cot[...], TN)
        grad_up = dot(ln_t[...], grad_hidden)
        sums = jnp.sum(grad_hidden.astype(F32), axis=0, keepdims=True)
        return activated, grad_hidden, grad_down, grad_up, sums

    @pl.when(lax.rem(step, 2) == 0)
    def _():
        activated, grad_hidden, grad_down, grad_up, sums = weight_grads(
            up_other, bu_other, down_other
        )
        stage_down[index] = grad_down.astype(BF16)
        stage_up[index] = grad_up.astype(BF16)
        for copy in stage_copies(index):
            copy.start()
        small[pl.ds(ROW_BU_OTHER + index, 1), :chunk] = sums
        kept_act[...] = activated
        kept_grad[...] = grad_hidden
        act_at("m", 0)

    @pl.when(lax.rem(step, 2) == 1)
    def _():
        activated, grad_hidden, grad_down, grad_up, sums = weight_grads(up_own, bu_own, down_own)
        for copy in stage_copies(index):
            copy.wait()
        held_down[index] = (grad_down + held_down[index].astype(F32)).astype(BF16)
        held_up[index] = (grad_up + held_up[index].astype(F32)).astype(BF16)
        small[pl.ds(ROW_BU + index, 1), :chunk] = sums

        act_at("m", 1)
        total[...] += dot(kept_act[...], down_other[...]) + dot(activated, down_own[...])
        grad_ln[...] += dot(kept_grad[...], up_other[...], NT) + dot(grad_hidden, up_own[...], NT)
        act_at("e", 1)

    @pl.when(step == 5)
    def _():
        grad = grad_ln[...]
        norm = normed[...]
        cot32 = cot[...].astype(F32)
        scaled = grad * gain[...].astype(F32).reshape(1, -1)
        mid = cot32 + row_normalize_back(scaled, norm, inverse[:, :1])
        grad_mid[...] = mid
        low = mid.astype(BF16)
        att_stage[1] = dot(wo_other[...], low, NT).astype(BF16)
        exchange = to_twin(att_stage.at[1], grad_att.at[:, own], 1)
        exchange.start()
        att_stage[0] = dot(wo_own[...], low, NT).astype(BF16)
        local = pltpu.make_async_copy(att_stage.at[0], grad_att.at[:, own], move_sems.at[0])
        local.start()
        out[...] = total[...].astype(BF16)
        small[0:1, :] = jnp.sum(grad * norm, axis=0, keepdims=True)
        small[1:2, :] = jnp.sum(grad, axis=0, keepdims=True)
        small[2:3, :] = jnp.sum(low.astype(F32), axis=0, keepdims=True)
        small[3:4, :] = jnp.sum(cot32, axis=0, keepdims=True)
        grad_wo[:heads] = dot(att_own[...], low).astype(BF16)
        grad_wo[heads:] = dot(att_other[...], low).astype(BF16)
        act("f_end")
        moves = [local]
        for i in range(3):
            if progress(i) > 3:
                continue
            for j in range(2):
                span = part(i, j).span(progress(i))
                move = pltpu.make_async_copy(
                    held[j].at[i, span, :], state[j].at[i, span, :], move_sems.at[1 + 2 * i + j]
                )
                move.start()
                moves.append(move)
        exchange.wait()
        for move in moves:
            move.wait()


def feed(
    row_chips, x, cot, attended, wo_own, wo_other, bias_o, gain, bias,
    up_other, up_own, bu_other, bu_own, down_other, down_own, bias_d,
):
    rows, width = x.shape
    hidden = up_own.shape[1]
    heads = wo_own.shape[0]
    chunk = hidden // 3
    once = pl.Buffered(1)
    fixed = lambda s: pl.BlockSpec(s, lambda j, nd=len(s): (0,) * nd, pipeline_mode=once)
    anywhere = pl.BlockSpec(memory_space=pl.ANY)
    up_spec = pl.BlockSpec((width, chunk), lambda j: (0, j // 2))
    down_spec = pl.BlockSpec((chunk, width), lambda j: (j // 2, 0))
    operands = (
        x, cot, attended, wo_own, wo_other, bias_o, gain, bias,
        up_other, up_own, bu_other, bu_own, down_other, down_own, bias_d,
    )
    specs = [fixed(a.shape) for a in operands]
    for i in range(5):
        specs[i] = anywhere
    specs[8] = specs[9] = up_spec
    specs[12] = specs[13] = down_spec
    results = [
        ((rows, width), BF16),
        ((rows, width), F32),
        ((heads, 2 * rows), BF16),
        ((3, chunk, width), BF16),
        ((3, width, chunk), BF16),
        ((2 * heads, width), BF16),
        ((SUM_ROWS, width), F32),
    ]
    out_specs = [fixed(s) for s, _ in results]
    out_specs[2] = out_specs[3] = out_specs[4] = anywhere
    slots = scatter_slots(FEED_PLAN, {i: ((chunk, width), (width, chunk)) for i in range(3)})
    return pl.pallas_call(
        functools.partial(feed_kernel, row_chips, list(slots)),
        grid=(6,),
        in_specs=specs,
        out_specs=out_specs,
        out_shape=[jax.ShapeDtypeStruct(s, t) for s, t in results],
        scratch_shapes=[
            pltpu.VMEM((heads, rows), BF16),
            pltpu.VMEM((heads, rows), BF16),
            pltpu.VMEM((rows, width), BF16),
            pltpu.VMEM((width, rows), BF16),
            pltpu.VMEM((rows, width), F32),
            pltpu.VMEM((rows, 128), F32),
            pltpu.VMEM((rows, width), F32),
            pltpu.VMEM((rows, width), F32),
            pltpu.VMEM((2, heads, rows), BF16),
            pltpu.VMEM((3, chunk, width), BF16),
            pltpu.VMEM((3, width, chunk), BF16),
            pltpu.VMEM((3, chunk, width), BF16),
            pltpu.VMEM((3, width, chunk), BF16),
            pltpu.VMEM((rows, width), BF16),
            pltpu.VMEM((rows, width), BF16),
            pltpu.VMEM((heads, width), BF16),
            pltpu.VMEM((heads, width), BF16),
            pltpu.VMEM((rows, chunk), BF16),
            pltpu.VMEM((rows, chunk), BF16),
            pltpu.SemaphoreType.DMA((7,)),
            pltpu.SemaphoreType.DMA((5,)),
            pltpu.SemaphoreType.DMA((2, 8)),
            pltpu.SemaphoreType.DMA((3, 2, 2, 11)),
        ]
        + [pltpu.VMEM(shape, BF16) for shape in slots.values()],
        compiler_params=pltpu.CompilerParams(
            vmem_limit_bytes=VMEM_LIMIT, collective_id=2, has_side_effects=True,
            dimension_semantics=("arbitrary",),
        ),
        name="feed",
    )(*operands)


def extra_rows(row, fourth):
    high = row.astype(BF16).astype(F32)
    middle = (row - high).astype(BF16).astype(F32)
    low = row - high - middle
    index = lax.broadcasted_iota(jnp.int32, (HEAD_DIM, row.shape[1]), 0)
    rest = jnp.where(index == 2, low, jnp.where(index == 3, fourth, 0.0))
    return jnp.where(index == 0, high, jnp.where(index == 1, middle, rest)).astype(BF16)


def attend_back_kernel(
    row_chips, block, slot_keys, split, gain, small, qt_far, k_far, kt_far, v_far, do_far, attended_far, lse_far,
    ln_far, x_far, wq_far, wk_far, wv_far, grad_wo_far, state_down, state_up,
    back, dv_first, sums, red_down, red_up, red_wo, red_low, red_v, red_last,
    stack, q_aug, d_aug, k_aug, v_aug, dk_sum, dv_sum, weights, terms_send, terms_got,
    wo_got, held_down, held_up, held_wo, held_low, held_v, held_last, sums_got,
    qt, k, kt, v, do, attended, lse, ln, x,
    move_sems, load_sems, pair_sems, tiny_sems, sum_sems, *slot_refs,
):
    state, held = (state_down, state_up), (held_down, held_up)
    slots = dict(zip(slot_keys, slot_refs))
    width, tokens = qt.shape
    half = tokens // 2
    fresh, model = wv_far.shape
    place = Place(row_chips)
    core = place.core
    pair_width = 2 * HEAD_DIM
    own = pl.ds(pl.multiple_of(core * half, half), half)
    theirs = pl.ds(pl.multiple_of((1 - core) * half, half), half)

    def to_twin(source, target, i):
        return pltpu.make_async_remote_copy(
            src_ref=source, dst_ref=target, send_sem=pair_sems.at[0, i],
            recv_sem=pair_sems.at[1, i], device_id=place.twin(), device_id_type=MESH,
        )

    def part(i, j):
        chunk = state_down.shape[1]
        if i < 3:
            holder = held[j].at[i]
            result = red_up.at[:, i * chunk : (i + 1) * chunk] if j else red_down.at[i]
        else:
            holder, result = {
                3: (held_wo.at[j], red_wo.at[j]),
                4: ((held_low, red_low), (held_v, red_v))[j],
                5: (held_last.at[j], red_last.at[j]),
            }[i]
        return Sum(
            place, ORDERS[j], holder, [slots.get((i, j, letter)) for letter in "ABC"], result,
            sum_sems.at[i, j],
        )

    def act(point):
        for i, action in BACK_PLAN.get(point, ()):
            for j in range(2):
                one = part(i, j)
                source = None
                if action[1] == "c":
                    source = one.held
                elif action[1] == "b" and i < 3 and progress(i) == 4:
                    source = state[j].at[i]
                one.run(action, source)

    loads = []
    for i in range(3):
        if progress(i) < 4:
            for j in range(2):
                span = part(i, j).span(progress(i))
                loads.append(
                    pltpu.make_async_copy(
                        state[j].at[i, span, :], held[j].at[i, span, :], move_sems.at[2 * i + j]
                    )
                )
    ready = greet(place)
    for load in loads:
        load.start()
    arriving = [
        pltpu.make_async_copy(far, near, load_sems.at[i])
        for i, (far, near) in enumerate(
            (
                (k_far, k), (qt_far, qt), (v_far, v), (do_far, do), (attended_far, attended),
                (lse_far, lse), (kt_far, kt), (wq_far, terms_send.at[:model, :width]),
                (wk_far, terms_send.at[:model, width:]), (wv_far, weights.at[2 * width :, :]), (ln_far, ln),
                (x_far, x),
            )
        )
    ]
    for copy in arriving:
        copy.start()
    ready()
    wo_exchange = to_twin(grad_wo_far.at[width:, :], wo_got, 0)
    wo_exchange.start()
    for load in loads:
        load.wait()
    act("start")
    for copy in arriving:
        copy.wait()
    weights[:width] = terms_send[:model, :width].T
    weights[width : 2 * width] = terms_send[:model, width:].T
    grad_wo = terms_send.at[:width, :]
    wo_load = pltpu.make_async_copy(grad_wo_far.at[:width, :], grad_wo, load_sems.at[12])
    wo_load.start()
    far = jnp.where(split[0] < tokens, -1e9, 0.0)
    token = lax.broadcasted_iota(jnp.int32, (1, tokens), 1)
    far_row = jnp.where(token >= half, far, 0.0)

    def weight_rows(rows):
        return dot(stack[rows, :], ln[...]).astype(BF16)

    def by_columns(target, start, values):
        cols = target.shape[2]
        for j in range(2):
            target[j, start : start + values.shape[0], :] = values[:, j * cols : (j + 1) * cols]

    def pair_step(pair, _):
        col = pl.multiple_of(pair * pair_width, pair_width)
        lane = lax.broadcasted_iota(jnp.int32, (tokens, pair_width), 1)
        key = lax.broadcasted_iota(jnp.int32, (tokens, pair_width), 0)
        within = lax.rem(lane, HEAD_DIM)
        ones = jnp.where((within < 3) | ((within == 3) & (key < half)), 1.0, 0.0).astype(BF16)
        keys = k[:, pl.ds(col, pair_width)]
        values = v[:, pl.ds(col, pair_width)]
        dk_sum[...] = jnp.zeros_like(dk_sum)
        dv_sum[...] = jnp.zeros_like(dv_sum)
        head_rows = [pl.ds(pl.multiple_of(col + HEAD_DIM * j, HEAD_DIM), HEAD_DIM) for j in range(2)]
        for j in range(2):
            mine = lane // HEAD_DIM == j
            k_aug[j] = jnp.where(mine, keys, ones)
            v_aug[j] = jnp.where(mine, values, ones)
            grad = do[head_rows[j], :]
            inner = jnp.sum(
                grad.astype(F32) * attended[head_rows[j], :].astype(F32), axis=0, keepdims=True
            )
            base, extra = HEAD_DIM * j, HEAD_DIM * (1 - j)
            q_aug[j, base : base + HEAD_DIM, :] = qt[head_rows[j], :]
            q_aug[j, extra : extra + HEAD_DIM, :] = extra_rows(
                -lse[pl.ds(pair * 2 + j, 1)][0], far_row
            )
            d_aug[j, base : base + HEAD_DIM, :] = grad
            d_aug[j, extra : extra + HEAD_DIM, :] = extra_rows(-inner, 0.0)

        def products(number, j):
            start, stop = number * block, (number + 1) * block
            return (
                dot(k_aug[j, :stop, :], q_aug[j, :, start:stop]),
                dot(v_aug[j, :stop, :], d_aug[j, :, start:stop]),
            )

        def gradients(number, j, scores, grad_probs):
            start, stop = number * block, (number + 1) * block
            probs = jnp.where(causal(block), jnp.exp(scores[start:]), 0.0)
            if start:
                probs = jnp.concatenate([jnp.exp(scores[:start]), probs], axis=0)
            grad_scores = (probs * grad_probs).astype(BF16)
            probs = probs.astype(BF16)
            rows = head_rows[j]
            stack[rows, start:stop] = (
                dot(kt[rows, :stop], grad_scores) * HEAD_DIM ** (-0.5)
            ).astype(BF16)
            dv_sum[j, :, :stop] += dot(do[rows, start:stop], probs, NT)
            dk_sum[j, :, :stop] += dot(qt[rows, start:stop], grad_scores, NT)

        units = [(number, j) for number in range(tokens // block) for j in range(2)]
        ahead = products(*units[0])
        for i, unit in enumerate(units):
            now = ahead
            if i + 1 < len(units):
                ahead = products(*units[i + 1])
            gradients(*unit, *now)
            if unit[1] and i + 1 < len(units):
                for p in range(width // pair_width):
                    if (p, unit[0]) in BACK_PLAN:
                        pl.when(pair == p)(functools.partial(act, (p, unit[0])))

        for j in range(2):
            stack[pl.ds(pl.multiple_of(width + col + HEAD_DIM * j, HEAD_DIM), HEAD_DIM), :] = dk_sum[
                j
            ].astype(BF16)

        @pl.when(pair == 0)
        def _():
            stack[2 * width : 2 * width + HEAD_DIM, :] = dv_sum[0].astype(BF16)
            stack[2 * width + HEAD_DIM : 2 * width + 2 * HEAD_DIM, :] = dv_sum[1].astype(BF16)
            wo_exchange.wait()
            wo_load.wait()
            summed = (grad_wo[...].astype(F32) + wo_got[...].astype(F32)).astype(BF16)
            by_columns(held_wo, 0, summed)
            for i in range(3):
                by_columns(
                    held_wo,
                    width + i * pair_width,
                    weight_rows(slice(i * width, i * width + pair_width)),
                )
            act((0, tokens // block - 1))

        @pl.when(pair == 1)
        def _():
            stack[2 * width + 2 * HEAD_DIM :, :] = dv_sum[0].astype(BF16)
            dv_first[:HEAD_DIM, :] = dv_sum[1]
            for i in range(2):
                held_low[i * pair_width : (i + 1) * pair_width] = weight_rows(
                    slice(i * width + pair_width, i * width + 2 * pair_width)
                )
            rest = weight_rows(slice(2 * width + 2 * HEAD_DIM, 2 * width + 3 * HEAD_DIM))
            cols = held_v.shape[1]
            held_v[...] = jnp.zeros_like(held_v)
            for j in range(2):
                held_v[HEAD_DIM * j : HEAD_DIM * (j + 1), :] = rest[:, j * cols : (j + 1) * cols]
            act((1, tokens // block - 1))

        @pl.when(pair == 2)
        def _():
            dv_first[HEAD_DIM : 2 * HEAD_DIM, :] = dv_sum[0]
            dv_first[2 * HEAD_DIM :, :] = dv_sum[1]
            for i in range(2):
                by_columns(
                    held_last,
                    i * pair_width,
                    weight_rows(slice(i * width + 2 * pair_width, i * width + 3 * pair_width)),
                )
            act((2, tokens // block - 1))

        return 0

    lax.fori_loop(0, width // pair_width, pair_step, 0)

    act("e0")
    terms_send[...] = dot(stack[:, theirs], weights[...], TN).astype(BF16)
    terms_exchange = to_twin(terms_send, terms_got, 1)
    terms_exchange.start()
    act("e1")
    back[...] = dot(stack[:, own], weights[...], TN)
    act("e2")
    normed, inverse = row_normalize(x[...].astype(F32))
    terms_exchange.wait()
    grad = back[...] + terms_got[...].astype(F32)
    sums[...] = small[...]
    sums[4:5, :] = jnp.sum(grad * normed, axis=0, keepdims=True)
    sums[5:6, :] = jnp.sum(grad, axis=0, keepdims=True)
    biases = dot(jnp.ones((8, tokens), BF16), stack[...], NT)
    sums[ROW_BQ : ROW_BQ + 1, :width] = biases[:1, :width]
    sums[ROW_BV : ROW_BV + 1, :fresh] = biases[:1, 2 * width :]
    tiny = to_twin(sums, sums_got.at[0], 2)
    tiny.start()
    act("e3")
    back[...] = row_normalize_back(grad * gain[...].astype(F32).reshape(1, -1), normed, inverse)
    tiny.wait()
    sums[:ROW_BU, :] = sums[:ROW_BU, :] + sums_got[0, :ROW_BU, :]
    sums[ROW_BU:ROW_BU_OTHER, :] = (
        sums[ROW_BU:ROW_BU_OTHER, :] + sums_got[0, ROW_BU_OTHER:ROW_BQ, :]
    )
    slot = 1
    points = iter(("e4", "e5", "e6"))
    for axis in AXES:
        copies = []
        for step in range(1, SIZE[axis]):
            _, device = place.peer(axis, step)
            copies.append(
                pltpu.make_async_remote_copy(
                    src_ref=sums, dst_ref=sums_got.at[slot], send_sem=tiny_sems.at[0, slot],
                    recv_sem=tiny_sems.at[1, slot], device_id=device, device_id_type=MESH,
                )
            )
            copies[-1].start()
            slot += 1
        act(next(points))
        for copy in copies:
            copy.wait()
        total = sums[...]
        for i in range(slot - len(copies), slot):
            total = total + sums_got[i]
        sums[...] = total
    for point in BACK_PLAN:
        if point == "e7" or point[0] == "w":
            act(point)


def attend_back(
    row_chips, split, gain, small, qt, k, kt, v, do, attended, lse, ln, x, wq, wk, wv_t, grad_wo,
    state_down, state_up, block=256,
):
    width, tokens = qt.shape
    rows, model = x.shape
    fresh = wv_t.shape[0]
    pair = 2 * HEAD_DIM
    chunk = state_down.shape[1]
    low_rows = 2 * pair
    cols = model // 2
    vmem = pl.BlockSpec(memory_space=pltpu.VMEM)
    anywhere = pl.BlockSpec(memory_space=pl.ANY)
    results = [
        ((rows, model), F32, vmem),
        ((width - fresh, tokens), F32, vmem),
        ((SUM_ROWS, model), F32, vmem),
        ((3, chunk, model), BF16, anywhere),
        ((model, 3 * chunk), BF16, anywhere),
        ((2, 2 * width, cols), BF16, anywhere),
        ((low_rows, model), BF16, anywhere),
        ((low_rows, cols), BF16, anywhere),
        ((2, low_rows, cols), BF16, anywhere),
    ]
    shapes = {i: ((chunk, model), (model, chunk)) for i in range(3)}
    shapes[3] = ((2 * width, cols),) * 2
    shapes[4] = ((low_rows, model), (low_rows, cols))
    shapes[5] = ((low_rows, cols),) * 2
    slots = scatter_slots(BACK_PLAN, shapes)
    scratch = [
        ((2 * width + fresh, tokens), BF16),
        ((2, pair, tokens), BF16),
        ((2, pair, tokens), BF16),
        ((2, tokens, pair), BF16),
        ((2, tokens, pair), BF16),
        ((2, HEAD_DIM, tokens), F32),
        ((2, HEAD_DIM, tokens), F32),
        ((2 * width + fresh, model), BF16),
        ((rows, model), BF16),
        ((rows, model), BF16),
        ((width, model), BF16),
        ((3, chunk, model), BF16),
        ((3, model, chunk), BF16),
        ((2, 2 * width, cols), BF16),
        ((low_rows, model), BF16),
        ((low_rows, cols), BF16),
        ((2, low_rows, cols), BF16),
        ((6, SUM_ROWS, model), F32),
    ]
    near = (qt, k, kt, v, do, attended, lse, ln, x)
    scratch += [(a.shape, a.dtype) for a in near]
    return pl.pallas_call(
        functools.partial(attend_back_kernel, row_chips, block, list(slots)),
        out_shape=[jax.ShapeDtypeStruct(s, t) for s, t, _ in results],
        in_specs=[pl.BlockSpec(memory_space=pltpu.SMEM), vmem, vmem] + [anywhere] * 15,
        out_specs=[spec for _, _, spec in results],
        scratch_shapes=[pltpu.VMEM(s, t) for s, t in scratch]
        + [
            pltpu.SemaphoreType.DMA((6,)),
            pltpu.SemaphoreType.DMA((13,)),
            pltpu.SemaphoreType.DMA((2, 3)),
            pltpu.SemaphoreType.DMA((2, 6)),
            pltpu.SemaphoreType.DMA((6, 2, 2, 11)),
        ]
        + [pltpu.VMEM(shape, BF16) for shape in slots.values()],
        compiler_params=pltpu.CompilerParams(
            vmem_limit_bytes=VMEM_LIMIT, collective_id=3, has_side_effects=True
        ),
        name="attend_back",
    )(
        split, gain, small, qt, k, kt, v, do, attended, lse, ln, x, wq, wk, wv_t, grad_wo,
        state_down, state_up,
    )


def finish_kernel(
    mid, back, dv, sums, down, up, wo, wo_low, low, thin, last,
    grad_input, grad_first, grad_down, grad_up, grad_wo, grad_q, grad_k, grad_v, bu,
    bias_q, bias_v, gain_two, shift_two, bias_o, bias_d, gain_one, shift_one,
):
    cols = wo.shape[2]
    pair = 2 * HEAD_DIM
    grad_input[...] = mid[...] + back[...]
    grad_first[...] = dv[...]
    grad_down[...] = down[0].astype(F32)
    grad_up[...] = up[...].astype(F32)
    for j in range(2):
        grad_wo[:, j * cols : (j + 1) * cols] = wo[j].astype(F32)
    for i, target in enumerate((grad_q, grad_k)):
        span = slice(i * pair, (i + 1) * pair)
        for j, source in enumerate((wo_low[0, span], low[span], last[0, span])):
            target[:, j * pair : (j + 1) * pair] = source.astype(F32).T
    grad_v[:pair] = wo_low[0, 2 * pair :].astype(F32)
    grad_v[pair:] = thin[...].astype(F32)

    @pl.when(pl.program_id(0) == 0)
    def _():
        chunk = bu.shape[0] // 3
        for i in range(3):
            bu[i * chunk : (i + 1) * chunk] = sums[ROW_BU + i, :chunk]
        bias_q[...] = sums[ROW_BQ, : bias_q.shape[0]]
        bias_v[...] = sums[ROW_BV, : bias_v.shape[0]]
        for i, target in enumerate((gain_two, shift_two, bias_o, bias_d, gain_one, shift_one)):
            target[...] = sums[i, :]


def finish(mid, back, dv, sums, down, up, wo, low, thin, last):
    rows, width = mid.shape
    heads = wo.shape[1] // 2
    fresh = heads // 2
    hidden = up.shape[1]
    steps = 6
    half = down.shape[1] // 2
    lanes = width // steps
    out_rows = 192
    operands = (mid, back, dv, sums, down, up, wo, wo, low, thin, last)
    fixed = lambda s: pl.BlockSpec(s, lambda i, nd=len(s): (0,) * nd)
    by_rows = lambda n, c: pl.BlockSpec((n, c), lambda i: (i, 0))
    by_lanes = lambda n: pl.BlockSpec((n, lanes), lambda i: (0, i))
    by_halves = lambda n, k: pl.BlockSpec((1, n, lanes), lambda i: (i // 3, k, lax.rem(i, 3)))
    moved = [
        by_rows(out_rows, width),
        by_rows(dv.shape[0] // steps, dv.shape[1]),
        by_rows(half, width),
        by_rows(width // steps, hidden),
        by_rows(heads // steps, width),
    ]
    specs = [
        moved[0],
        moved[0],
        moved[1],
        fixed(sums.shape),
        pl.BlockSpec((1, half, width), lambda i: (i // 2, lax.rem(i, 2), 0)),
        moved[3],
        pl.BlockSpec((2, heads // steps, wo.shape[2]), lambda i: (0, i, 0)),
        by_halves(heads, 1),
        by_lanes(low.shape[0]),
        pl.BlockSpec((HEAD_DIM, lanes), lambda i: (i // 3, lax.rem(i, 3))),
        by_halves(last.shape[1], 0),
    ]
    shapes = [(rows, width), dv.shape, (hidden, width), (width, hidden), (heads, width)]
    shapes += [(width, heads), (width, heads), (fresh, width)]
    shapes += [(hidden,), (heads,), (fresh,)] + [(width,)] * 6
    out_specs = moved + [by_rows(lanes, heads)] * 2 + [by_lanes(fresh)]
    out_specs += [fixed(s) for s in shapes[8:]]
    return pl.pallas_call(
        finish_kernel,
        grid=(steps,),
        in_specs=specs,
        out_specs=out_specs,
        out_shape=[jax.ShapeDtypeStruct(s, F32) for s in shapes],
        compiler_params=pltpu.CompilerParams(vmem_limit_bytes=VMEM_LIMIT),
        name="finish",
    )(*operands)


def swap(array):
    return lax.ppermute(array, "tensor", [(0, 1), (1, 0)])


def across_blocks(array, row_chips):
    chips = 4 * row_chips * row_chips
    shift = 2
    while shift < row_chips:
        for stride in (shift, shift * row_chips):
            pairs = [(i, i ^ stride) for i in range(chips)]
            array = array + lax.ppermute(array, "dp", pairs)
        shift *= 2
    return array


def on_device(
    row_chips,
    input_rows, first_values, doc_split, gain_norm1, bias_norm1, w_query, bias_query, w_key,
    w_value, bias_value, w_out, bias_attn_out, gain_norm2, bias_norm2, w_up, bias_up, w_down,
    bias_down, cotangent,
):
    heads = w_query.shape[1]
    fresh = w_value.shape[1]
    hidden = w_up.shape[1]
    pair = 2 * HEAD_DIM
    wv_t = w_value.T
    ln, qt, k, kt, v, vt = project(
        input_rows, first_values.T, gain_norm1, bias_norm1, w_query, bias_query, w_key, wv_t,
        bias_value,
    )
    up, down, wo, bu, vt = lax.optimization_barrier((w_up, w_down, w_out, bias_up, vt))
    up_other, down_other, wo_other, bu_other = swap(up), swap(down), swap(wo), swap(bu)
    attended, lse = attend(doc_split, qt, k, vt)
    output, grad_middle, grad_att, state_down, state_up, grad_wo, small = feed(
        row_chips, input_rows, cotangent, attended, w_out, wo_other, bias_attn_out, gain_norm2,
        bias_norm2, up_other, w_up, bu_other, bias_up, down_other, w_down, bias_down,
    )
    back, dv_first, *reduced = attend_back(
        row_chips, doc_split, gain_norm1, small, qt, k, kt, v, grad_att, attended, lse, ln,
        input_rows, w_query, w_key, wv_t, grad_wo, state_down, state_up,
    )
    reduced = [across_blocks(a, row_chips) for a in reduced]
    (
        grad_input, grad_first, grad_down, grad_up, grad_wo, grad_q, grad_k, grad_v, bias_grad_up,
        bias_grad_q, bias_grad_v, gain_two, shift_two, bias_grad_o, bias_grad_d, gain_one, shift_one,
    ) = finish(grad_middle, back, dv_first, *reduced)
    return (
        output, grad_input, grad_first.T, gain_one, shift_one, grad_q, bias_grad_q, grad_k, grad_v.T,
        bias_grad_v, grad_wo, bias_grad_o, gain_two, shift_two, grad_up, bias_grad_up, grad_down,
        bias_grad_d,
    )


def solution(mesh):
    row_chips = 1
    while 4 * row_chips * row_chips < mesh.shape["dp"]:
        row_chips += 1
    rows = P(("dp", "tensor"), None)
    cols = P(None, "tensor")
    split = P("tensor")
    firsts = P("dp", "tensor")
    wide = P("tensor", None)
    return jax.shard_map(
        functools.partial(on_device, row_chips),
        mesh=mesh,
        in_specs=(
            rows, firsts, P("dp"), P(), P(), cols, split, cols, cols, split, wide, P(), P(), P(),
            cols, split, wide, P(), rows,
        ),
        out_specs=(
            rows, rows, firsts, P(), P(), cols, split, cols, cols, split, wide, P(), P(), P(),
            cols, split, wide, P(),
        ),
        check_vma=False,
    )
```

```python
import functools

import jax
import jax.numpy as jnp
from jax import lax
from jax.experimental import pallas as pl
from jax.experimental.pallas import tpu as pltpu
from jax.sharding import PartitionSpec as P

HEAD_DIM = 64
NORM_EPS = 1e-05
GELU_ROOT = 0.7978845608028654
GELU_CUBE = 0.044715
NN = (((1,), (0,)), ((), ()))
NT = (((1,), (1,)), ((), ()))
TN = (((0,), (0,)), ((), ()))
F32 = jnp.float32
BF16 = jnp.bfloat16
VMEM_LIMIT = 60 << 20
MESH = pl.DeviceIdType.MESH


def dot(left, right, dims=NN):
    return lax.dot_general(left, right, dims, preferred_element_type=F32)


def whole(array):
    return pl.BlockSpec(array.shape, lambda *_, nd=array.ndim: (0,) * nd)


def whole_shape(shape):
    return pl.BlockSpec(shape, lambda *_, nd=len(shape): (0,) * nd)


def row_normalize(rows):
    centered = rows - jnp.mean(rows, axis=1, keepdims=True)
    inverse = lax.rsqrt(jnp.mean(centered * centered, axis=1, keepdims=True) + NORM_EPS)
    return centered * inverse, inverse


def row_normalize_back(scaled, normed, inverse):
    return inverse * (
        scaled
        - jnp.mean(scaled, axis=1, keepdims=True)
        - normed * jnp.mean(scaled * normed, axis=1, keepdims=True)
    )


AXES = ("x", "y", "z")
SIZE = {"x": 2, "y": 2, "z": 4}


class Place:
    def __init__(self, row_chips):
        index = lax.axis_index("dp")
        self.core = lax.axis_index("tensor")
        self.wide = row_chips
        self.index = index
        self.x = lax.rem(index, row_chips)
        self.y = lax.rem(index // row_chips, row_chips)
        self.z = index // (row_chips * row_chips)
        self.at = {"x": lax.rem(self.x, 2), "y": lax.rem(self.y, 2), "z": self.z}

    def peer(self, axis, step):
        size = SIZE[axis]
        spot = lax.rem(self.at[axis] + step, size)
        stride = {"x": 1, "y": self.wide, "z": self.wide * self.wide}[axis]
        return spot, (self.index + (spot - self.at[axis]) * stride, self.core)

    def twin(self):
        return (self.index, 1 - self.core)

    def across(self, step_x, step_y, other_core):
        index = self.index
        for axis, step, stride in (("x", step_x, 1), ("y", step_y, self.wide)):
            index = index + (lax.rem(self.at[axis] + step, 2) - self.at[axis]) * stride
        return (index, 1 - self.core if other_core else self.core)

    def block(self):
        places = [(0, 1), (1, 0), (1, 1)]
        return [self.across(*p, False) for p in places] + [
            self.across(*p, True) for p in [(0, 0)] + places
        ]

    def others(self):
        return self.block() + [self.peer("z", k)[1] for k in range(1, SIZE["z"])]


def greet(place):
    barrier = pltpu.get_barrier_semaphore()
    devices = place.others()
    for device in devices:
        pl.semaphore_signal(barrier, inc=1, device_id=device, device_id_type=MESH)
    return lambda: pl.semaphore_wait(barrier, len(devices))


class Sum:
    def __init__(self, place, order, held, slots, result, sems):
        self.place, self.order, self.held = place, order, held
        self.slots, self.result, self.sems = slots, result, sems
        self.rows = (held if held is not None else result).shape[0]

    def region(self, depth):
        start, size = 0, self.rows
        for axis in self.order[:depth]:
            size //= SIZE[axis]
            start = start + self.place.at[axis] * size
        return start, size

    def span(self, depth):
        start, size = self.region(depth)
        return pl.ds(pl.multiple_of(start, 16) if depth else start, size)

    def first_sem(self, gather, stage):
        count = 0
        for axis in self.order[:stage]:
            count += SIZE[axis] - 1
        return count + (5 if gather else 0)

    def scatter_copies(self, stage):
        axis = self.order[stage]
        start, size = self.region(stage)
        piece = size // SIZE[axis]
        base = self.first_sem(False, stage)
        copies = []
        for step in range(1, SIZE[axis]):
            spot, device = self.place.peer(axis, step)
            copies.append(
                pltpu.make_async_remote_copy(
                    src_ref=self.held.at[pl.ds(pl.multiple_of(start + spot * piece, 16), piece), :],
                    dst_ref=self.slots[stage].at[step - 1],
                    send_sem=self.sems.at[0, base + step - 1],
                    recv_sem=self.sems.at[1, base + step - 1],
                    device_id=device,
                    device_id_type=MESH,
                )
            )
        return copies

    def scatter_end(self, stage):
        for copy in self.scatter_copies(stage):
            copy.wait()
        span = self.span(stage + 1)
        total = self.held[span, :].astype(F32)
        for step in range(SIZE[self.order[stage]] - 1):
            total = total + self.slots[stage][step].astype(F32)
        self.held[span, :] = total.astype(BF16)

    def gather_copies(self, stage, source):
        axis = self.order[stage]
        span = self.span(stage + 1)
        base = self.first_sem(True, stage)
        copies = []
        origin = self.result.at[span, :] if source is None else source
        for step in range(1, SIZE[axis]):
            _, device = self.place.peer(axis, step)
            copies.append(
                pltpu.make_async_remote_copy(
                    src_ref=origin,
                    dst_ref=self.result.at[span, :],
                    send_sem=self.sems.at[0, base + step - 1],
                    recv_sem=self.sems.at[1, base + step - 1],
                    device_id=device,
                    device_id_type=MESH,
                )
            )
        if source is not None:
            copies.append(
                pltpu.make_async_copy(source, self.result.at[span, :], self.sems.at[0, 10])
            )
        return copies

    def run(self, action, source=None):
        verb, letter = action
        gather = letter in "cba"
        stage = "abc".index(letter) if gather else "ABC".index(letter)
        if gather:
            for copy in self.gather_copies(stage, source):
                copy.start() if verb == "s" else copy.wait()
        elif verb == "s":
            for copy in self.scatter_copies(stage):
                copy.start()
        else:
            self.scatter_end(stage)


def slot_shapes(order, rows, cols):
    shapes = []
    for axis in order:
        rows //= SIZE[axis]
        shapes.append((SIZE[axis] - 1, rows, cols))
    return shapes


ORDERS = ("xyz", "yxz")
FEED_PLAN = {
    "s1m": ((0, "sA"),),
    "s3q": ((0, "fA"), (0, "sB"),),
    "s3m": ((1, "sA"),),
    "s3e": ((0, "fB"), (0, "sC"),),
    "s5q": ((1, "fA"), (1, "sB"),),
    "s5m": ((0, "fC"), (0, "sc"), (2, "sA"),),
    "s5e": ((1, "fB"),),
    "f_end": ((0, "fc"), (2, "fA"),),
}
BACK_PLAN = {
    "start": ((1, "sC"), (0, "sb"), (2, "sB"),),
    (0, 2): ((0, "fb"), (0, "sa"),),
    (0, 4): ((1, "fC"), (2, "fB"), (1, "sc"), (2, "sC"),),
    (0, 7): ((0, "fa"), (3, "sA"),),
    (1, 0): ((1, "fc"), (1, "sb"),),
    (1, 5): ((3, "fA"), (2, "fC"), (2, "sc"), (3, "sB"),),
    (1, 6): ((1, "fb"), (1, "sa"),),
    (1, 7): ((3, "fB"), (3, "sC"), (4, "sA"),),
    (2, 1): ((2, "fc"), (2, "sb"),),
    (2, 4): ((1, "fa"),),
    (2, 5): ((3, "fC"), (3, "sc"),),
    (2, 6): ((4, "fA"), (4, "sB"),),
    (2, 7): ((2, "fb"), (4, "fB"), (2, "sa"), (4, "sC"), (5, "sA"),),
    "e0": ((3, "fc"), (3, "sb"),),
    "e2": ((4, "fC"), (4, "sc"),),
    "e3": ((2, "fa"),),
    "e4": ((4, "fc"), (5, "fA"), (5, "sB"), (4, "sb"),),
    "e5": ((3, "fb"), (3, "sa"),),
    "e6": ((5, "fB"), (4, "fb"), (5, "sC"), (4, "sa"),),
    "w0": ((5, "fC"), (5, "sc"),),
    "w1": ((3, "fa"),),
    "w2": ((5, "fc"), (5, "sb"),),
    "w3": ((4, "fa"),),
    "w4": ((5, "fb"), (5, "sa"),),
    "w5": ((5, "fa"),),
}


def started(plan):
    return [(i, action[1]) for actions in plan.values() for i, action in actions if action[0] == "s"]


def progress(batch):
    return sum(1 for i, _ in started(FEED_PLAN) if i == batch)


def unfinished():
    return [i for i in range(3) if progress(i) < 3]


def scatter_slots(plan, shapes):
    slots = {}
    for i, letter in started(plan):
        if letter in "ABC":
            for j, order in enumerate(ORDERS):
                shape = slot_shapes(order, *shapes[i][j])["ABC".index(letter)]
                slots[i, j, letter] = shape
    return slots


def project_kernel(
    block, x, first_t, gain, bias, wq, bq, wk, wv_t, bv, ln, qt, k, kt, v, vt,
    x_other, weights, s_ln, s_qt, s_k, s_kt, s_v, s_vt, pair_sems, out_sems,
):
    rows = x.shape[0]
    heads, fresh = wq.shape[1], wv_t.shape[0]
    core = lax.axis_index("tensor")
    twin = (lax.axis_index("dp"), 1 - core)
    barrier = pltpu.get_barrier_semaphore()
    pl.semaphore_signal(barrier, inc=1, device_id=twin, device_id_type=MESH)
    weights[:, :heads] = wq[...]
    weights[:, heads : 2 * heads] = wk[...]
    weights[:, 2 * heads :] = wv_t[...].T
    pl.semaphore_wait(barrier, 1)
    send = pltpu.make_async_remote_copy(
        src_ref=x, dst_ref=x_other, send_sem=pair_sems.at[0], recv_sem=pair_sems.at[1],
        device_id=twin, device_id_type=MESH,
    )
    send.start()
    gain_row = gain[...].astype(F32).reshape(1, -1)
    bias_row = bias[...].astype(F32).reshape(1, -1)
    bq_row = bq[...].astype(F32).reshape(1, -1)
    bv_row = bv[...].astype(F32).reshape(1, -1)
    copies = []
    for part, source in enumerate((x, x_other)):
        if part:
            send.wait_recv()
        spot = pl.multiple_of((core if part == 0 else 1 - core) * rows, rows)
        for first in range(0, rows, block):
            span = pl.ds(first, block)
            normed, _ = row_normalize(source[span, :].astype(F32))
            low = (normed * gain_row + bias_row).astype(BF16)
            s_ln[part, span] = low
            product = dot(low, weights[...])
            queries = (product[:, :heads] + bq_row).astype(BF16).astype(F32) * HEAD_DIM ** (-0.5)
            s_qt[part, :, span] = queries.astype(BF16).T
            keys = product[:, heads : 2 * heads].astype(BF16)
            s_k[part, span] = keys
            s_kt[part, :, span] = keys.T
            values = (product[:, 2 * heads :] + bv_row).astype(BF16)
            reused = first_t[:, pl.ds(pl.multiple_of(spot + first, block), block)]
            s_vt[part, :fresh, span] = values.T
            s_vt[part, fresh:, span] = reused
            s_v[part, span] = jnp.concatenate([values, reused.T], axis=1)
        targets = (
            (s_ln, ln.at[pl.ds(spot, rows), :]),
            (s_qt, qt.at[:, pl.ds(spot, rows)]),
            (s_k, k.at[pl.ds(spot, rows), :]),
            (s_kt, kt.at[:, pl.ds(spot, rows)]),
            (s_v, v.at[pl.ds(spot, rows), :]),
            (s_vt, vt.at[:, pl.ds(spot, rows)]),
        )
        for i, (held, target) in enumerate(targets):
            copy = pltpu.make_async_copy(held.at[part], target, out_sems.at[part, i])
            copy.start()
            copies.append(copy)
    send.wait_send()
    for copy in copies:
        copy.wait()


def project(x, first_t, gain, bias, wq, bq, wk, wv_t, bv, block=256):
    rows, width = x.shape
    heads = wq.shape[1]
    tall, flat = (rows, heads), (heads, rows)
    vmem = pl.BlockSpec(memory_space=pltpu.VMEM)
    shapes = ((2 * rows, width), (heads, 2 * rows), (2 * rows, heads)) + (
        (heads, 2 * rows), (2 * rows, heads), (heads, 2 * rows),
    )
    scratch = [(rows, width), (width, 2 * heads + wv_t.shape[0])]
    scratch += [(2,) + s for s in ((rows, width), flat, tall, flat, tall, flat)]
    return pl.pallas_call(
        functools.partial(project_kernel, block),
        out_shape=[jax.ShapeDtypeStruct(s, BF16) for s in shapes],
        in_specs=[vmem] * 9,
        out_specs=[pl.BlockSpec(memory_space=pl.ANY)] * 6,
        scratch_shapes=[pltpu.VMEM(s, BF16) for s in scratch]
        + [pltpu.SemaphoreType.DMA((2,)), pltpu.SemaphoreType.DMA((2, 6))],
        compiler_params=pltpu.CompilerParams(
            vmem_limit_bytes=VMEM_LIMIT, collective_id=1, has_side_effects=True
        ),
        name="project",
    )(x, first_t, gain, bias, wq, bq, wk, wv_t, bv)


def causal(size):
    keys = lax.broadcasted_iota(jnp.int32, (size, size), 0)
    return keys <= lax.broadcasted_iota(jnp.int32, (size, size), 1)


def attend_kernel(block, ahead, split, qt, k, vt, attended, lse, sums, k_aug, q_aug):
    width, tokens = qt.shape
    half = tokens // 2
    pair_width = 2 * HEAD_DIM
    far = jnp.where(split[0] < tokens, -1e9, 0.0)
    row = lax.broadcasted_iota(jnp.int32, (HEAD_DIM, tokens), 0)
    token = lax.broadcasted_iota(jnp.int32, (HEAD_DIM, tokens), 1)
    far_rows = jnp.where((row == 0) & (token >= half), far, 0.0).astype(BF16)
    lane = lax.broadcasted_iota(jnp.int32, (tokens, pair_width), 1)
    key = lax.broadcasted_iota(jnp.int32, (tokens, pair_width), 0)
    first_half = jnp.where((lax.rem(lane, HEAD_DIM) == 0) & (key < half), 1.0, 0.0).astype(BF16)
    ones = (lax.broadcasted_iota(jnp.int32, (16, tokens), 0) == 0).astype(BF16)
    for j in range(2):
        sums[j, HEAD_DIM:, :] = ones
        extra = HEAD_DIM * (1 - j)
        q_aug[j, extra : extra + HEAD_DIM, :] = far_rows

    def pair_step(pair, _):
        col = pl.multiple_of(pair * pair_width, pair_width)
        head_rows = [pl.ds(pl.multiple_of(col + HEAD_DIM * j, HEAD_DIM), HEAD_DIM) for j in range(2)]
        keys = k[:, pl.ds(col, pair_width)]
        for j in range(2):
            base = HEAD_DIM * j
            sums[j, :HEAD_DIM, :] = vt[head_rows[j], :]
            k_aug[j] = jnp.where(lane // HEAD_DIM == j, keys, first_half)
            q_aug[j, base : base + HEAD_DIM, :] = qt[head_rows[j], :]

        def products(number, j):
            start, stop = number * block, (number + 1) * block
            return dot(k_aug[j, :stop, :], q_aug[j, :, start:stop])

        def average(number, j, scores):
            start, stop = number * block, (number + 1) * block
            edge = jnp.where(causal(block), scores[start:], -1e30)
            top = jnp.max(edge, axis=0, keepdims=True)
            if start:
                near = scores[:start]
                top = jnp.maximum(top, jnp.max(near, axis=0, keepdims=True))
                weights = jnp.concatenate(
                    [jnp.exp(near - top).astype(BF16), jnp.exp(edge - top).astype(BF16)], axis=0
                )
            else:
                weights = jnp.exp(edge - top).astype(BF16)
            total = dot(sums[j, :, :stop], weights)
            denominator = total[HEAD_DIM : HEAD_DIM + 1]
            attended[head_rows[j], start:stop] = (total[:HEAD_DIM] * (1.0 / denominator)).astype(BF16)
            lse[pl.ds(pair * 2 + j, 1), :, start:stop] = (top + jnp.log(denominator))[None]

        units = [(number, j) for number in range(tokens // block) for j in range(2)]
        queue = [products(*unit) for unit in units[:ahead]]
        for i, unit in enumerate(units):
            if i + ahead < len(units):
                queue.append(products(*units[i + ahead]))
            average(*unit, queue.pop(0))
        return 0

    lax.fori_loop(0, width // pair_width, pair_step, 0)


def attend(split, qt, k, vt, block=256, ahead=4):
    width, tokens = qt.shape
    pair_width = 2 * HEAD_DIM
    vmem = pl.BlockSpec(memory_space=pltpu.VMEM)
    return pl.pallas_call(
        functools.partial(attend_kernel, block, ahead),
        out_shape=(
            jax.ShapeDtypeStruct((width, tokens), BF16),
            jax.ShapeDtypeStruct((width // HEAD_DIM, 1, tokens), F32),
        ),
        in_specs=[pl.BlockSpec(memory_space=pltpu.SMEM), vmem, vmem, vmem],
        out_specs=(vmem, vmem),
        scratch_shapes=[
            pltpu.VMEM((2, HEAD_DIM + 16, tokens), BF16),
            pltpu.VMEM((2, tokens, pair_width), BF16),
            pltpu.VMEM((2, pair_width, tokens), BF16),
        ],
        compiler_params=pltpu.CompilerParams(vmem_limit_bytes=VMEM_LIMIT),
        name="attend",
    )(split, qt, k, vt)


def gelu_both(v):
    square = v * v
    tanh = jnp.tanh(v * (GELU_ROOT + (GELU_ROOT * GELU_CUBE) * square))
    half = 0.5 * v
    slope = 0.5 + 0.5 * tanh + half * (1.0 - tanh * tanh) * (
        GELU_ROOT + (3.0 * GELU_ROOT * GELU_CUBE) * square
    )
    return half + half * tanh, slope


SUM_ROWS = 16
ROW_BU, ROW_BU_OTHER, ROW_BQ, ROW_BV = 6, 9, 12, 13


def feed_kernel(
    row_chips, slot_keys, x_far, cot_far, attended, wo_own_far, wo_other_far, bias_o, gain, bias,
    up_other, up_own, bu_other, bu_own, down_other, down_own, bias_d,
    out, grad_mid, grad_att, state_down, state_up, grad_wo, small,
    att_own, att_other, ln, ln_t, normed, inverse, total, grad_ln, att_stage, stage_down, stage_up,
    held_down, held_up, x, cot, wo_own, wo_other, kept_act, kept_grad,
    move_sems, load_sems, pair_sems, sum_sems, *slot_refs,
):
    state, stage, held = (state_down, state_up), (stage_down, stage_up), (held_down, held_up)
    slots = dict(zip(slot_keys, slot_refs))
    step = pl.program_id(0)
    place = Place(row_chips)
    core = place.core
    rows = x.shape[0]
    heads = att_own.shape[0]
    chunk = up_own.shape[1]
    index = step // 2
    own = pl.ds(pl.multiple_of(core * rows, rows), rows)
    theirs = pl.ds(pl.multiple_of((1 - core) * rows, rows), rows)

    def to_twin(source, target, i):
        return pltpu.make_async_remote_copy(
            src_ref=source, dst_ref=target, send_sem=pair_sems.at[0, i],
            recv_sem=pair_sems.at[1, i], device_id=place.twin(), device_id_type=MESH,
        )

    def stage_copies(i):
        return [to_twin(stage[j].at[i], held[j].at[i], 2 + 2 * i + j) for j in range(2)]

    def part(i, j):
        return Sum(
            place, ORDERS[j], held[j].at[i], [slots.get((i, j, letter)) for letter in "ABC"],
            state[j].at[i], sum_sems.at[i, j],
        )

    def act(point):
        for i, action in FEED_PLAN.get(point, ()):
            for j in range(2):
                one = part(i, j)
                one.run(action, one.held.at[one.span(3), :] if action[1] == "c" else None)

    def act_at(name, odd):
        for k in range(odd, 6, 2):
            point = "s%d%s" % (k, name)
            if point in FEED_PLAN:
                pl.when(step == k)(functools.partial(act, point))

    @pl.when(step == 0)
    def _():
        ready = greet(place)
        loads = [
            pltpu.make_async_copy(source, target, load_sems.at[i])
            for i, (source, target) in enumerate(
                (
                    (attended.at[:, own], att_own), (wo_own_far, wo_own), (x_far, x),
                    (wo_other_far, wo_other), (cot_far, cot),
                )
            )
        ]
        for load in loads:
            load.start()
        ready()
        exchange = to_twin(attended.at[:, theirs], att_other, 0)
        exchange.start()
        grad_ln[...] = jnp.zeros_like(grad_ln)
        small[...] = jnp.zeros_like(small)
        for load in loads:
            load.wait()
        total[...] = x[...].astype(F32) + (
            dot(att_own[...], wo_own[...], TN) + bias_o[...].astype(F32).reshape(1, -1)
        )
        exchange.wait()
        mid = total[...] + dot(att_other[...], wo_other[...], TN)
        total[...] = mid + bias_d[...].astype(F32).reshape(1, -1)
        norm, inv = row_normalize(mid)
        normed[...] = norm
        inverse[...] = jnp.broadcast_to(inv, inverse.shape)
        low = (
            norm * gain[...].astype(F32).reshape(1, -1) + bias[...].astype(F32).reshape(1, -1)
        ).astype(BF16)
        ln[...] = low
        ln_t[...] = low.T

    def weight_grads(up, bias_up, down, odd):
        hidden = dot(ln[...], up[...]) + bias_up[
            pl.ds(pl.multiple_of(index * chunk, chunk), chunk)
        ].astype(F32).reshape(1, -1)
        activated, slope = gelu_both(hidden)
        activated = activated.astype(BF16)
        grad_hidden = (dot(cot[...], down[...], NT) * slope).astype(BF16)
        act_at("q", odd)
        grad_down = dot(activated, cot[...], TN)
        grad_up = dot(ln_t[...], grad_hidden)
        sums = jnp.sum(grad_hidden.astype(F32), axis=0, keepdims=True)
        return activated, grad_hidden, grad_down, grad_up, sums

    @pl.when(lax.rem(step, 2) == 0)
    def _():
        activated, grad_hidden, grad_down, grad_up, sums = weight_grads(
            up_other, bu_other, down_other, 0
        )
        stage_down[index] = grad_down.astype(BF16)
        stage_up[index] = grad_up.astype(BF16)
        for copy in stage_copies(index):
            copy.start()
        small[pl.ds(ROW_BU_OTHER + index, 1), :chunk] = sums
        kept_act[...] = activated
        kept_grad[...] = grad_hidden
        act_at("m", 0)

    @pl.when(lax.rem(step, 2) == 1)
    def _():
        activated, grad_hidden, grad_down, grad_up, sums = weight_grads(up_own, bu_own, down_own, 1)
        for copy in stage_copies(index):
            copy.wait()
        held_down[index] = (grad_down + held_down[index].astype(F32)).astype(BF16)
        held_up[index] = (grad_up + held_up[index].astype(F32)).astype(BF16)
        small[pl.ds(ROW_BU + index, 1), :chunk] = sums

        act_at("m", 1)
        total[...] += dot(kept_act[...], down_other[...]) + dot(activated, down_own[...])
        grad_ln[...] += dot(kept_grad[...], up_other[...], NT) + dot(grad_hidden, up_own[...], NT)
        act_at("e", 1)

    @pl.when(step == 5)
    def _():
        grad = grad_ln[...]
        norm = normed[...]
        cot32 = cot[...].astype(F32)
        scaled = grad * gain[...].astype(F32).reshape(1, -1)
        mid = cot32 + row_normalize_back(scaled, norm, inverse[:, :1])
        grad_mid[...] = mid
        low = mid.astype(BF16)
        att_stage[1] = dot(wo_other[...], low, NT).astype(BF16)
        exchange = to_twin(att_stage.at[1], grad_att.at[:, own], 1)
        exchange.start()
        att_stage[0] = dot(wo_own[...], low, NT).astype(BF16)
        local = pltpu.make_async_copy(att_stage.at[0], grad_att.at[:, own], move_sems.at[0])
        local.start()
        out[...] = total[...].astype(BF16)
        small[0:1, :] = jnp.sum(grad * norm, axis=0, keepdims=True)
        small[1:2, :] = jnp.sum(grad, axis=0, keepdims=True)
        small[2:3, :] = jnp.sum(low.astype(F32), axis=0, keepdims=True)
        small[3:4, :] = jnp.sum(cot32, axis=0, keepdims=True)
        grad_wo[:heads] = dot(att_own[...], low).astype(BF16)
        grad_wo[heads:] = dot(att_other[...], low).astype(BF16)
        act("f_end")
        moves = [local]
        for i in range(3):
            if progress(i) > 3:
                continue
            for j in range(2):
                span = part(i, j).span(progress(i))
                move = pltpu.make_async_copy(
                    held[j].at[i, span, :], state[j].at[i, span, :], move_sems.at[1 + 2 * i + j]
                )
                move.start()
                moves.append(move)
        exchange.wait()
        for move in moves:
            move.wait()


def feed(
    row_chips, x, cot, attended, wo_own, wo_other, bias_o, gain, bias,
    up_other, up_own, bu_other, bu_own, down_other, down_own, bias_d,
):
    rows, width = x.shape
    hidden = up_own.shape[1]
    heads = wo_own.shape[0]
    chunk = hidden // 3
    once = pl.Buffered(1)
    fixed = lambda s: pl.BlockSpec(s, lambda j, nd=len(s): (0,) * nd, pipeline_mode=once)
    anywhere = pl.BlockSpec(memory_space=pl.ANY)
    up_spec = pl.BlockSpec((width, chunk), lambda j: (0, j // 2))
    down_spec = pl.BlockSpec((chunk, width), lambda j: (j // 2, 0))
    operands = (
        x, cot, attended, wo_own, wo_other, bias_o, gain, bias,
        up_other, up_own, bu_other, bu_own, down_other, down_own, bias_d,
    )
    specs = [fixed(a.shape) for a in operands]
    for i in range(5):
        specs[i] = anywhere
    specs[8] = specs[9] = up_spec
    specs[12] = specs[13] = down_spec
    results = [
        ((rows, width), BF16),
        ((rows, width), F32),
        ((heads, 2 * rows), BF16),
        ((3, chunk, width), BF16),
        ((3, width, chunk), BF16),
        ((2 * heads, width), BF16),
        ((SUM_ROWS, width), F32),
    ]
    out_specs = [fixed(s) for s, _ in results]
    out_specs[2] = out_specs[3] = out_specs[4] = anywhere
    slots = scatter_slots(FEED_PLAN, {i: ((chunk, width), (width, chunk)) for i in range(3)})
    return pl.pallas_call(
        functools.partial(feed_kernel, row_chips, list(slots)),
        grid=(6,),
        in_specs=specs,
        out_specs=out_specs,
        out_shape=[jax.ShapeDtypeStruct(s, t) for s, t in results],
        scratch_shapes=[
            pltpu.VMEM((heads, rows), BF16),
            pltpu.VMEM((heads, rows), BF16),
            pltpu.VMEM((rows, width), BF16),
            pltpu.VMEM((width, rows), BF16),
            pltpu.VMEM((rows, width), F32),
            pltpu.VMEM((rows, 128), F32),
            pltpu.VMEM((rows, width), F32),
            pltpu.VMEM((rows, width), F32),
            pltpu.VMEM((2, heads, rows), BF16),
            pltpu.VMEM((3, chunk, width), BF16),
            pltpu.VMEM((3, width, chunk), BF16),
            pltpu.VMEM((3, chunk, width), BF16),
            pltpu.VMEM((3, width, chunk), BF16),
            pltpu.VMEM((rows, width), BF16),
            pltpu.VMEM((rows, width), BF16),
            pltpu.VMEM((heads, width), BF16),
            pltpu.VMEM((heads, width), BF16),
            pltpu.VMEM((rows, chunk), BF16),
            pltpu.VMEM((rows, chunk), BF16),
            pltpu.SemaphoreType.DMA((7,)),
            pltpu.SemaphoreType.DMA((5,)),
            pltpu.SemaphoreType.DMA((2, 8)),
            pltpu.SemaphoreType.DMA((3, 2, 2, 11)),
        ]
        + [pltpu.VMEM(shape, BF16) for shape in slots.values()],
        compiler_params=pltpu.CompilerParams(
            vmem_limit_bytes=VMEM_LIMIT, collective_id=2, has_side_effects=True,
            dimension_semantics=("arbitrary",),
        ),
        name="feed",
    )(*operands)


def extra_rows(row, fourth):
    high = row.astype(BF16).astype(F32)
    middle = (row - high).astype(BF16).astype(F32)
    low = row - high - middle
    index = lax.broadcasted_iota(jnp.int32, (HEAD_DIM, row.shape[1]), 0)
    rest = jnp.where(index == 2, low, jnp.where(index == 3, fourth, 0.0))
    return jnp.where(index == 0, high, jnp.where(index == 1, middle, rest)).astype(BF16)


def attend_back_kernel(
    row_chips, block, slot_keys, split, gain, small, qt_far, k_far, kt_far, v_far, do_far, attended_far, lse_far,
    ln_far, x_far, wq_far, wk_far, wv_far, grad_wo_far, state_down, state_up,
    back, dv_first, sums, red_down, red_up, red_wo, red_low, red_v, red_last,
    stack, q_aug, d_aug, k_aug, v_aug, dk_sum, dv_sum, weights, terms_send, terms_got,
    wo_got, held_down, held_up, held_wo, held_low, held_v, held_last, sums_got,
    qt, k, kt, v, do, attended, lse, ln, x,
    move_sems, load_sems, pair_sems, tiny_sems, sum_sems, *slot_refs,
):
    state, held = (state_down, state_up), (held_down, held_up)
    slots = dict(zip(slot_keys, slot_refs))
    live = unfinished()
    done = [i for i in range(3) if i not in live]
    packed = dict(zip([(i, j) for i in done for j in range(2)], slot_refs[len(slot_keys) :]))
    width, tokens = qt.shape
    half = tokens // 2
    fresh, model = wv_far.shape
    place = Place(row_chips)
    core = place.core
    pair_width = 2 * HEAD_DIM
    own = pl.ds(pl.multiple_of(core * half, half), half)
    theirs = pl.ds(pl.multiple_of((1 - core) * half, half), half)

    def to_twin(source, target, i):
        return pltpu.make_async_remote_copy(
            src_ref=source, dst_ref=target, send_sem=pair_sems.at[0, i],
            recv_sem=pair_sems.at[1, i], device_id=place.twin(), device_id_type=MESH,
        )

    def part(i, j):
        chunk = state_down.shape[1]
        if i < 3:
            holder = held[j].at[live.index(i)] if i in live else None
            result = red_up.at[:, i * chunk : (i + 1) * chunk] if j else red_down.at[i]
        else:
            holder, result = {
                3: (held_wo.at[j], red_wo.at[j]),
                4: ((held_low, red_low), (held_v, red_v))[j],
                5: (held_last.at[j], red_last.at[j]),
            }[i]
        return Sum(
            place, ORDERS[j], holder, [slots.get((i, j, letter)) for letter in "ABC"], result,
            sum_sems.at[i, j],
        )

    def act(point):
        for i, action in BACK_PLAN.get(point, ()):
            for j in range(2):
                one = part(i, j)
                source = None
                if action[1] == "cb"[progress(i) - 3] if i in done else action[1] == "c":
                    source = packed[i, j] if i in done else one.held.at[one.span(3), :]
                one.run(action, source)

    loads = []
    for i in range(3):
        for j in range(2):
            span = part(i, j).span(progress(i) if i in live else 6 - progress(i))
            target = part(i, j).held.at[span, :] if i in live else packed[i, j]
            loads.append(
                pltpu.make_async_copy(state[j].at[i, span, :], target, move_sems.at[2 * i + j])
            )
    ready = greet(place)
    for load in loads:
        load.start()
    arriving = [
        pltpu.make_async_copy(far, near, load_sems.at[i])
        for i, (far, near) in enumerate(
            (
                (k_far, k), (qt_far, qt), (v_far, v), (do_far, do), (attended_far, attended),
                (lse_far, lse), (kt_far, kt), (wq_far, terms_send.at[:model, :width]),
                (wk_far, terms_send.at[:model, width:]), (wv_far, weights.at[2 * width :, :]), (ln_far, ln),
                (x_far, x),
            )
        )
    ]
    for copy in arriving:
        copy.start()
    ready()
    wo_exchange = to_twin(grad_wo_far.at[width:, :], wo_got, 0)
    wo_exchange.start()
    for load in loads:
        load.wait()
    act("start")
    for copy in arriving:
        copy.wait()
    weights[:width] = terms_send[:model, :width].T
    weights[width : 2 * width] = terms_send[:model, width:].T
    grad_wo = terms_send.at[:width, :]
    wo_load = pltpu.make_async_copy(grad_wo_far.at[:width, :], grad_wo, load_sems.at[12])
    wo_load.start()
    far = jnp.where(split[0] < tokens, -1e9, 0.0)
    token = lax.broadcasted_iota(jnp.int32, (1, tokens), 1)
    far_row = jnp.where(token >= half, far, 0.0)

    def weight_rows(rows):
        return dot(stack[rows, :], ln[...]).astype(BF16)

    def bias_sums(target, lanes, rows):
        sums[target : target + 1, lanes] = dot(jnp.ones((8, tokens), BF16), stack[rows, :], NT)[:1]

    def by_columns(target, start, values):
        cols = target.shape[2]
        for j in range(2):
            target[j, start : start + values.shape[0], :] = values[:, j * cols : (j + 1) * cols]

    def pair_step(pair, _):
        col = pl.multiple_of(pair * pair_width, pair_width)
        lane = lax.broadcasted_iota(jnp.int32, (tokens, pair_width), 1)
        key = lax.broadcasted_iota(jnp.int32, (tokens, pair_width), 0)
        within = lax.rem(lane, HEAD_DIM)
        ones = jnp.where((within < 3) | ((within == 3) & (key < half)), 1.0, 0.0).astype(BF16)
        keys = k[:, pl.ds(col, pair_width)]
        values = v[:, pl.ds(col, pair_width)]
        dk_sum[...] = jnp.zeros_like(dk_sum)
        dv_sum[...] = jnp.zeros_like(dv_sum)
        head_rows = [pl.ds(pl.multiple_of(col + HEAD_DIM * j, HEAD_DIM), HEAD_DIM) for j in range(2)]
        for j in range(2):
            mine = lane // HEAD_DIM == j
            k_aug[j] = jnp.where(mine, keys, ones)
            v_aug[j] = jnp.where(mine, values, ones)
            grad = do[head_rows[j], :]
            inner = jnp.sum(
                grad.astype(F32) * attended[head_rows[j], :].astype(F32), axis=0, keepdims=True
            )
            base, extra = HEAD_DIM * j, HEAD_DIM * (1 - j)
            q_aug[j, base : base + HEAD_DIM, :] = qt[head_rows[j], :]
            q_aug[j, extra : extra + HEAD_DIM, :] = extra_rows(
                -lse[pl.ds(pair * 2 + j, 1)][0], far_row
            )
            d_aug[j, base : base + HEAD_DIM, :] = grad
            d_aug[j, extra : extra + HEAD_DIM, :] = extra_rows(-inner, 0.0)

        def products(number, j):
            start, stop = number * block, (number + 1) * block
            return (
                dot(k_aug[j, :stop, :], q_aug[j, :, start:stop]),
                dot(v_aug[j, :stop, :], d_aug[j, :, start:stop]),
            )

        def gradients(number, j, scores, grad_probs):
            start, stop = number * block, (number + 1) * block
            probs = jnp.where(causal(block), jnp.exp(scores[start:]), 0.0)
            if start:
                probs = jnp.concatenate([jnp.exp(scores[:start]), probs], axis=0)
            grad_scores = (probs * grad_probs).astype(BF16)
            probs = probs.astype(BF16)
            rows = head_rows[j]
            stack[rows, start:stop] = (
                dot(kt[rows, :stop], grad_scores) * HEAD_DIM ** (-0.5)
            ).astype(BF16)
            dv_sum[j, :, :stop] += dot(do[rows, start:stop], probs, NT)
            dk_sum[j, :, :stop] += dot(qt[rows, start:stop], grad_scores, NT)

        units = [(number, j) for number in range(tokens // block) for j in range(2)]
        ahead = products(*units[0])
        for i, unit in enumerate(units):
            now = ahead
            if i + 1 < len(units):
                ahead = products(*units[i + 1])
            gradients(*unit, *now)
            if unit[1] and i + 1 < len(units):
                for p in range(width // pair_width):
                    if (p, unit[0]) in BACK_PLAN:
                        pl.when(pair == p)(functools.partial(act, (p, unit[0])))

        for j in range(2):
            stack[pl.ds(pl.multiple_of(width + col + HEAD_DIM * j, HEAD_DIM), HEAD_DIM), :] = dk_sum[
                j
            ].astype(BF16)

        @pl.when(pair == 0)
        def _():
            stack[2 * width : 2 * width + HEAD_DIM, :] = dv_sum[0].astype(BF16)
            stack[2 * width + HEAD_DIM : 2 * width + 2 * HEAD_DIM, :] = dv_sum[1].astype(BF16)
            sums[...] = small[...]
            bias_sums(ROW_BQ, slice(0, pair_width), slice(0, pair_width))
            bias_sums(ROW_BV, slice(0, pair_width), slice(2 * width, 2 * width + pair_width))
            wo_exchange.wait()
            wo_load.wait()
            summed = (grad_wo[...].astype(F32) + wo_got[...].astype(F32)).astype(BF16)
            by_columns(held_wo, 0, summed)
            for i in range(3):
                by_columns(
                    held_wo,
                    width + i * pair_width,
                    weight_rows(slice(i * width, i * width + pair_width)),
                )
            act((0, tokens // block - 1))

        @pl.when(pair == 1)
        def _():
            stack[2 * width + 2 * HEAD_DIM :, :] = dv_sum[0].astype(BF16)
            dv_first[:HEAD_DIM, :] = dv_sum[1]
            bias_sums(
                ROW_BQ, slice(pair_width, 2 * pair_width), slice(pair_width, 2 * pair_width)
            )
            bias_sums(
                ROW_BV, slice(pair_width, pair_width + HEAD_DIM),
                slice(2 * width + pair_width, 2 * width + pair_width + HEAD_DIM),
            )
            for i in range(2):
                held_low[i * pair_width : (i + 1) * pair_width] = weight_rows(
                    slice(i * width + pair_width, i * width + 2 * pair_width)
                )
            rest = weight_rows(slice(2 * width + 2 * HEAD_DIM, 2 * width + 3 * HEAD_DIM))
            cols = held_v.shape[1]
            held_v[...] = jnp.zeros_like(held_v)
            for j in range(2):
                held_v[HEAD_DIM * j : HEAD_DIM * (j + 1), :] = rest[:, j * cols : (j + 1) * cols]
            act((1, tokens // block - 1))

        @pl.when(pair == 2)
        def _():
            dv_first[HEAD_DIM : 2 * HEAD_DIM, :] = dv_sum[0]
            dv_first[2 * HEAD_DIM :, :] = dv_sum[1]
            bias_sums(
                ROW_BQ, slice(2 * pair_width, 3 * pair_width),
                slice(2 * pair_width, 3 * pair_width),
            )
            for i in range(2):
                by_columns(
                    held_last,
                    i * pair_width,
                    weight_rows(slice(i * width + 2 * pair_width, i * width + 3 * pair_width)),
                )
            act((2, tokens // block - 1))

        return 0

    lax.fori_loop(0, width // pair_width, pair_step, 0)

    act("e0")
    terms_send[...] = dot(stack[:, theirs], weights[...], TN).astype(BF16)
    terms_exchange = to_twin(terms_send, terms_got, 1)
    terms_exchange.start()
    act("e1")
    back[...] = dot(stack[:, own], weights[...], TN)
    act("e2")
    normed, inverse = row_normalize(x[...].astype(F32))
    terms_exchange.wait()
    grad = back[...] + terms_got[...].astype(F32)
    sums[4:5, :] = jnp.sum(grad * normed, axis=0, keepdims=True)
    sums[5:6, :] = jnp.sum(grad, axis=0, keepdims=True)

    def spread(devices, first):
        return [
            pltpu.make_async_remote_copy(
                src_ref=sums, dst_ref=sums_got.at[first + i], send_sem=tiny_sems.at[0, first + i],
                recv_sem=tiny_sems.at[1, first + i], device_id=device, device_id_type=MESH,
            )
            for i, device in enumerate(devices)
        ]

    copies = spread(place.block(), 0)
    for copy in copies:
        copy.start()
    act("e3")
    back[...] = row_normalize_back(grad * gain[...].astype(F32).reshape(1, -1), normed, inverse)
    act("e4")
    for copy in copies:
        copy.wait()
    total = sums[...]
    for i in range(3):
        total = total + sums_got[i]
    sums[...] = total
    for i in range(3, 7):
        sums[:ROW_BU, :] = sums[:ROW_BU, :] + sums_got[i, :ROW_BU, :]
        sums[ROW_BU:ROW_BU_OTHER, :] = (
            sums[ROW_BU:ROW_BU_OTHER, :] + sums_got[i, ROW_BU_OTHER:ROW_BQ, :]
        )
    copies = spread([place.peer("z", step)[1] for step in range(1, SIZE["z"])], 7)
    for copy in copies:
        copy.start()
    act("e5")
    for copy in copies:
        copy.wait()
    sums[...] = sums[...] + sums_got[7] + sums_got[8] + sums_got[9]
    for point in BACK_PLAN:
        if point == "e6" or point[0] == "w":
            act(point)


def attend_back(
    row_chips, split, gain, small, qt, k, kt, v, do, attended, lse, ln, x, wq, wk, wv_t, grad_wo,
    state_down, state_up, block=256,
):
    width, tokens = qt.shape
    rows, model = x.shape
    fresh = wv_t.shape[0]
    pair = 2 * HEAD_DIM
    chunk = state_down.shape[1]
    low_rows = 2 * pair
    cols = model // 2
    vmem = pl.BlockSpec(memory_space=pltpu.VMEM)
    anywhere = pl.BlockSpec(memory_space=pl.ANY)
    results = [
        ((rows, model), F32, vmem),
        ((width - fresh, tokens), F32, vmem),
        ((SUM_ROWS, model), F32, vmem),
        ((3, chunk, model), BF16, anywhere),
        ((model, 3 * chunk), BF16, anywhere),
        ((2, 2 * width, cols), BF16, anywhere),
        ((low_rows, model), BF16, anywhere),
        ((low_rows, cols), BF16, anywhere),
        ((2, low_rows, cols), BF16, anywhere),
    ]
    shapes = {i: ((chunk, model), (model, chunk)) for i in range(3)}
    shapes[3] = ((2 * width, cols),) * 2
    shapes[4] = ((low_rows, model), (low_rows, cols))
    shapes[5] = ((low_rows, cols),) * 2
    slots = scatter_slots(BACK_PLAN, shapes)
    live = unfinished()
    scratch = [
        ((2 * width + fresh, tokens), BF16),
        ((2, pair, tokens), BF16),
        ((2, pair, tokens), BF16),
        ((2, tokens, pair), BF16),
        ((2, tokens, pair), BF16),
        ((2, HEAD_DIM, tokens), F32),
        ((2, HEAD_DIM, tokens), F32),
        ((2 * width + fresh, model), BF16),
        ((rows, model), BF16),
        ((rows, model), BF16),
        ((width, model), BF16),
        ((max(len(live), 1), chunk, model), BF16),
        ((max(len(live), 1), model, chunk), BF16),
        ((2, 2 * width, cols), BF16),
        ((low_rows, model), BF16),
        ((low_rows, cols), BF16),
        ((2, low_rows, cols), BF16),
        ((10, SUM_ROWS, model), F32),
    ]
    near = (qt, k, kt, v, do, attended, lse, ln, x)
    scratch += [(a.shape, a.dtype) for a in near]
    return pl.pallas_call(
        functools.partial(attend_back_kernel, row_chips, block, list(slots)),
        out_shape=[jax.ShapeDtypeStruct(s, t) for s, t, _ in results],
        in_specs=[pl.BlockSpec(memory_space=pltpu.SMEM), vmem, vmem] + [anywhere] * 15,
        out_specs=[spec for _, _, spec in results],
        scratch_shapes=[pltpu.VMEM(s, t) for s, t in scratch]
        + [
            pltpu.SemaphoreType.DMA((6,)),
            pltpu.SemaphoreType.DMA((13,)),
            pltpu.SemaphoreType.DMA((2, 3)),
            pltpu.SemaphoreType.DMA((2, 10)),
            pltpu.SemaphoreType.DMA((6, 2, 2, 11)),
        ]
        + [pltpu.VMEM(shape, BF16) for shape in slots.values()]
        + [
            pltpu.VMEM((shape[0] // (16 if progress(i) == 3 else 4), shape[1]), BF16)
            for i in range(3)
            if i not in live
            for shape in shapes[i]
        ],
        compiler_params=pltpu.CompilerParams(
            vmem_limit_bytes=VMEM_LIMIT, collective_id=3, has_side_effects=True
        ),
        name="attend_back",
    )(
        split, gain, small, qt, k, kt, v, do, attended, lse, ln, x, wq, wk, wv_t, grad_wo,
        state_down, state_up,
    )


def finish_kernel(
    mid, back, dv, sums, down, up, wo, wo_low, low, thin, last,
    grad_input, grad_first, grad_down, grad_up, grad_wo, grad_q, grad_k, grad_v, bu,
    bias_q, bias_v, gain_two, shift_two, bias_o, bias_d, gain_one, shift_one,
):
    cols = wo.shape[2]
    pair = 2 * HEAD_DIM
    grad_input[...] = mid[...] + back[...]
    grad_first[...] = dv[...]
    grad_down[...] = down[0].astype(F32)
    grad_up[...] = up[...].astype(F32)
    for j in range(2):
        grad_wo[:, j * cols : (j + 1) * cols] = wo[j].astype(F32)
    for i, target in enumerate((grad_q, grad_k)):
        span = slice(i * pair, (i + 1) * pair)
        for j, source in enumerate((wo_low[0, span], low[span], last[0, span])):
            target[:, j * pair : (j + 1) * pair] = source.astype(F32).T
    grad_v[:pair] = wo_low[0, 2 * pair :].astype(F32)
    grad_v[pair:] = thin[...].astype(F32)

    @pl.when(pl.program_id(0) == 0)
    def _():
        chunk = bu.shape[0] // 3
        for i in range(3):
            bu[i * chunk : (i + 1) * chunk] = sums[ROW_BU + i, :chunk]
        bias_q[...] = sums[ROW_BQ, : bias_q.shape[0]]
        bias_v[...] = sums[ROW_BV, : bias_v.shape[0]]
        for i, target in enumerate((gain_two, shift_two, bias_o, bias_d, gain_one, shift_one)):
            target[...] = sums[i, :]


def finish(mid, back, dv, sums, down, up, wo, low, thin, last):
    rows, width = mid.shape
    heads = wo.shape[1] // 2
    fresh = heads // 2
    hidden = up.shape[1]
    steps = 6
    half = down.shape[1] // 2
    lanes = width // steps
    out_rows = 192
    operands = (mid, back, dv, sums, down, up, wo, wo, low, thin, last)
    fixed = lambda s: pl.BlockSpec(s, lambda i, nd=len(s): (0,) * nd)
    by_rows = lambda n, c: pl.BlockSpec((n, c), lambda i: (i, 0))
    by_lanes = lambda n: pl.BlockSpec((n, lanes), lambda i: (0, i))
    by_halves = lambda n, k: pl.BlockSpec((1, n, lanes), lambda i: (i // 3, k, lax.rem(i, 3)))
    moved = [
        by_rows(out_rows, width),
        by_rows(dv.shape[0] // steps, dv.shape[1]),
        by_rows(half, width),
        by_rows(width // steps, hidden),
        by_rows(heads // steps, width),
    ]
    specs = [
        moved[0],
        moved[0],
        moved[1],
        fixed(sums.shape),
        pl.BlockSpec((1, half, width), lambda i: (i // 2, lax.rem(i, 2), 0)),
        moved[3],
        pl.BlockSpec((2, heads // steps, wo.shape[2]), lambda i: (0, i, 0)),
        by_halves(heads, 1),
        by_lanes(low.shape[0]),
        pl.BlockSpec((HEAD_DIM, lanes), lambda i: (i // 3, lax.rem(i, 3))),
        by_halves(last.shape[1], 0),
    ]
    shapes = [(rows, width), dv.shape, (hidden, width), (width, hidden), (heads, width)]
    shapes += [(width, heads), (width, heads), (fresh, width)]
    shapes += [(hidden,), (heads,), (fresh,)] + [(width,)] * 6
    out_specs = moved + [by_rows(lanes, heads)] * 2 + [by_lanes(fresh)]
    out_specs += [fixed(s) for s in shapes[8:]]
    return pl.pallas_call(
        finish_kernel,
        grid=(steps,),
        in_specs=specs,
        out_specs=out_specs,
        out_shape=[jax.ShapeDtypeStruct(s, F32) for s in shapes],
        compiler_params=pltpu.CompilerParams(vmem_limit_bytes=VMEM_LIMIT),
        name="finish",
    )(*operands)


def swap(array):
    return lax.ppermute(array, "tensor", [(0, 1), (1, 0)])


def across_blocks(array, row_chips):
    chips = 4 * row_chips * row_chips
    shift = 2
    while shift < row_chips:
        for stride in (shift, shift * row_chips):
            pairs = [(i, i ^ stride) for i in range(chips)]
            array = array + lax.ppermute(array, "dp", pairs)
        shift *= 2
    return array


def on_device(
    row_chips,
    input_rows, first_values, doc_split, gain_norm1, bias_norm1, w_query, bias_query, w_key,
    w_value, bias_value, w_out, bias_attn_out, gain_norm2, bias_norm2, w_up, bias_up, w_down,
    bias_down, cotangent,
):
    heads = w_query.shape[1]
    fresh = w_value.shape[1]
    hidden = w_up.shape[1]
    pair = 2 * HEAD_DIM
    wv_t = w_value.T
    ln, qt, k, kt, v, vt = project(
        input_rows, first_values.T, gain_norm1, bias_norm1, w_query, bias_query, w_key, wv_t,
        bias_value,
    )
    up, down, wo, bu, vt = lax.optimization_barrier((w_up, w_down, w_out, bias_up, vt))
    up_other, down_other, wo_other, bu_other = swap(up), swap(down), swap(wo), swap(bu)
    attended, lse = attend(doc_split, qt, k, vt)
    output, grad_middle, grad_att, state_down, state_up, grad_wo, small = feed(
        row_chips, input_rows, cotangent, attended, w_out, wo_other, bias_attn_out, gain_norm2,
        bias_norm2, up_other, w_up, bu_other, bias_up, down_other, w_down, bias_down,
    )
    back, dv_first, *reduced = attend_back(
        row_chips, doc_split, gain_norm1, small, qt, k, kt, v, grad_att, attended, lse, ln,
        input_rows, w_query, w_key, wv_t, grad_wo, state_down, state_up,
    )
    reduced = [across_blocks(a, row_chips) for a in reduced]
    (
        grad_input, grad_first, grad_down, grad_up, grad_wo, grad_q, grad_k, grad_v, bias_grad_up,
        bias_grad_q, bias_grad_v, gain_two, shift_two, bias_grad_o, bias_grad_d, gain_one, shift_one,
    ) = finish(grad_middle, back, dv_first, *reduced)
    return (
        output, grad_input, grad_first.T, gain_one, shift_one, grad_q, bias_grad_q, grad_k, grad_v.T,
        bias_grad_v, grad_wo, bias_grad_o, gain_two, shift_two, grad_up, bias_grad_up, grad_down,
        bias_grad_d,
    )


def solution(mesh):
    row_chips = 1
    while 4 * row_chips * row_chips < mesh.shape["dp"]:
        row_chips += 1
    rows = P(("dp", "tensor"), None)
    cols = P(None, "tensor")
    split = P("tensor")
    firsts = P("dp", "tensor")
    wide = P("tensor", None)
    return jax.shard_map(
        functools.partial(on_device, row_chips),
        mesh=mesh,
        in_specs=(
            rows, firsts, P("dp"), P(), P(), cols, split, cols, cols, split, wide, P(), P(), P(),
            cols, split, wide, P(), rows,
        ),
        out_specs=(
            rows, rows, firsts, P(), P(), cols, split, cols, cols, split, wide, P(), P(), P(),
            cols, split, wide, P(),
        ),
        check_vma=False,
    )
```

```python
import functools

import jax
import jax.numpy as jnp
from jax import lax
from jax.experimental import pallas as pl
from jax.experimental.pallas import tpu as pltpu
from jax.sharding import PartitionSpec as P

HEAD_DIM = 64
NORM_EPS = 1e-05
GELU_ROOT = 0.7978845608028654
GELU_CUBE = 0.044715
NN = (((1,), (0,)), ((), ()))
NT = (((1,), (1,)), ((), ()))
TN = (((0,), (0,)), ((), ()))
F32 = jnp.float32
BF16 = jnp.bfloat16
VMEM_LIMIT = 60 << 20
MESH = pl.DeviceIdType.MESH


def dot(left, right, dims=NN):
    return lax.dot_general(left, right, dims, preferred_element_type=F32)


def whole(array):
    return pl.BlockSpec(array.shape, lambda *_, nd=array.ndim: (0,) * nd)


def whole_shape(shape):
    return pl.BlockSpec(shape, lambda *_, nd=len(shape): (0,) * nd)


def row_normalize(rows):
    centered = rows - jnp.mean(rows, axis=1, keepdims=True)
    inverse = lax.rsqrt(jnp.mean(centered * centered, axis=1, keepdims=True) + NORM_EPS)
    return centered * inverse, inverse


def row_normalize_back(scaled, normed, inverse):
    return inverse * (
        scaled
        - jnp.mean(scaled, axis=1, keepdims=True)
        - normed * jnp.mean(scaled * normed, axis=1, keepdims=True)
    )


AXES = ("x", "y", "z")
SIZE = {"x": 2, "y": 2, "z": 4}


class Place:
    def __init__(self, row_chips):
        index = lax.axis_index("dp")
        self.core = lax.axis_index("tensor")
        self.wide = row_chips
        self.index = index
        self.x = lax.rem(index, row_chips)
        self.y = lax.rem(index // row_chips, row_chips)
        self.z = index // (row_chips * row_chips)
        self.at = {"x": lax.rem(self.x, 2), "y": lax.rem(self.y, 2), "z": self.z}

    def peer(self, axis, step):
        size = SIZE[axis]
        spot = lax.rem(self.at[axis] + step, size)
        stride = {"x": 1, "y": self.wide, "z": self.wide * self.wide}[axis]
        return spot, (self.index + (spot - self.at[axis]) * stride, self.core)

    def twin(self):
        return (self.index, 1 - self.core)

    def across(self, step_x, step_y, other_core):
        index = self.index
        for axis, step, stride in (("x", step_x, 1), ("y", step_y, self.wide)):
            index = index + (lax.rem(self.at[axis] + step, 2) - self.at[axis]) * stride
        return (index, 1 - self.core if other_core else self.core)

    def block(self):
        places = [(0, 1), (1, 0), (1, 1)]
        return [self.across(*p, False) for p in places] + [
            self.across(*p, True) for p in [(0, 0)] + places
        ]

    def others(self):
        return self.block() + [self.peer("z", k)[1] for k in range(1, SIZE["z"])]


def greet(place):
    barrier = pltpu.get_barrier_semaphore()
    devices = place.others()
    for device in devices:
        pl.semaphore_signal(barrier, inc=1, device_id=device, device_id_type=MESH)
    return lambda: pl.semaphore_wait(barrier, len(devices))


class Sum:
    def __init__(self, place, order, held, slots, result, sems):
        self.place, self.order, self.held = place, order, held
        self.slots, self.result, self.sems = slots, result, sems
        self.rows = (held if held is not None else result).shape[0]

    def region(self, depth):
        start, size = 0, self.rows
        for axis in self.order[:depth]:
            size //= SIZE[axis]
            start = start + self.place.at[axis] * size
        return start, size

    def span(self, depth):
        start, size = self.region(depth)
        return pl.ds(pl.multiple_of(start, 16) if depth else start, size)

    def first_sem(self, gather, stage):
        count = 0
        for axis in self.order[:stage]:
            count += SIZE[axis] - 1
        return count + (5 if gather else 0)

    def scatter_copies(self, stage):
        axis = self.order[stage]
        start, size = self.region(stage)
        piece = size // SIZE[axis]
        base = self.first_sem(False, stage)
        copies = []
        for step in range(1, SIZE[axis]):
            spot, device = self.place.peer(axis, step)
            copies.append(
                pltpu.make_async_remote_copy(
                    src_ref=self.held.at[pl.ds(pl.multiple_of(start + spot * piece, 16), piece), :],
                    dst_ref=self.slots[stage].at[step - 1],
                    send_sem=self.sems.at[0, base + step - 1],
                    recv_sem=self.sems.at[1, base + step - 1],
                    device_id=device,
                    device_id_type=MESH,
                )
            )
        return copies

    def scatter_end(self, stage):
        for copy in self.scatter_copies(stage):
            copy.wait()
        span = self.span(stage + 1)
        total = self.held[span, :].astype(F32)
        for step in range(SIZE[self.order[stage]] - 1):
            total = total + self.slots[stage][step].astype(F32)
        self.held[span, :] = total.astype(BF16)

    def gather_copies(self, stage, source):
        axis = self.order[stage]
        span = self.span(stage + 1)
        base = self.first_sem(True, stage)
        copies = []
        origin = self.result.at[span, :] if source is None else source
        for step in range(1, SIZE[axis]):
            _, device = self.place.peer(axis, step)
            copies.append(
                pltpu.make_async_remote_copy(
                    src_ref=origin,
                    dst_ref=self.result.at[span, :],
                    send_sem=self.sems.at[0, base + step - 1],
                    recv_sem=self.sems.at[1, base + step - 1],
                    device_id=device,
                    device_id_type=MESH,
                )
            )
        if source is not None:
            copies.append(
                pltpu.make_async_copy(source, self.result.at[span, :], self.sems.at[0, 10])
            )
        return copies

    def run(self, action, source=None):
        verb, letter = action
        gather = letter in "cba"
        stage = "abc".index(letter) if gather else "ABC".index(letter)
        if gather:
            for copy in self.gather_copies(stage, source):
                copy.start() if verb == "s" else copy.wait()
        elif verb == "s":
            for copy in self.scatter_copies(stage):
                copy.start()
        else:
            self.scatter_end(stage)


def slot_shapes(order, rows, cols):
    shapes = []
    for axis in order:
        rows //= SIZE[axis]
        shapes.append((SIZE[axis] - 1, rows, cols))
    return shapes


ORDERS = ("xyz", "yxz")
FEED_PLAN = {
    "s1m": ((0, "sA"),),
    "s3q": ((0, "fA"), (0, "sB"),),
    "s3m": ((1, "sA"),),
    "s3e": ((0, "fB"), (0, "sC"),),
    "s5q": ((1, "fA"), (1, "sB"),),
    "s5m": ((0, "fC"), (0, "sc"), (2, "sA"),),
    "s5e": ((1, "fB"),),
    "f_end": ((0, "fc"), (2, "fA"),),
}
BACK_PLAN = {
    "start": ((0, "sb"), (1, "sC"), (2, "sB"),),
    (0, 3): ((0, "fb"), (0, "sa"),),
    (0, 5): ((1, "fC"), (2, "fB"), (1, "sc"), (2, "sC"),),
    (0, 7): ((0, "fa"), (3, "sA"),),
    (1, 0): ((1, "fc"), (1, "sb"),),
    (1, 4): ((3, "fA"), (3, "sB"),),
    (1, 5): ((2, "fC"), (1, "fb"), (1, "sa"), (2, "sc"),),
    (1, 6): ((3, "fB"), (3, "sC"),),
    (1, 7): ((4, "sA"),),
    (2, 0): ((2, "fc"), (2, "sb"),),
    (2, 1): ((1, "fa"),),
    (2, 4): ((4, "fA"), (3, "fC"), (3, "sc"), (4, "sB"),),
    (2, 5): ((2, "fb"), (2, "sa"),),
    (2, 6): ((4, "fB"), (4, "sC"),),
    (2, 7): ((3, "fc"), (5, "sA"), (3, "sb"),),
    "e0": ((4, "fC"), (4, "sc"),),
    "e1": ((2, "fa"), (5, "fA"), (4, "fc"), (5, "sB"), (4, "sb"),),
    "e2": ((3, "fb"), (5, "fB"), (3, "sa"), (5, "sC"),),
    "e3": ((4, "fb"), (5, "fC"), (5, "sc"), (4, "sa"),),
    "e5": ((5, "fc"), (3, "fa"), (5, "sb"),),
    "e6": ((4, "fa"),),
    "w0": ((5, "fb"), (5, "sa"),),
    "w1": ((5, "fa"),),
}


def started(plan):
    return [(i, action[1]) for actions in plan.values() for i, action in actions if action[0] == "s"]


def progress(batch):
    return sum(1 for i, _ in started(FEED_PLAN) if i == batch)


def unfinished():
    return [i for i in range(3) if progress(i) < 3]


def scatter_slots(plan, shapes):
    slots = {}
    for i, letter in started(plan):
        if letter in "ABC":
            for j, order in enumerate(ORDERS):
                shape = slot_shapes(order, *shapes[i][j])["ABC".index(letter)]
                slots[i, j, letter] = shape
    return slots


def project_kernel(
    block, x, first_t, gain, bias, wq, bq, wk, wv_t, bv, ln, qt, k, kt, v, vt,
    x_other, weights, s_ln, s_qt, s_k, s_kt, s_v, s_vt, pair_sems, out_sems,
):
    rows = x.shape[0]
    heads, fresh = wq.shape[1], wv_t.shape[0]
    core = lax.axis_index("tensor")
    twin = (lax.axis_index("dp"), 1 - core)
    barrier = pltpu.get_barrier_semaphore()
    pl.semaphore_signal(barrier, inc=1, device_id=twin, device_id_type=MESH)
    weights[:, :heads] = wq[...]
    weights[:, heads : 2 * heads] = wk[...]
    weights[:, 2 * heads :] = wv_t[...].T
    pl.semaphore_wait(barrier, 1)
    send = pltpu.make_async_remote_copy(
        src_ref=x, dst_ref=x_other, send_sem=pair_sems.at[0], recv_sem=pair_sems.at[1],
        device_id=twin, device_id_type=MESH,
    )
    send.start()
    gain_row = gain[...].astype(F32).reshape(1, -1)
    bias_row = bias[...].astype(F32).reshape(1, -1)
    bq_row = bq[...].astype(F32).reshape(1, -1)
    bv_row = bv[...].astype(F32).reshape(1, -1)
    copies = []
    for part, source in enumerate((x, x_other)):
        if part:
            send.wait_recv()
        spot = pl.multiple_of((core if part == 0 else 1 - core) * rows, rows)
        for first in range(0, rows, block):
            span = pl.ds(first, block)
            normed, _ = row_normalize(source[span, :].astype(F32))
            low = (normed * gain_row + bias_row).astype(BF16)
            s_ln[part, span] = low
            product = dot(low, weights[...])
            queries = (product[:, :heads] + bq_row).astype(BF16).astype(F32) * HEAD_DIM ** (-0.5)
            s_qt[part, :, span] = queries.astype(BF16).T
            keys = product[:, heads : 2 * heads].astype(BF16)
            s_k[part, span] = keys
            s_kt[part, :, span] = keys.T
            values = (product[:, 2 * heads :] + bv_row).astype(BF16)
            reused = first_t[:, pl.ds(pl.multiple_of(spot + first, block), block)]
            s_vt[part, :fresh, span] = values.T
            s_vt[part, fresh:, span] = reused
            s_v[part, span] = jnp.concatenate([values, reused.T], axis=1)
        targets = (
            (s_ln, ln.at[pl.ds(spot, rows), :]),
            (s_qt, qt.at[:, pl.ds(spot, rows)]),
            (s_k, k.at[pl.ds(spot, rows), :]),
            (s_kt, kt.at[:, pl.ds(spot, rows)]),
            (s_v, v.at[pl.ds(spot, rows), :]),
            (s_vt, vt.at[:, pl.ds(spot, rows)]),
        )
        for i, (held, target) in enumerate(targets):
            copy = pltpu.make_async_copy(held.at[part], target, out_sems.at[part, i])
            copy.start()
            copies.append(copy)
    send.wait_send()
    for copy in copies:
        copy.wait()


def project(x, first_t, gain, bias, wq, bq, wk, wv_t, bv, block=1024):
    rows, width = x.shape
    heads = wq.shape[1]
    tall, flat = (rows, heads), (heads, rows)
    vmem = pl.BlockSpec(memory_space=pltpu.VMEM)
    shapes = ((2 * rows, width), (heads, 2 * rows), (2 * rows, heads)) + (
        (heads, 2 * rows), (2 * rows, heads), (heads, 2 * rows),
    )
    scratch = [(rows, width), (width, 2 * heads + wv_t.shape[0])]
    scratch += [(2,) + s for s in ((rows, width), flat, tall, flat, tall, flat)]
    return pl.pallas_call(
        functools.partial(project_kernel, block),
        out_shape=[jax.ShapeDtypeStruct(s, BF16) for s in shapes],
        in_specs=[vmem] * 9,
        out_specs=[pl.BlockSpec(memory_space=pl.ANY)] * 6,
        scratch_shapes=[pltpu.VMEM(s, BF16) for s in scratch]
        + [pltpu.SemaphoreType.DMA((2,)), pltpu.SemaphoreType.DMA((2, 6))],
        compiler_params=pltpu.CompilerParams(
            vmem_limit_bytes=VMEM_LIMIT, collective_id=1, has_side_effects=True
        ),
        name="project",
    )(x, first_t, gain, bias, wq, bq, wk, wv_t, bv)


def causal(size):
    keys = lax.broadcasted_iota(jnp.int32, (size, size), 0)
    return keys <= lax.broadcasted_iota(jnp.int32, (size, size), 1)


def attend_kernel(block, ahead, split, qt, k, vt, attended, lse, sums, k_aug, q_aug):
    width, tokens = qt.shape
    half = tokens // 2
    pair_width = 2 * HEAD_DIM
    far = jnp.where(split[0] < tokens, -1e9, 0.0)
    row = lax.broadcasted_iota(jnp.int32, (HEAD_DIM, tokens), 0)
    token = lax.broadcasted_iota(jnp.int32, (HEAD_DIM, tokens), 1)
    far_rows = jnp.where((row == 0) & (token >= half), far, 0.0).astype(BF16)
    lane = lax.broadcasted_iota(jnp.int32, (tokens, pair_width), 1)
    key = lax.broadcasted_iota(jnp.int32, (tokens, pair_width), 0)
    first_half = jnp.where((lax.rem(lane, HEAD_DIM) == 0) & (key < half), 1.0, 0.0).astype(BF16)
    ones = (lax.broadcasted_iota(jnp.int32, (16, tokens), 0) == 0).astype(BF16)
    for j in range(2):
        sums[j, HEAD_DIM:, :] = ones
        extra = HEAD_DIM * (1 - j)
        q_aug[j, extra : extra + HEAD_DIM, :] = far_rows

    def pair_step(pair, _):
        col = pl.multiple_of(pair * pair_width, pair_width)
        head_rows = [pl.ds(pl.multiple_of(col + HEAD_DIM * j, HEAD_DIM), HEAD_DIM) for j in range(2)]
        keys = k[:, pl.ds(col, pair_width)]
        for j in range(2):
            base = HEAD_DIM * j
            sums[j, :HEAD_DIM, :] = vt[head_rows[j], :]
            k_aug[j] = jnp.where(lane // HEAD_DIM == j, keys, first_half)
            q_aug[j, base : base + HEAD_DIM, :] = qt[head_rows[j], :]

        def products(number, j):
            start, stop = number * block, (number + 1) * block
            return dot(k_aug[j, :stop, :], q_aug[j, :, start:stop])

        def average(number, j, scores):
            start, stop = number * block, (number + 1) * block
            edge = jnp.where(causal(block), scores[start:], -1e30)
            top = jnp.max(edge, axis=0, keepdims=True)
            if start:
                near = scores[:start]
                top = jnp.maximum(top, jnp.max(near, axis=0, keepdims=True))
                weights = jnp.concatenate(
                    [jnp.exp(near - top).astype(BF16), jnp.exp(edge - top).astype(BF16)], axis=0
                )
            else:
                weights = jnp.exp(edge - top).astype(BF16)
            total = dot(sums[j, :, :stop], weights)
            denominator = total[HEAD_DIM : HEAD_DIM + 1]
            attended[head_rows[j], start:stop] = (total[:HEAD_DIM] * (1.0 / denominator)).astype(BF16)
            lse[pl.ds(pair * 2 + j, 1), :, start:stop] = (top + jnp.log(denominator))[None]

        units = [(number, j) for number in range(tokens // block) for j in range(2)]
        queue = [products(*unit) for unit in units[:ahead]]
        for i, unit in enumerate(units):
            if i + ahead < len(units):
                queue.append(products(*units[i + ahead]))
            average(*unit, queue.pop(0))
        return 0

    lax.fori_loop(0, width // pair_width, pair_step, 0)


def attend(split, qt, k, vt, block=256, ahead=4):
    width, tokens = qt.shape
    pair_width = 2 * HEAD_DIM
    vmem = pl.BlockSpec(memory_space=pltpu.VMEM)
    return pl.pallas_call(
        functools.partial(attend_kernel, block, ahead),
        out_shape=(
            jax.ShapeDtypeStruct((width, tokens), BF16),
            jax.ShapeDtypeStruct((width // HEAD_DIM, 1, tokens), F32),
        ),
        in_specs=[pl.BlockSpec(memory_space=pltpu.SMEM), vmem, vmem, vmem],
        out_specs=(vmem, vmem),
        scratch_shapes=[
            pltpu.VMEM((2, HEAD_DIM + 16, tokens), BF16),
            pltpu.VMEM((2, tokens, pair_width), BF16),
            pltpu.VMEM((2, pair_width, tokens), BF16),
        ],
        compiler_params=pltpu.CompilerParams(vmem_limit_bytes=VMEM_LIMIT),
        name="attend",
    )(split, qt, k, vt)


def gelu_both(v):
    square = v * v
    tanh = jnp.tanh(v * (GELU_ROOT + (GELU_ROOT * GELU_CUBE) * square))
    half = 0.5 * v
    slope = 0.5 + 0.5 * tanh + half * (1.0 - tanh * tanh) * (
        GELU_ROOT + (3.0 * GELU_ROOT * GELU_CUBE) * square
    )
    return half + half * tanh, slope


SUM_ROWS = 16
ROW_BU, ROW_BU_OTHER, ROW_BQ, ROW_BV = 6, 9, 12, 13


def feed_kernel(
    row_chips, slot_keys, x_far, cot_far, attended, wo_own_far, wo_other_far, bias_o, gain, bias,
    up_other, up_own, bu_other, bu_own, down_other, down_own, bias_d,
    out, grad_mid, grad_att, state_down, state_up, grad_wo, small,
    att_own, att_other, ln, ln_t, normed, inverse, total, grad_ln, att_stage, stage_down, stage_up,
    held_down, held_up, x, cot, wo_own, wo_other, kept_act, kept_grad,
    move_sems, load_sems, pair_sems, sum_sems, *slot_refs,
):
    state, stage, held = (state_down, state_up), (stage_down, stage_up), (held_down, held_up)
    slots = dict(zip(slot_keys, slot_refs))
    step = pl.program_id(0)
    place = Place(row_chips)
    core = place.core
    rows = x.shape[0]
    heads = att_own.shape[0]
    chunk = up_own.shape[1]
    index = step // 2
    own = pl.ds(pl.multiple_of(core * rows, rows), rows)
    theirs = pl.ds(pl.multiple_of((1 - core) * rows, rows), rows)

    def to_twin(source, target, i):
        return pltpu.make_async_remote_copy(
            src_ref=source, dst_ref=target, send_sem=pair_sems.at[0, i],
            recv_sem=pair_sems.at[1, i], device_id=place.twin(), device_id_type=MESH,
        )

    def stage_copies(i):
        return [to_twin(stage[j].at[i], held[j].at[i], 2 + 2 * i + j) for j in range(2)]

    def part(i, j):
        return Sum(
            place, ORDERS[j], held[j].at[i], [slots.get((i, j, letter)) for letter in "ABC"],
            state[j].at[i], sum_sems.at[i, j],
        )

    def act(point):
        for i, action in FEED_PLAN.get(point, ()):
            for j in range(2):
                one = part(i, j)
                one.run(action, one.held.at[one.span(3), :] if action[1] == "c" else None)

    def act_at(name, odd):
        for k in range(odd, 6, 2):
            point = "s%d%s" % (k, name)
            if point in FEED_PLAN:
                pl.when(step == k)(functools.partial(act, point))

    @pl.when(step == 0)
    def _():
        ready = greet(place)
        loads = [
            pltpu.make_async_copy(source, target, load_sems.at[i])
            for i, (source, target) in enumerate(
                (
                    (attended.at[:, own], att_own), (wo_own_far, wo_own), (x_far, x),
                    (wo_other_far, wo_other), (cot_far, cot),
                )
            )
        ]
        for load in loads:
            load.start()
        ready()
        exchange = to_twin(attended.at[:, theirs], att_other, 0)
        exchange.start()
        grad_ln[...] = jnp.zeros_like(grad_ln)
        small[...] = jnp.zeros_like(small)
        for load in loads:
            load.wait()
        total[...] = x[...].astype(F32) + (
            dot(att_own[...], wo_own[...], TN) + bias_o[...].astype(F32).reshape(1, -1)
        )
        exchange.wait()
        mid = total[...] + dot(att_other[...], wo_other[...], TN)
        total[...] = mid + bias_d[...].astype(F32).reshape(1, -1)
        norm, inv = row_normalize(mid)
        normed[...] = norm
        inverse[...] = jnp.broadcast_to(inv, inverse.shape)
        low = (
            norm * gain[...].astype(F32).reshape(1, -1) + bias[...].astype(F32).reshape(1, -1)
        ).astype(BF16)
        ln[...] = low
        ln_t[...] = low.T

    def weight_grads(up, bias_up, down, odd):
        hidden = dot(ln[...], up[...]) + bias_up[
            pl.ds(pl.multiple_of(index * chunk, chunk), chunk)
        ].astype(F32).reshape(1, -1)
        activated, slope = gelu_both(hidden)
        activated = activated.astype(BF16)
        grad_hidden = (dot(cot[...], down[...], NT) * slope).astype(BF16)
        act_at("q", odd)
        grad_down = dot(activated, cot[...], TN)
        grad_up = dot(ln_t[...], grad_hidden)
        sums = jnp.sum(grad_hidden.astype(F32), axis=0, keepdims=True)
        return activated, grad_hidden, grad_down, grad_up, sums

    @pl.when(lax.rem(step, 2) == 0)
    def _():
        activated, grad_hidden, grad_down, grad_up, sums = weight_grads(
            up_other, bu_other, down_other, 0
        )
        stage_down[index] = grad_down.astype(BF16)
        stage_up[index] = grad_up.astype(BF16)
        for copy in stage_copies(index):
            copy.start()
        small[pl.ds(ROW_BU_OTHER + index, 1), :chunk] = sums
        kept_act[...] = activated
        kept_grad[...] = grad_hidden
        act_at("m", 0)

    @pl.when(lax.rem(step, 2) == 1)
    def _():
        activated, grad_hidden, grad_down, grad_up, sums = weight_grads(up_own, bu_own, down_own, 1)
        for copy in stage_copies(index):
            copy.wait()
        held_down[index] = (grad_down + held_down[index].astype(F32)).astype(BF16)
        held_up[index] = (grad_up + held_up[index].astype(F32)).astype(BF16)
        small[pl.ds(ROW_BU + index, 1), :chunk] = sums

        act_at("m", 1)
        total[...] += dot(kept_act[...], down_other[...]) + dot(activated, down_own[...])
        grad_ln[...] += dot(kept_grad[...], up_other[...], NT) + dot(grad_hidden, up_own[...], NT)
        act_at("e", 1)

    @pl.when(step == 5)
    def _():
        grad = grad_ln[...]
        norm = normed[...]
        cot32 = cot[...].astype(F32)
        scaled = grad * gain[...].astype(F32).reshape(1, -1)
        mid = cot32 + row_normalize_back(scaled, norm, inverse[:, :1])
        grad_mid[...] = mid
        low = mid.astype(BF16)
        att_stage[1] = dot(wo_other[...], low, NT).astype(BF16)
        exchange = to_twin(att_stage.at[1], grad_att.at[:, own], 1)
        exchange.start()
        att_stage[0] = dot(wo_own[...], low, NT).astype(BF16)
        local = pltpu.make_async_copy(att_stage.at[0], grad_att.at[:, own], move_sems.at[0])
        local.start()
        out[...] = total[...].astype(BF16)
        small[0:1, :] = jnp.sum(grad * norm, axis=0, keepdims=True)
        small[1:2, :] = jnp.sum(grad, axis=0, keepdims=True)
        small[2:3, :] = jnp.sum(low.astype(F32), axis=0, keepdims=True)
        small[3:4, :] = jnp.sum(cot32, axis=0, keepdims=True)
        grad_wo[:heads] = dot(att_own[...], low).astype(BF16)
        grad_wo[heads:] = dot(att_other[...], low).astype(BF16)
        act("f_end")
        moves = [local]
        for i in range(3):
            if progress(i) > 3:
                continue
            for j in range(2):
                span = part(i, j).span(progress(i))
                move = pltpu.make_async_copy(
                    held[j].at[i, span, :], state[j].at[i, span, :], move_sems.at[1 + 2 * i + j]
                )
                move.start()
                moves.append(move)
        exchange.wait()
        for move in moves:
            move.wait()


def feed(
    row_chips, x, cot, attended, wo_own, wo_other, bias_o, gain, bias,
    up_other, up_own, bu_other, bu_own, down_other, down_own, bias_d,
):
    rows, width = x.shape
    hidden = up_own.shape[1]
    heads = wo_own.shape[0]
    chunk = hidden // 3
    once = pl.Buffered(1)
    fixed = lambda s: pl.BlockSpec(s, lambda j, nd=len(s): (0,) * nd, pipeline_mode=once)
    anywhere = pl.BlockSpec(memory_space=pl.ANY)
    up_spec = pl.BlockSpec((width, chunk), lambda j: (0, j // 2))
    down_spec = pl.BlockSpec((chunk, width), lambda j: (j // 2, 0))
    operands = (
        x, cot, attended, wo_own, wo_other, bias_o, gain, bias,
        up_other, up_own, bu_other, bu_own, down_other, down_own, bias_d,
    )
    specs = [fixed(a.shape) for a in operands]
    for i in range(5):
        specs[i] = anywhere
    specs[8] = specs[9] = up_spec
    specs[12] = specs[13] = down_spec
    results = [
        ((rows, width), BF16),
        ((rows, width), F32),
        ((heads, 2 * rows), BF16),
        ((3, chunk, width), BF16),
        ((3, width, chunk), BF16),
        ((2 * heads, width), BF16),
        ((SUM_ROWS, width), F32),
    ]
    out_specs = [fixed(s) for s, _ in results]
    out_specs[2] = out_specs[3] = out_specs[4] = anywhere
    slots = scatter_slots(FEED_PLAN, {i: ((chunk, width), (width, chunk)) for i in range(3)})
    return pl.pallas_call(
        functools.partial(feed_kernel, row_chips, list(slots)),
        grid=(6,),
        in_specs=specs,
        out_specs=out_specs,
        out_shape=[jax.ShapeDtypeStruct(s, t) for s, t in results],
        scratch_shapes=[
            pltpu.VMEM((heads, rows), BF16),
            pltpu.VMEM((heads, rows), BF16),
            pltpu.VMEM((rows, width), BF16),
            pltpu.VMEM((width, rows), BF16),
            pltpu.VMEM((rows, width), F32),
            pltpu.VMEM((rows, 128), F32),
            pltpu.VMEM((rows, width), F32),
            pltpu.VMEM((rows, width), F32),
            pltpu.VMEM((2, heads, rows), BF16),
            pltpu.VMEM((3, chunk, width), BF16),
            pltpu.VMEM((3, width, chunk), BF16),
            pltpu.VMEM((3, chunk, width), BF16),
            pltpu.VMEM((3, width, chunk), BF16),
            pltpu.VMEM((rows, width), BF16),
            pltpu.VMEM((rows, width), BF16),
            pltpu.VMEM((heads, width), BF16),
            pltpu.VMEM((heads, width), BF16),
            pltpu.VMEM((rows, chunk), BF16),
            pltpu.VMEM((rows, chunk), BF16),
            pltpu.SemaphoreType.DMA((7,)),
            pltpu.SemaphoreType.DMA((5,)),
            pltpu.SemaphoreType.DMA((2, 8)),
            pltpu.SemaphoreType.DMA((3, 2, 2, 11)),
        ]
        + [pltpu.VMEM(shape, BF16) for shape in slots.values()],
        compiler_params=pltpu.CompilerParams(
            vmem_limit_bytes=VMEM_LIMIT, collective_id=2, has_side_effects=True,
            dimension_semantics=("arbitrary",),
        ),
        name="feed",
    )(*operands)


def extra_rows(row, fourth):
    high = row.astype(BF16).astype(F32)
    middle = (row - high).astype(BF16).astype(F32)
    low = row - high - middle
    index = lax.broadcasted_iota(jnp.int32, (HEAD_DIM, row.shape[1]), 0)
    rest = jnp.where(index == 2, low, jnp.where(index == 3, fourth, 0.0))
    return jnp.where(index == 0, high, jnp.where(index == 1, middle, rest)).astype(BF16)


def attend_back_kernel(
    row_chips, block, slot_keys, split, gain, small, qt_far, k_far, kt_far, v_far, do_far, attended_far, lse_far,
    ln_far, x_far, wq_far, wk_far, wv_far, grad_wo_far, state_down, state_up,
    back, dv_first, sums, red_down, red_up, red_wo, red_low, red_v, red_last,
    stack, q_aug, d_aug, k_aug, v_aug, dk_sum, dv_sum, weights, terms_send, terms_got,
    wo_got, held_down, held_up, held_wo, held_low, held_v, held_last, sums_got,
    qt, k, kt, v, do, attended, lse, ln, x,
    move_sems, load_sems, pair_sems, tiny_sems, sum_sems, *slot_refs,
):
    state, held = (state_down, state_up), (held_down, held_up)
    slots = dict(zip(slot_keys, slot_refs))
    live = unfinished()
    done = [i for i in range(3) if i not in live]
    packed = dict(zip([(i, j) for i in done for j in range(2)], slot_refs[len(slot_keys) :]))
    width, tokens = qt.shape
    half = tokens // 2
    fresh, model = wv_far.shape
    place = Place(row_chips)
    core = place.core
    pair_width = 2 * HEAD_DIM
    own = pl.ds(pl.multiple_of(core * half, half), half)
    theirs = pl.ds(pl.multiple_of((1 - core) * half, half), half)

    def to_twin(source, target, i):
        return pltpu.make_async_remote_copy(
            src_ref=source, dst_ref=target, send_sem=pair_sems.at[0, i],
            recv_sem=pair_sems.at[1, i], device_id=place.twin(), device_id_type=MESH,
        )

    def part(i, j):
        chunk = state_down.shape[1]
        if i < 3:
            holder = held[j].at[live.index(i)] if i in live else None
            result = red_up.at[:, i * chunk : (i + 1) * chunk] if j else red_down.at[i]
        else:
            holder, result = {
                3: (held_wo.at[j], red_wo.at[j]),
                4: ((held_low, red_low), (held_v, red_v))[j],
                5: (held_last.at[j], red_last.at[j]),
            }[i]
        return Sum(
            place, ORDERS[j], holder, [slots.get((i, j, letter)) for letter in "ABC"], result,
            sum_sems.at[i, j],
        )

    def act(point):
        for i, action in BACK_PLAN.get(point, ()):
            for j in range(2):
                one = part(i, j)
                source = None
                if action[1] == "cb"[progress(i) - 3] if i in done else action[1] == "c":
                    source = packed[i, j] if i in done else one.held.at[one.span(3), :]
                one.run(action, source)

    loads = []
    for i in range(3):
        for j in range(2):
            span = part(i, j).span(progress(i) if i in live else 6 - progress(i))
            target = part(i, j).held.at[span, :] if i in live else packed[i, j]
            loads.append(
                pltpu.make_async_copy(state[j].at[i, span, :], target, move_sems.at[2 * i + j])
            )
    ready = greet(place)
    for load in loads:
        load.start()
    pairs = width // pair_width

    def pair_loads(pair):
        lanes = pl.ds(pl.multiple_of(pair * pair_width, pair_width), pair_width)
        heads = pl.ds(pair * 2, 2)
        moves = [(far.at[:, lanes], near.at[:, lanes]) for far, near in ((k_far, k), (v_far, v))]
        moves += [
            (far.at[lanes, :], near.at[lanes, :])
            for far, near in ((qt_far, qt), (kt_far, kt), (do_far, do), (attended_far, attended))
        ]
        moves.append((lse_far.at[heads], lse.at[heads]))
        return [
            pltpu.make_async_copy(far, near, load_sems.at[pair, i])
            for i, (far, near) in enumerate(moves)
        ]

    arriving = [
        pltpu.make_async_copy(far, near, load_sems.at[pairs, i])
        for i, (far, near) in enumerate(
            (
                (grad_wo_far.at[:width, : model // 2], held_wo.at[0, :width, :]),
                (grad_wo_far.at[:width, model // 2 :], held_wo.at[1, :width, :]),
                (ln_far, ln), (wq_far, terms_send.at[:model, :width]),
                (wk_far, terms_send.at[:model, width:]), (wv_far, weights.at[2 * width :, :]),
                (x_far, x),
            )
        )
    ]
    for copy in pair_loads(0):
        copy.start()
    ready()
    wo_exchange = to_twin(grad_wo_far.at[width:, :], wo_got, 0)
    wo_exchange.start()
    for load in loads:
        load.wait()
    act("start")
    for copy in arriving[:3]:
        copy.start()
    for pair in range(1, pairs):
        for copy in pair_loads(pair):
            copy.start()
    for copy in arriving[3:]:
        copy.start()
    far = jnp.where(split[0] < tokens, -1e9, 0.0)
    token = lax.broadcasted_iota(jnp.int32, (1, tokens), 1)
    far_row = jnp.where(token >= half, far, 0.0)

    def weight_rows(rows):
        return dot(stack[rows, :], ln[...]).astype(BF16)

    def bias_sums(target, lanes, rows):
        sums[target : target + 1, lanes] = dot(jnp.ones((8, tokens), BF16), stack[rows, :], NT)[:1]

    def by_columns(target, start, values):
        cols = target.shape[2]
        for j in range(2):
            target[j, start : start + values.shape[0], :] = values[:, j * cols : (j + 1) * cols]

    def pair_step(pair, _):
        for copy in pair_loads(pair):
            copy.wait()
        col = pl.multiple_of(pair * pair_width, pair_width)
        lane = lax.broadcasted_iota(jnp.int32, (tokens, pair_width), 1)
        key = lax.broadcasted_iota(jnp.int32, (tokens, pair_width), 0)
        within = lax.rem(lane, HEAD_DIM)
        ones = jnp.where((within < 3) | ((within == 3) & (key < half)), 1.0, 0.0).astype(BF16)
        keys = k[:, pl.ds(col, pair_width)]
        values = v[:, pl.ds(col, pair_width)]
        dk_sum[...] = jnp.zeros_like(dk_sum)
        dv_sum[...] = jnp.zeros_like(dv_sum)
        head_rows = [pl.ds(pl.multiple_of(col + HEAD_DIM * j, HEAD_DIM), HEAD_DIM) for j in range(2)]
        for j in range(2):
            mine = lane // HEAD_DIM == j
            k_aug[j] = jnp.where(mine, keys, ones)
            v_aug[j] = jnp.where(mine, values, ones)
            grad = do[head_rows[j], :]
            inner = jnp.sum(
                grad.astype(F32) * attended[head_rows[j], :].astype(F32), axis=0, keepdims=True
            )
            base, extra = HEAD_DIM * j, HEAD_DIM * (1 - j)
            q_aug[j, base : base + HEAD_DIM, :] = qt[head_rows[j], :]
            q_aug[j, extra : extra + HEAD_DIM, :] = extra_rows(
                -lse[pl.ds(pair * 2 + j, 1)][0], far_row
            )
            d_aug[j, base : base + HEAD_DIM, :] = grad
            d_aug[j, extra : extra + HEAD_DIM, :] = extra_rows(-inner, 0.0)

        def products(number, j):
            start, stop = number * block, (number + 1) * block
            return (
                dot(k_aug[j, :stop, :], q_aug[j, :, start:stop]),
                dot(v_aug[j, :stop, :], d_aug[j, :, start:stop]),
            )

        def gradients(number, j, scores, grad_probs):
            start, stop = number * block, (number + 1) * block
            probs = jnp.where(causal(block), jnp.exp(scores[start:]), 0.0)
            if start:
                probs = jnp.concatenate([jnp.exp(scores[:start]), probs], axis=0)
            grad_scores = (probs * grad_probs).astype(BF16)
            probs = probs.astype(BF16)
            rows = head_rows[j]
            stack[rows, start:stop] = (
                dot(kt[rows, :stop], grad_scores) * HEAD_DIM ** (-0.5)
            ).astype(BF16)
            dv_sum[j, :, :stop] += dot(do[rows, start:stop], probs, NT)
            dk_sum[j, :, :stop] += dot(qt[rows, start:stop], grad_scores, NT)

        units = [(number, j) for number in range(tokens // block) for j in range(2)]
        ahead = products(*units[0])
        for i, unit in enumerate(units):
            now = ahead
            if i + 1 < len(units):
                ahead = products(*units[i + 1])
            gradients(*unit, *now)
            if unit[1] and i + 1 < len(units):
                for p in range(width // pair_width):
                    if (p, unit[0]) in BACK_PLAN:
                        pl.when(pair == p)(functools.partial(act, (p, unit[0])))

        for j in range(2):
            stack[pl.ds(pl.multiple_of(width + col + HEAD_DIM * j, HEAD_DIM), HEAD_DIM), :] = dk_sum[
                j
            ].astype(BF16)

        @pl.when(pair == 0)
        def _():
            stack[2 * width : 2 * width + HEAD_DIM, :] = dv_sum[0].astype(BF16)
            stack[2 * width + HEAD_DIM : 2 * width + 2 * HEAD_DIM, :] = dv_sum[1].astype(BF16)
            wo_exchange.wait()
            for copy in arriving[:3]:
                copy.wait()
            for j in range(2):
                got = wo_got[:, j * (model // 2) : (j + 1) * (model // 2)].astype(F32)
                held_wo[j, :width, :] = (held_wo[j, :width, :].astype(F32) + got).astype(BF16)
            for i in range(3):
                by_columns(
                    held_wo,
                    width + i * pair_width,
                    weight_rows(slice(i * width, i * width + pair_width)),
                )
            act((0, tokens // block - 1))
            sums[...] = small[...]
            bias_sums(ROW_BQ, slice(0, pair_width), slice(0, pair_width))
            bias_sums(ROW_BV, slice(0, pair_width), slice(2 * width, 2 * width + pair_width))

        @pl.when(pair == 1)
        def _():
            stack[2 * width + 2 * HEAD_DIM :, :] = dv_sum[0].astype(BF16)
            dv_first[:HEAD_DIM, :] = dv_sum[1]
            for i in range(2):
                held_low[i * pair_width : (i + 1) * pair_width] = weight_rows(
                    slice(i * width + pair_width, i * width + 2 * pair_width)
                )
            rest = weight_rows(slice(2 * width + 2 * HEAD_DIM, 2 * width + 3 * HEAD_DIM))
            cols = held_v.shape[1]
            held_v[...] = jnp.zeros_like(held_v)
            for j in range(2):
                held_v[HEAD_DIM * j : HEAD_DIM * (j + 1), :] = rest[:, j * cols : (j + 1) * cols]
            act((1, tokens // block - 1))
            bias_sums(
                ROW_BQ, slice(pair_width, 2 * pair_width), slice(pair_width, 2 * pair_width)
            )
            bias_sums(
                ROW_BV, slice(pair_width, pair_width + HEAD_DIM),
                slice(2 * width + pair_width, 2 * width + pair_width + HEAD_DIM),
            )

        @pl.when(pair == 2)
        def _():
            dv_first[HEAD_DIM : 2 * HEAD_DIM, :] = dv_sum[0]
            dv_first[2 * HEAD_DIM :, :] = dv_sum[1]
            for i in range(2):
                by_columns(
                    held_last,
                    i * pair_width,
                    weight_rows(slice(i * width + 2 * pair_width, i * width + 3 * pair_width)),
                )
            act((2, tokens // block - 1))
            bias_sums(
                ROW_BQ, slice(2 * pair_width, 3 * pair_width),
                slice(2 * pair_width, 3 * pair_width),
            )

        return 0

    lax.fori_loop(0, width // pair_width, pair_step, 0)

    act("e0")
    for copy in arriving[3:]:
        copy.wait()
    weights[:width] = terms_send[:model, :width].T
    weights[width : 2 * width] = terms_send[:model, width:].T
    terms_send[...] = dot(stack[:, theirs], weights[...], TN).astype(BF16)
    terms_exchange = to_twin(terms_send, terms_got, 1)
    terms_exchange.start()
    act("e1")
    back[...] = dot(stack[:, own], weights[...], TN)
    act("e2")
    normed, inverse = row_normalize(x[...].astype(F32))
    terms_exchange.wait()
    grad = back[...] + terms_got[...].astype(F32)
    sums[4:5, :] = jnp.sum(grad * normed, axis=0, keepdims=True)
    sums[5:6, :] = jnp.sum(grad, axis=0, keepdims=True)

    def spread(devices, first):
        return [
            pltpu.make_async_remote_copy(
                src_ref=sums, dst_ref=sums_got.at[first + i], send_sem=tiny_sems.at[0, first + i],
                recv_sem=tiny_sems.at[1, first + i], device_id=device, device_id_type=MESH,
            )
            for i, device in enumerate(devices)
        ]

    copies = spread(place.block(), 0)
    for copy in copies:
        copy.start()
    act("e3")
    back[...] = row_normalize_back(grad * gain[...].astype(F32).reshape(1, -1), normed, inverse)
    act("e4")
    for copy in copies:
        copy.wait()
    total = sums[...]
    for i in range(3):
        total = total + sums_got[i]
    sums[...] = total
    for i in range(3, 7):
        sums[:ROW_BU, :] = sums[:ROW_BU, :] + sums_got[i, :ROW_BU, :]
        sums[ROW_BU:ROW_BU_OTHER, :] = (
            sums[ROW_BU:ROW_BU_OTHER, :] + sums_got[i, ROW_BU_OTHER:ROW_BQ, :]
        )
    copies = spread([place.peer("z", step)[1] for step in range(1, SIZE["z"])], 7)
    for copy in copies:
        copy.start()
    act("e5")
    for copy in copies:
        copy.wait()
    sums[...] = sums[...] + sums_got[7] + sums_got[8] + sums_got[9]
    for point in BACK_PLAN:
        if point == "e6" or point[0] == "w":
            act(point)


def attend_back(
    row_chips, split, gain, small, qt, k, kt, v, do, attended, lse, ln, x, wq, wk, wv_t, grad_wo,
    state_down, state_up, block=256,
):
    width, tokens = qt.shape
    rows, model = x.shape
    fresh = wv_t.shape[0]
    pair = 2 * HEAD_DIM
    chunk = state_down.shape[1]
    low_rows = 2 * pair
    cols = model // 2
    vmem = pl.BlockSpec(memory_space=pltpu.VMEM)
    anywhere = pl.BlockSpec(memory_space=pl.ANY)
    results = [
        ((rows, model), F32, vmem),
        ((width - fresh, tokens), F32, vmem),
        ((SUM_ROWS, model), F32, vmem),
        ((3, chunk, model), BF16, anywhere),
        ((model, 3 * chunk), BF16, anywhere),
        ((2, 2 * width, cols), BF16, anywhere),
        ((low_rows, model), BF16, anywhere),
        ((low_rows, cols), BF16, anywhere),
        ((2, low_rows, cols), BF16, anywhere),
    ]
    shapes = {i: ((chunk, model), (model, chunk)) for i in range(3)}
    shapes[3] = ((2 * width, cols),) * 2
    shapes[4] = ((low_rows, model), (low_rows, cols))
    shapes[5] = ((low_rows, cols),) * 2
    slots = scatter_slots(BACK_PLAN, shapes)
    live = unfinished()
    scratch = [
        ((2 * width + fresh, tokens), BF16),
        ((2, pair, tokens), BF16),
        ((2, pair, tokens), BF16),
        ((2, tokens, pair), BF16),
        ((2, tokens, pair), BF16),
        ((2, HEAD_DIM, tokens), F32),
        ((2, HEAD_DIM, tokens), F32),
        ((2 * width + fresh, model), BF16),
        ((rows, model), BF16),
        ((rows, model), BF16),
        ((width, model), BF16),
        ((max(len(live), 1), chunk, model), BF16),
        ((max(len(live), 1), model, chunk), BF16),
        ((2, 2 * width, cols), BF16),
        ((low_rows, model), BF16),
        ((low_rows, cols), BF16),
        ((2, low_rows, cols), BF16),
        ((10, SUM_ROWS, model), F32),
    ]
    near = (qt, k, kt, v, do, attended, lse, ln, x)
    scratch += [(a.shape, a.dtype) for a in near]
    return pl.pallas_call(
        functools.partial(attend_back_kernel, row_chips, block, list(slots)),
        out_shape=[jax.ShapeDtypeStruct(s, t) for s, t, _ in results],
        in_specs=[pl.BlockSpec(memory_space=pltpu.SMEM), vmem, vmem] + [anywhere] * 15,
        out_specs=[spec for _, _, spec in results],
        scratch_shapes=[pltpu.VMEM(s, t) for s, t in scratch]
        + [
            pltpu.SemaphoreType.DMA((6,)),
            pltpu.SemaphoreType.DMA((4, 7)),
            pltpu.SemaphoreType.DMA((2, 3)),
            pltpu.SemaphoreType.DMA((2, 10)),
            pltpu.SemaphoreType.DMA((6, 2, 2, 11)),
        ]
        + [pltpu.VMEM(shape, BF16) for shape in slots.values()]
        + [
            pltpu.VMEM((shape[0] // (16 if progress(i) == 3 else 4), shape[1]), BF16)
            for i in range(3)
            if i not in live
            for shape in shapes[i]
        ],
        compiler_params=pltpu.CompilerParams(
            vmem_limit_bytes=VMEM_LIMIT, collective_id=3, has_side_effects=True
        ),
        name="attend_back",
    )(
        split, gain, small, qt, k, kt, v, do, attended, lse, ln, x, wq, wk, wv_t, grad_wo,
        state_down, state_up,
    )


def finish_kernel(
    mid, back, dv, sums, down, up, wo, wo_low, low, thin, last,
    grad_input, grad_first, grad_down, grad_up, grad_wo, grad_q, grad_k, grad_v, bu,
    bias_q, bias_v, gain_two, shift_two, bias_o, bias_d, gain_one, shift_one,
):
    cols = wo.shape[2]
    pair = 2 * HEAD_DIM
    grad_input[...] = mid[...] + back[...]
    grad_first[...] = dv[...]
    grad_down[...] = down[0].astype(F32)
    grad_up[...] = up[...].astype(F32)
    for j in range(2):
        grad_wo[:, j * cols : (j + 1) * cols] = wo[j].astype(F32)
    for i, target in enumerate((grad_q, grad_k)):
        span = slice(i * pair, (i + 1) * pair)
        for j, source in enumerate((wo_low[0, span], low[span], last[0, span])):
            target[:, j * pair : (j + 1) * pair] = source.astype(F32).T
    grad_v[:pair] = wo_low[0, 2 * pair :].astype(F32)
    grad_v[pair:] = thin[...].astype(F32)

    @pl.when(pl.program_id(0) == 0)
    def _():
        chunk = bu.shape[0] // 3
        for i in range(3):
            bu[i * chunk : (i + 1) * chunk] = sums[ROW_BU + i, :chunk]
        bias_q[...] = sums[ROW_BQ, : bias_q.shape[0]]
        bias_v[...] = sums[ROW_BV, : bias_v.shape[0]]
        for i, target in enumerate((gain_two, shift_two, bias_o, bias_d, gain_one, shift_one)):
            target[...] = sums[i, :]


def finish(mid, back, dv, sums, down, up, wo, low, thin, last):
    rows, width = mid.shape
    heads = wo.shape[1] // 2
    fresh = heads // 2
    hidden = up.shape[1]
    steps = 6
    half = down.shape[1] // 2
    lanes = width // steps
    out_rows = 192
    operands = (mid, back, dv, sums, down, up, wo, wo, low, thin, last)
    fixed = lambda s: pl.BlockSpec(s, lambda i, nd=len(s): (0,) * nd)
    by_rows = lambda n, c: pl.BlockSpec((n, c), lambda i: (i, 0))
    by_lanes = lambda n: pl.BlockSpec((n, lanes), lambda i: (0, i))
    by_halves = lambda n, k: pl.BlockSpec((1, n, lanes), lambda i: (i // 3, k, lax.rem(i, 3)))
    moved = [
        by_rows(out_rows, width),
        by_rows(dv.shape[0] // steps, dv.shape[1]),
        by_rows(half, width),
        by_rows(width // steps, hidden),
        by_rows(heads // steps, width),
    ]
    specs = [
        moved[0],
        moved[0],
        moved[1],
        fixed(sums.shape),
        pl.BlockSpec((1, half, width), lambda i: (i // 2, lax.rem(i, 2), 0)),
        moved[3],
        pl.BlockSpec((2, heads // steps, wo.shape[2]), lambda i: (0, i, 0)),
        by_halves(heads, 1),
        by_lanes(low.shape[0]),
        pl.BlockSpec((HEAD_DIM, lanes), lambda i: (i // 3, lax.rem(i, 3))),
        by_halves(last.shape[1], 0),
    ]
    shapes = [(rows, width), dv.shape, (hidden, width), (width, hidden), (heads, width)]
    shapes += [(width, heads), (width, heads), (fresh, width)]
    shapes += [(hidden,), (heads,), (fresh,)] + [(width,)] * 6
    out_specs = moved + [by_rows(lanes, heads)] * 2 + [by_lanes(fresh)]
    out_specs += [fixed(s) for s in shapes[8:]]
    return pl.pallas_call(
        finish_kernel,
        grid=(steps,),
        in_specs=specs,
        out_specs=out_specs,
        out_shape=[jax.ShapeDtypeStruct(s, F32) for s in shapes],
        compiler_params=pltpu.CompilerParams(vmem_limit_bytes=VMEM_LIMIT),
        name="finish",
    )(*operands)


def swap(array):
    return lax.ppermute(array, "tensor", [(0, 1), (1, 0)])


def across_blocks(array, row_chips):
    chips = 4 * row_chips * row_chips
    shift = 2
    while shift < row_chips:
        for stride in (shift, shift * row_chips):
            pairs = [(i, i ^ stride) for i in range(chips)]
            array = array + lax.ppermute(array, "dp", pairs)
        shift *= 2
    return array


def on_device(
    row_chips,
    input_rows, first_values, doc_split, gain_norm1, bias_norm1, w_query, bias_query, w_key,
    w_value, bias_value, w_out, bias_attn_out, gain_norm2, bias_norm2, w_up, bias_up, w_down,
    bias_down, cotangent,
):
    heads = w_query.shape[1]
    fresh = w_value.shape[1]
    hidden = w_up.shape[1]
    pair = 2 * HEAD_DIM
    wv_t = w_value.T
    ln, qt, k, kt, v, vt = project(
        input_rows, first_values.T, gain_norm1, bias_norm1, w_query, bias_query, w_key, wv_t,
        bias_value,
    )
    up, down, wo, bu, vt = lax.optimization_barrier((w_up, w_down, w_out, bias_up, vt))
    up_other, down_other, wo_other, bu_other = swap(up), swap(down), swap(wo), swap(bu)
    attended, lse = attend(doc_split, qt, k, vt)
    output, grad_middle, grad_att, state_down, state_up, grad_wo, small = feed(
        row_chips, input_rows, cotangent, attended, w_out, wo_other, bias_attn_out, gain_norm2,
        bias_norm2, up_other, w_up, bu_other, bias_up, down_other, w_down, bias_down,
    )
    back, dv_first, *reduced = attend_back(
        row_chips, doc_split, gain_norm1, small, qt, k, kt, v, grad_att, attended, lse, ln,
        input_rows, w_query, w_key, wv_t, grad_wo, state_down, state_up,
    )
    reduced = [across_blocks(a, row_chips) for a in reduced]
    (
        grad_input, grad_first, grad_down, grad_up, grad_wo, grad_q, grad_k, grad_v, bias_grad_up,
        bias_grad_q, bias_grad_v, gain_two, shift_two, bias_grad_o, bias_grad_d, gain_one, shift_one,
    ) = finish(grad_middle, back, dv_first, *reduced)
    return (
        output, grad_input, grad_first.T, gain_one, shift_one, grad_q, bias_grad_q, grad_k, grad_v.T,
        bias_grad_v, grad_wo, bias_grad_o, gain_two, shift_two, grad_up, bias_grad_up, grad_down,
        bias_grad_d,
    )


def solution(mesh):
    row_chips = 1
    while 4 * row_chips * row_chips < mesh.shape["dp"]:
        row_chips += 1
    rows = P(("dp", "tensor"), None)
    cols = P(None, "tensor")
    split = P("tensor")
    firsts = P("dp", "tensor")
    wide = P("tensor", None)
    return jax.shard_map(
        functools.partial(on_device, row_chips),
        mesh=mesh,
        in_specs=(
            rows, firsts, P("dp"), P(), P(), cols, split, cols, cols, split, wide, P(), P(), P(),
            cols, split, wide, P(), rows,
        ),
        out_specs=(
            rows, rows, firsts, P(), P(), cols, split, cols, cols, split, wide, P(), P(), P(),
            cols, split, wide, P(),
        ),
        check_vma=False,
    )
```
